32 devices in a mesh: space: 8 (over y, x, core), chan: 4 (over z).
Axes of the slice: x: 2, y: 2, z: 4, core: 2. Of those that a mesh axis runs over, the one named last changes fastest.
Arguments:
- features: bfloat16 [8, 128, 8, 8, 256], P('space'), may hold values from -6 to 6
- column_heights: int32 [8], replicated, may hold values from 1 to 32, as said below
- weight_one: bfloat16 [27, 128, 128], P(None, 'chan'), may hold values from -0.109375 to 0.109375
- bias_one: float32 [128], P('chan'), may hold values from 0 to 1
- weight_two: bfloat16 [27, 128, 128], P(None, 'chan'), may hold values from -0.109375 to 0.109375
- bias_two: float32 [128], P('chan'), may hold values from 0 to 1
Outputs:
- output: bfloat16 [8, 128, 8, 8, 256], P('space', 'chan')
The draws below stay inside these ranges and needn't reach their ends.
Inputs may be any that keep to these rules, and one draw needn't show every extreme that they name: Column c holds its active bricks at its lowest column_heights[c] of 32 levels; some column holds exactly 32.
All inputs are finite; a program needn't handle non-finite values.
Results may differ from the reference program's by a relative error of at most 0.004.
Values may be sent and summed in bfloat16 or wider, within the bound.
No kernel may reach another device: no remote copies, remote signals or barrier semaphores. Data moves between devices by JAX's collectives and lax.ppermute only.
A program may use at most 128 MiB of HBM per device.

```python
import jax
import jax.numpy as jnp
from jax import lax

CHANNELS = 128
COL_Y = 8
BRICKS_Z = 32
COLUMNS = 8
DEPTH = 256


def draw_column_heights(key, part):
    key_levels, key_tallest = jax.random.split(key)
    levels = jax.random.randint(key_levels, (COLUMNS,), 0, BRICKS_Z)
    heights = 1 + levels * levels // BRICKS_Z
    tallest = jax.random.randint(key_tallest, (), 0, COLUMNS)
    return jnp.where(jnp.arange(COLUMNS) == tallest, BRICKS_Z, heights).astype(jnp.int32)


def block_scale(stream_key, extent, cuts, smallest, high):
    gain, own = 1.0, jax.random.fold_in(stream_key, 6)
    for dim, shards_of in cuts:
        steps = jnp.exp(jax.random.uniform(jax.random.fold_in(own, dim), (shards_of,), jnp.float32, smallest / len(cuts), high / len(cuts)))
        gain = gain * jnp.repeat(steps, extent[dim] // shards_of).reshape([-1 if axis == dim else 1 for axis in range(len(extent))])
    return gain


def bell_draw(own_key, dims, width, bound, cuts=(), kind=jnp.bfloat16):
    values = width * jax.random.normal(own_key, dims, jnp.float32)
    if cuts:
        values = values * block_scale(own_key, dims, cuts, -0.22, 0.18)
    return jnp.clip(values, -bound, bound).astype(kind)


def setup_inputs(seed: int = 0) -> dict:
    key_of = jax.random.split(jax.random.key(seed), 7)
    return {
        "features": bell_draw(key_of[0], (COLUMNS, CHANNELS, 8, 8, DEPTH), 1.0, 6.0, ((0, 8),)),
        "column_heights": draw_column_heights(jax.random.fold_in(key_of[6], 71), 0),
        "weight_one": bell_draw(key_of[2], (27, CHANNELS, CHANNELS), (27 * CHANNELS) ** -0.5, 0.109375, ((1, 4),)),
        "bias_one": jnp.clip(1.0 * jax.random.uniform(key_of[3], (CHANNELS,), jnp.float32) ** block_scale(key_of[3], (CHANNELS,), ((0, 4),), -0.2, 0.2), 0.0, 1.0),
        "weight_two": bell_draw(key_of[4], (27, CHANNELS, CHANNELS), (27 * CHANNELS) ** -0.5, 0.109375, ((1, 4),)),
        "bias_two": jnp.clip(1.0 * jax.random.uniform(key_of[5], (CHANNELS,), jnp.float32) ** block_scale(key_of[5], (CHANNELS,), ((0, 4),), -0.2, 0.2), 0.0, 1.0),
    }


def block_size(depth_cells):
    return 16


def conv_layer(columns_in, heights, weights, biases):
    grid_rows = COLUMNS // COL_Y
    volume = columns_in.reshape(grid_rows, COL_Y, CHANNELS, 8, 8, DEPTH)
    volume = volume.transpose(2, 0, 3, 1, 4, 5).reshape(CHANNELS, grid_rows * 8, COL_Y * 8, DEPTH)
    padded = jnp.pad(volume, ((0, 0), (1, 1), (1, 1), (1, 1)))
    block_len = block_size(DEPTH)
    weights_wide = weights.astype(jnp.float32)

    def column(col_id):
        grid_x = col_id // COL_Y
        grid_y = col_id % COL_Y
        anchor = jnp.zeros((), jnp.int32)
        box_part = lax.dynamic_slice(padded, (anchor, (grid_x * 8).astype(jnp.int32), (grid_y * 8).astype(jnp.int32), anchor), (CHANNELS, 10, 10, DEPTH + 2))
        live_top = (heights[col_id] * 8).astype(jnp.int32)
        blocks = (live_top + block_len - 1) // block_len

        def advance(block_id, output):
            start = (block_id * block_len).astype(jnp.int32)
            summed = jnp.zeros((CHANNELS, 64 * block_len), jnp.float32)
            for shift_x in range(3):
                for shift_y in range(3):
                    for shift_z in range(3):
                        sliced = lax.dynamic_slice(box_part, (anchor, anchor + shift_x, anchor + shift_y, start + shift_z), (CHANNELS, 8, 8, block_len))
                        sliced = sliced.reshape(CHANNELS, 64 * block_len).astype(jnp.float32)
                        summed = summed + jnp.dot(weights_wide[9 * shift_x + 3 * shift_y + shift_z], sliced, precision=lax.Precision.HIGHEST, preferred_element_type=jnp.float32)
            result = jax.nn.relu(summed + biases[:, None]).reshape(CHANNELS, 8, 8, block_len)
            inside = (start + jnp.arange(block_len, dtype=jnp.int32)) < live_top
            result = (result * inside.astype(jnp.float32)).astype(jnp.bfloat16)
            return lax.dynamic_update_slice(output, result, (anchor, anchor, anchor, start))

        return lax.fori_loop(0, blocks, advance, jnp.zeros((CHANNELS, 8, 8, DEPTH), jnp.bfloat16))

    return lax.map(column, jnp.arange(COLUMNS, dtype=jnp.int32))


def reference(features, column_heights, weight_one, bias_one, weight_two, bias_two):
    z_cells = jnp.arange(DEPTH, dtype=jnp.int32)
    active = (z_cells[None, :] < column_heights[:, None] * 8).astype(jnp.float32)
    inputs = (features * active[:, None, None, None, :].astype(features.dtype)).astype(jnp.bfloat16)
    hidden = conv_layer(inputs, column_heights, weight_one, bias_one)
    return conv_layer(hidden, column_heights, weight_two, bias_two)
```

```python
import functools

import jax
import jax.numpy as jnp
from jax import lax
from jax.experimental import pallas as pl
from jax.experimental.pallas import tpu as pltpu
from jax.sharding import PartitionSpec as P

COL_Y = 8
TAPS = 3
BF16 = jnp.bfloat16
F32 = jnp.float32


def shifted(value, axis, pairs):
    return lax.ppermute(value, axis, pairs)


def y_pairs(peers, by):
    return [(i, i + by) for i in range(peers) if 0 <= i + by < peers and i // COL_Y == (i + by) // COL_Y]


def x_pairs(peers, by):
    return [(i, i + by * COL_Y) for i in range(peers) if 0 <= i + by * COL_Y < peers]


def finish(partial, bias, live_top):
    rows, depth = partial.shape[0] // TAPS, partial.shape[1]
    z = lax.broadcasted_iota(jnp.int32, (rows, depth), 1)
    below = jnp.where(z == 0, 0.0, pltpu.roll(partial[:rows], 1, 1))
    above = jnp.where(z == depth - 1, 0.0, pltpu.roll(partial[2 * rows :], depth - 1, 1))
    total = jnp.maximum(below + partial[rows : 2 * rows] + above + bias, 0.0)
    return jnp.where(z < live_top, total, 0.0).astype(BF16)


def x_reach(x, width, halo):
    first, last = x - 1 + halo, x + width + halo
    limit = COL_Y + 2 * halo
    low = max(first, 0)
    return low, min(last + 1, limit), low - first


def row_fields(rows, y, low, high):
    return jnp.concatenate(
        [rows[y + j, low:high].reshape((high - low) * rows.shape[2], rows.shape[3]) for j in range(TAPS)], axis=0
    )


def start_rows(sources, rows, sems):
    for slot, source in sources:
        pltpu.make_async_copy(source, rows.at[slot], sems.at[slot]).start()


def wait_row(source, rows, slot, sems):
    pltpu.make_async_copy(source, rows.at[slot], sems.at[slot]).wait()


def mask_row(rows, slot, tops):
    top = jnp.where(slot == 0, tops[0], jnp.where(slot == COL_Y + 1, tops[2], tops[1]))
    depth = rows.shape[3]
    keep = (lax.broadcasted_iota(jnp.int32, (1, depth), 1) < top).astype(F32).astype(BF16)
    rows[slot] = rows[slot] * keep[None]


def first_kernel(border, halo, n_parts, *refs):
    tops, order, low, own, high = refs[:5]
    parts, (out, rows, matrix, low_matrix, high_matrix, bias, sems) = refs[5 : 5 + n_parts], refs[5 + n_parts :]
    step = pl.program_id(0)
    quarter, channels = parts[0].shape[1], parts[0].shape[2]
    sources = [(y + 1, own.at[y]) for y in ((0, 1, 6, 7) if border else range(COL_Y))]
    if border:
        sources = [(0, low)] + sources + [(COL_Y + 1, high)]

    @pl.when(step == 0)
    def _():
        start_rows(sources, rows, sems)
        for s, part in enumerate(parts):
            at = order[s] * quarter
            for k in range(TAPS):
                span = pl.ds(pl.multiple_of(k * channels + at, quarter), quarter)
                for j in range(TAPS):
                    for i in range(TAPS):
                        tile = part[9 * i + 3 * j + k]
                        matrix[span, pl.ds((j * TAPS + i) * channels, channels)] = tile
                        if not halo and i > 0:
                            low_matrix[span, pl.ds((j * 2 + i - 1) * channels, channels)] = tile
                        if not halo and i < 2:
                            high_matrix[span, pl.ds((j * 2 + i) * channels, channels)] = tile
            extra = part[27].astype(F32)
            value = extra[:, 0:1] + extra[:, 1:2] + extra[:, 2:3]
            bias[pl.ds(pl.multiple_of(at, quarter), quarter), :] = jnp.broadcast_to(value, (quarter, bias.shape[1]))

    if border:
        y = step * (COL_Y - 1)
        for j in range(TAPS):
            wait_row(low, rows, y + j, sems)
            mask_row(rows, y + j, tops)
    else:
        y = step + 1

        @pl.when(step == 0)
        def _():
            for slot in (1, 2):
                wait_row(low, rows, slot, sems)
                mask_row(rows, slot, tops)

        wait_row(low, rows, y + 2, sems)
        mask_row(rows, y + 2, tops)

    for x in range(COL_Y):
        first, last, _ = x_reach(x, 1, halo)
        lhs = matrix
        if last - first == 2:
            lhs = low_matrix if x == 0 else high_matrix
        partial = jnp.dot(lhs[...], row_fields(rows, y, first, last), preferred_element_type=F32)
        out[0, x] = finish(partial, bias[:, 0:1], tops[3])


def second_kernel(halo, tops, low, edge, inner, edge_high, high, weights, bias, out, rows, matrix, low_matrix, high_matrix, sems):
    step = pl.program_id(0)
    quarter, channels = weights.shape[1], weights.shape[2]
    sources = [(0, low), (1, edge)] + [(y + 2, inner.at[y]) for y in range(COL_Y - 2)]
    sources = sources + [(COL_Y, edge_high), (COL_Y + 1, high)]

    @pl.when(step == 0)
    def _():
        start_rows(sources, rows, sems)
        matrix[...] = jnp.zeros_like(matrix)
        low_matrix[...] = jnp.zeros_like(low_matrix)
        high_matrix[...] = jnp.zeros_like(high_matrix)
        for k in range(TAPS):
            for to in range(2):
                span = pl.ds((k * 2 + to) * quarter, quarter)
                for j in range(TAPS):
                    for i in range(TAPS):
                        tile, at = weights[9 * i + 3 * j + k], to + i
                        matrix[span, pl.ds((j * 4 + at) * channels, channels)] = tile
                        if at > 0:
                            low_matrix[span, pl.ds((j * 3 + at - 1) * channels, channels)] = tile
                        if at < 3:
                            high_matrix[span, pl.ds((j * 3 + at) * channels, channels)] = tile
        for slot in (0, 1):
            wait_row(low, rows, slot, sems)

    wait_row(low, rows, step + 2, sems)
    both = jnp.concatenate([bias[...], bias[...]], axis=0)
    for x in range(0, COL_Y, 2):
        first, last, _ = x_reach(x, 2, halo)
        lhs = matrix
        if last - first == 3:
            lhs = low_matrix if x == 0 else high_matrix
        partial = jnp.dot(lhs[...], row_fields(rows, step, first, last), preferred_element_type=F32)
        done = finish(partial, both, tops[3])
        out[0, x] = done[:quarter]
        out[0, x + 1] = done[quarter:]


ANY = pl.BlockSpec(memory_space=pl.ANY)
WHOLE = pl.BlockSpec(memory_space=pltpu.VMEM)
SCALARS = pl.BlockSpec(memory_space=pltpu.SMEM)


def cost(flops, nbytes):
    return pl.CostEstimate(flops=int(flops), bytes_accessed=int(nbytes), transcendentals=0)


def first_layer(border, halo, tops, order, low, own, high, parts):
    _, width, channels, depth = own.shape
    steps = 2 if border else COL_Y - 2
    wide = TAPS * channels
    return pl.pallas_call(
        functools.partial(first_kernel, border, halo, len(parts)),
        grid=(steps,),
        out_shape=jax.ShapeDtypeStruct((steps, COL_Y, channels, depth), BF16),
        in_specs=[SCALARS, SCALARS, ANY, ANY, ANY] + [WHOLE] * len(parts),
        out_specs=pl.BlockSpec((1, COL_Y, channels, depth), lambda i: (i, 0, 0, 0)),
        scratch_shapes=[
            pltpu.VMEM((COL_Y + 2, width, channels, depth), BF16),
            pltpu.VMEM((wide, 3 * wide), BF16),
            pltpu.VMEM((wide, 2 * wide), BF16),
            pltpu.VMEM((wide, 2 * wide), BF16),
            pltpu.VMEM((channels, 128), F32),
            pltpu.SemaphoreType.DMA((COL_Y + 2,)),
        ],
        compiler_params=pltpu.CompilerParams(vmem_limit_bytes=40 * 2**20),
        cost_estimate=cost(2 * steps * COL_Y * depth * 27 * channels * channels, 2 * own.size),
        name="first_border" if border else "first_inner",
    )(tops, order, low, own, high, *parts)


def second_layer(halo, tops, low, edge, inner, edge_high, high, weights, bias):
    _, width, channels, depth = inner.shape
    quarter = weights.shape[1]
    tall = TAPS * 2 * quarter
    return pl.pallas_call(
        functools.partial(second_kernel, halo),
        grid=(COL_Y,),
        out_shape=jax.ShapeDtypeStruct((COL_Y, COL_Y, quarter, depth), BF16),
        in_specs=[SCALARS, ANY, ANY, ANY, ANY, ANY, WHOLE, WHOLE],
        out_specs=pl.BlockSpec((1, COL_Y, quarter, depth), lambda i: (i, 0, 0, 0)),
        scratch_shapes=[
            pltpu.VMEM((COL_Y + 2, width, channels, depth), BF16),
            pltpu.VMEM((tall, 12 * channels), BF16),
            pltpu.VMEM((tall, 9 * channels), BF16),
            pltpu.VMEM((tall, 9 * channels), BF16),
            pltpu.SemaphoreType.DMA((COL_Y + 2,)),
        ],
        compiler_params=pltpu.CompilerParams(vmem_limit_bytes=40 * 2**20),
        cost_estimate=cost(2 * COL_Y * COL_Y * depth * 27 * channels * quarter, 2 * inner.size),
        name="second",
    )(tops, low, edge, inner, edge_high, high, weights, bias)


def with_x_borders(low, own, high, peers):
    tall = jnp.concatenate([low[None], own, high[None]], axis=0)
    before = shifted(tall[:, COL_Y - 1], "space", x_pairs(peers, 1))
    after = shifted(tall[:, 0], "space", x_pairs(peers, -1))
    tall = jnp.concatenate([before[:, None], tall, after[:, None]], axis=1)
    return tall[0], tall[1:-1], tall[-1]


def exact_parts(value):
    found = []
    for _ in range(3):
        piece = lax.reduce_precision(value, 8, 7)
        found.append(piece.astype(BF16))
        value = value - piece
    return jnp.stack(found, axis=-1)


def on_device(features, column_heights, weight_one, bias_one, weight_two, bias_two):
    column = lax.axis_index("space")
    peers, chans, own_chan = lax.axis_size("space"), lax.axis_size("chan"), lax.axis_index("chan")
    _, channels, _, _, depth = features.shape
    halo = 1 if peers > COL_Y else 0
    up, down = y_pairs(peers, 1), y_pairs(peers, -1)

    quarter = weight_one.shape[1]
    packed = jnp.pad(exact_parts(bias_one), ((0, 0), (0, channels - 3)))[None]
    packed = jnp.concatenate([weight_one, packed], axis=0)
    parts = [packed]
    for s in range(1, chans):
        parts.append(shifted(packed, "chan", [(i, (i + s) % chans) for i in range(chans)]))
    order = (own_chan - jnp.arange(chans, dtype=jnp.int32)) % chans

    live = column_heights * 8
    own_top = live[column]
    beside = [live[jnp.clip(column + by, 0, peers - 1)] for by in (-1, 0, 1)]
    fields = jnp.transpose(features[0], (2, 1, 0, 3))
    if halo:
        fields = fields * (lax.iota(jnp.int32, depth) < own_top).astype(BF16)
        beside = [jnp.full_like(own_top, depth)] * 3
    tops = jnp.stack(beside + [own_top])

    low = shifted(fields[COL_Y - 1], "space", up)
    high = shifted(fields[0], "space", down)
    if halo:
        low, fields, high = with_x_borders(low, fields, high, peers)
    edges = first_layer(True, halo, tops, order, low, fields, high, parts)
    low_hidden = shifted(edges[1], "space", up)
    high_hidden = shifted(edges[0], "space", down)
    inner = first_layer(False, halo, tops, order, low, fields, high, parts)
    first, last = edges[0], edges[1]
    if halo:
        own = jnp.concatenate([edges[:1], inner, edges[1:]], axis=0)
        low_hidden, own, high_hidden = with_x_borders(low_hidden, own, high_hidden, peers)
        first, inner, last = own[0], own[1:-1], own[-1]
    output = second_layer(halo, tops, low_hidden, first, inner, last, high_hidden, weight_two, bias_two[:, None])
    return jnp.transpose(output, (2, 1, 0, 3))[None]


def solution(mesh):
    placed = (
        P("space", None, None, None, None),
        P(),
        P(None, "chan", None),
        P("chan"),
        P(None, "chan", None),
        P("chan"),
    )
    return jax.shard_map(
        on_device,
        mesh=mesh,
        in_specs=placed,
        out_specs=P("space", "chan", None, None, None),
        check_vma=False,
    )
```

```python
import functools

import jax
import jax.numpy as jnp
from jax import lax
from jax.experimental import pallas as pl
from jax.experimental.pallas import tpu as pltpu
from jax.sharding import PartitionSpec as P

COL_Y = 8
TAPS = 3
BF16 = jnp.bfloat16
F32 = jnp.float32
ANY = pl.BlockSpec(memory_space=pl.ANY)
WHOLE = pl.BlockSpec(memory_space=pltpu.VMEM)
SCALARS = pl.BlockSpec(memory_space=pltpu.SMEM)
VMEM_LIMIT = 40 * 2**20


def pack_kernel(weights, bias, packed):
    taps, rows, lanes = weights.shape
    packed[:taps] = weights[...]
    column = as_column(bias[...])
    lane = lax.broadcasted_iota(jnp.int32, (rows, lanes), 1)
    extra = jnp.zeros((rows, lanes), F32)
    for at in range(3):
        piece = column.astype(BF16).astype(F32)
        extra = jnp.where(lane == at, piece, extra)
        column = column - piece
    packed[taps] = extra.astype(BF16)


def as_column(row):
    size = row.shape[1]
    wide = jnp.broadcast_to(row, (size, size))
    same = lax.broadcasted_iota(jnp.int32, (size, size), 0) == lax.broadcasted_iota(jnp.int32, (size, size), 1)
    return jnp.sum(jnp.where(same, wide, 0.0), axis=1, keepdims=True)


def swap_matrix(outer, inner):
    size = outer * inner
    row = lax.broadcasted_iota(jnp.int32, (size, size), 0)
    column = lax.broadcasted_iota(jnp.int32, (size, size), 1)
    return (column == lax.rem(row, inner) * outer + lax.div(row, inner)).astype(F32).astype(BF16)


def arrange_kernel(scalars, features, fields, cross, mate, swap):
    channels, _, depth = features.shape[1], features.shape[3], features.shape[4]
    group = swap.shape[0] // COL_Y
    top, odd = scalars[0], scalars[1] == 1

    @pl.when(pl.program_id(0) == 0)
    def _():
        swap[...] = swap_matrix(COL_Y, group)

    live = lax.broadcasted_iota(jnp.int32, (1, depth), 1) < top
    for first in range(0, channels, group):
        tile = features[0, first : first + group, 0].reshape(group * COL_Y, depth)
        moved = jnp.dot(swap[...], tile, preferred_element_type=F32)
        moved = jnp.where(live, moved, 0.0).astype(BF16).reshape(COL_Y, group, depth)
        fields[:, 0, first : first + group] = moved
        cross[0, first : first + group] = jnp.where(odd, moved[COL_Y - 1], moved[0])
        mate[0, first : first + group] = jnp.where(odd, moved[0], moved[COL_Y - 1])


def finish(partial, bias, live_top):
    rows, depth = partial.shape[0] // TAPS, partial.shape[1]
    z = lax.broadcasted_iota(jnp.int32, (rows, depth), 1)
    below = jnp.where(z == 0, 0.0, pltpu.roll(partial[:rows], 1, 1))
    above = jnp.where(z == depth - 1, 0.0, pltpu.roll(partial[2 * rows :], depth - 1, 1))
    total = jnp.maximum(below + partial[rows : 2 * rows] + above + bias, 0.0)
    return jnp.where(z < live_top, total, 0.0).astype(BF16)


def x_reach(x, width, halo):
    first, last = x - 1 + halo, x + width + halo
    return max(first, 0), min(last + 1, COL_Y + 2 * halo)


def row_fields(rows, y, low, high):
    return jnp.concatenate(
        [rows[y + j, low:high].reshape((high - low) * rows.shape[2], rows.shape[3]) for j in range(TAPS)], axis=0
    )


class Arrivals:
    def __init__(self, rows, sems):
        self.rows, self.sems = rows, sems

    def start(self, source, slot):
        pltpu.make_async_copy(source, self.rows.at[slot], self.sems.at[slot]).start()

    def start_part(self, source, slot, at, count):
        target = self.rows.at[slot, :, pl.ds(pl.multiple_of(at, count), count)]
        pltpu.make_async_copy(source, target, self.sems.at[slot]).start()

    def wait(self, slot):
        pltpu.make_async_copy(self.rows.at[slot], self.rows.at[slot], self.sems.at[slot]).wait()


def fill_first(parts, places, matrix, low_matrix, high_matrix, bias, halo):
    quarter, channels = parts[0].shape[1], parts[0].shape[2]
    block = quarter * len(parts)
    for part, place in zip(parts, places, strict=True):
        for k in range(TAPS):
            span = pl.ds(pl.multiple_of(k * block + place, quarter), quarter)
            for j in range(TAPS):
                for i in range(TAPS):
                    tile = part[9 * i + 3 * j + k]
                    matrix[span, pl.ds((j * TAPS + i) * channels, channels)] = tile
                    if not halo and i > 0:
                        low_matrix[span, pl.ds((j * 2 + i - 1) * channels, channels)] = tile
                    if not halo and i < 2:
                        high_matrix[span, pl.ds((j * 2 + i) * channels, channels)] = tile
        extra = part[27].astype(F32)
        value = extra[:, 0:1] + extra[:, 1:2] + extra[:, 2:3]
        bias[pl.ds(pl.multiple_of(place, quarter), quarter), :] = jnp.broadcast_to(value, (quarter, bias.shape[1]))


def first_row(rows, y, matrices, bias, top, halo):
    for x in range(COL_Y):
        first, last = x_reach(x, 1, halo)
        lhs = matrices[0]
        if last - first == 2:
            lhs = matrices[1] if x == 0 else matrices[2]
        partial = jnp.dot(lhs[...], row_fields(rows, y, first, last), preferred_element_type=F32)
        yield x, finish(partial, bias[:, 0:1], top)


def first_inner_kernel(halo, scalars, own, part_a, part_b, out, rows, matrix, low_matrix, high_matrix, bias, sems):
    step = pl.program_id(0)
    arrive = Arrivals(rows, sems)
    quarter = part_a.shape[1]

    @pl.when(step == 0)
    def _():
        for y in range(COL_Y):
            arrive.start(own.at[y], y)
        places = [scalars[1] * quarter, scalars[2] * quarter]
        fill_first([part_a, part_b], places, matrix, low_matrix, high_matrix, bias, halo)
        arrive.wait(0)
        arrive.wait(1)

    arrive.wait(step + 2)
    for x, done in first_row(rows, step, (matrix, low_matrix, high_matrix), bias, scalars[0], halo):
        out[0, x] = done


def first_border_kernel(halo, scalars, own, cross, mate, *refs):
    parts, (out_cross, out_mate, rows, matrix, low_matrix, high_matrix, bias, sems) = refs[:4], refs[4:]
    step = pl.program_id(0)
    arrive = Arrivals(rows, sems)
    quarter = parts[0].shape[1]
    odd = scalars[1]
    at_cross, at_mate = jnp.where(odd == 1, 5, 0), jnp.where(odd == 1, 0, 5)

    @pl.when(step == 0)
    def _():
        arrive.start(cross, at_cross)
        arrive.start(mate, at_mate)
        for y, slot in ((0, 1), (1, 2), (6, 3), (7, 4)):
            arrive.start(own.at[y], slot)
        places = [scalars[2 + s] * quarter for s in range(4)]
        fill_first(parts, places, matrix, low_matrix, high_matrix, bias, halo)

    y = jnp.where(odd == step, 0, 3)
    for j in range(TAPS):
        arrive.wait(y + j)

    matrices = (matrix, low_matrix, high_matrix)
    for x, done in first_row(rows, y, matrices, bias, scalars[0], halo):
        @pl.when(step == 0)
        def _(x=x, done=done):
            out_cross[x] = done

        @pl.when(step == 1)
        def _(x=x, done=done):
            out_mate[x] = done


def fill_second(weights, matrix, low_matrix, high_matrix):
    quarter, channels = weights.shape[1], weights.shape[2]
    matrix[...] = jnp.zeros_like(matrix)
    low_matrix[...] = jnp.zeros_like(low_matrix)
    high_matrix[...] = jnp.zeros_like(high_matrix)
    for k in range(TAPS):
        for to in range(2):
            span = pl.ds((k * 2 + to) * quarter, quarter)
            for j in range(TAPS):
                for i in range(TAPS):
                    tile, at = weights[9 * i + 3 * j + k], to + i
                    matrix[span, pl.ds((j * 4 + at) * channels, channels)] = tile
                    if at > 0:
                        low_matrix[span, pl.ds((j * 3 + at - 1) * channels, channels)] = tile
                    if at < 3:
                        high_matrix[span, pl.ds((j * 3 + at) * channels, channels)] = tile


def second_row(rows, y, matrices, both, top, halo):
    quarter = both.shape[0] // 2
    for x in range(0, COL_Y, 2):
        first, last = x_reach(x, 2, halo)
        lhs = matrices[0]
        if last - first == 3:
            lhs = matrices[1] if x == 0 else matrices[2]
        partial = jnp.dot(lhs[...], row_fields(rows, y, first, last), preferred_element_type=F32)
        done = finish(partial, both, top)
        yield x, done[:quarter], done[quarter:]


def second_inner_kernel(halo, scalars, edge_cross, edge_mate, inner_a, inner_b, weights, bias, out, rows, matrix, low_matrix, high_matrix, both, sems):
    step = pl.program_id(0)
    arrive = Arrivals(rows, sems)
    half, quarter = inner_a.shape[2], weights.shape[1]

    @pl.when(step == 0)
    def _():
        odd, place = scalars[1], scalars[2]
        arrive.start(edge_cross, jnp.where(odd == 1, 7, 0))
        arrive.start(edge_mate, jnp.where(odd == 1, 0, 7))
        for y in range(COL_Y - 2):
            arrive.start_part(inner_a.at[y], y + 1, place * half, half)
            arrive.start_part(inner_b.at[y], y + 1, (1 - place) * half, half)
        fill_second(weights, matrix, low_matrix, high_matrix)
        column = jnp.broadcast_to(as_column(bias[...]), (quarter, both.shape[1]))
        both[:quarter] = column
        both[quarter:] = column
        arrive.wait(0)
        arrive.wait(1)

    arrive.wait(step + 2)
    for x, here, beside in second_row(rows, step, (matrix, low_matrix, high_matrix), both[:, 0:1], scalars[0], halo):
        out[0, x] = here
        out[0, x + 1] = beside


def second_border_kernel(halo, scalars, cross, mate, edge_cross, edge_mate, inner_a, inner_b, done_inner, weights, bias, out, rows, matrix, low_matrix, high_matrix, both, done_rows, sems):
    arrive = Arrivals(rows, sems)
    half, quarter = inner_a.shape[2], weights.shape[1]
    odd, place = scalars[1], scalars[2]
    inner_copy = pltpu.make_async_copy(done_inner, done_rows.at[1 : COL_Y - 1], sems.at[6])
    inner_copy.start()
    for source, when_even, when_odd in ((cross, 0, 5), (edge_cross, 1, 4), (edge_mate, 4, 1), (mate, 5, 0)):
        arrive.start(source, jnp.where(odd == 1, when_odd, when_even))
    for y, slot in ((0, 2), (COL_Y - 3, 3)):
        arrive.start_part(inner_a.at[y], slot, place * half, half)
        arrive.start_part(inner_b.at[y], slot, (1 - place) * half, half)
    fill_second(weights, matrix, low_matrix, high_matrix)
    column = jnp.broadcast_to(as_column(bias[...]), (quarter, both.shape[1]))
    both[:quarter] = column
    both[quarter:] = column
    for slot in range(6):
        arrive.wait(slot)
    for y, slot in ((0, 0), (COL_Y - 1, 3)):
        for x, here, beside in second_row(rows, slot, (matrix, low_matrix, high_matrix), both[:, 0:1], scalars[0], halo):
            done_rows[y, x] = here
            done_rows[y, x + 1] = beside
    inner_copy.wait()
    depth = out.shape[4]
    swap = swap_matrix(quarter, COL_Y)
    for x in range(COL_Y):
        tile = jnp.concatenate([done_rows[y, x] for y in range(COL_Y)], axis=0)
        moved = jnp.dot(swap, tile, preferred_element_type=F32).astype(BF16)
        out[0, :, x] = moved.reshape(quarter, COL_Y, depth)


def cost(flops, nbytes):
    return pl.CostEstimate(flops=int(flops), bytes_accessed=int(nbytes), transcendentals=0)


def params():
    return pltpu.CompilerParams(vmem_limit_bytes=VMEM_LIMIT)


def shape_of(*dims):
    return jax.ShapeDtypeStruct(dims, BF16)


def pack(weights, bias):
    taps, rows, lanes = weights.shape
    return pl.pallas_call(
        pack_kernel,
        out_shape=shape_of(taps + 1, rows, lanes),
        in_specs=[WHOLE, WHOLE],
        out_specs=WHOLE,
        compiler_params=params(),
        cost_estimate=cost(0, 4 * weights.size),
        name="pack",
    )(weights, bias[None])


def arrange(scalars, features):
    _, channels, width, _, depth = features.shape
    edge = pl.BlockSpec((1, channels, depth), lambda i: (i, 0, 0))
    return pl.pallas_call(
        arrange_kernel,
        grid=(width,),
        out_shape=[
            shape_of(COL_Y, width, channels, depth),
            shape_of(width, channels, depth),
            shape_of(width, channels, depth),
        ],
        in_specs=[SCALARS, pl.BlockSpec((1, channels, 1, COL_Y, depth), lambda i: (0, 0, i, 0, 0))],
        out_specs=[pl.BlockSpec((COL_Y, 1, channels, depth), lambda i: (0, i, 0, 0)), edge, edge],
        scratch_shapes=[pltpu.VMEM((256, 256), BF16)],
        compiler_params=params(),
        cost_estimate=cost(2 * 256 * features.size, 5 * features.size),
        name="arrange",
    )(scalars, features)


def first_scratch(slots, width, channels, depth, rows):
    wide = TAPS * channels
    return [
        pltpu.VMEM((slots, width, channels, depth), BF16),
        pltpu.VMEM((TAPS * rows, 3 * wide), BF16),
        pltpu.VMEM((TAPS * rows, 2 * wide), BF16),
        pltpu.VMEM((TAPS * rows, 2 * wide), BF16),
        pltpu.VMEM((rows, 128), F32),
        pltpu.SemaphoreType.DMA((slots,)),
    ]


def first_inner(halo, scalars, own, part_a, part_b):
    _, width, channels, depth = own.shape
    half = 2 * part_a.shape[1]
    steps = COL_Y - 2
    return pl.pallas_call(
        functools.partial(first_inner_kernel, halo),
        grid=(steps,),
        out_shape=shape_of(steps, COL_Y, half, depth),
        in_specs=[SCALARS, ANY, WHOLE, WHOLE],
        out_specs=pl.BlockSpec((1, COL_Y, half, depth), lambda i: (i, 0, 0, 0)),
        scratch_shapes=first_scratch(COL_Y, width, channels, depth, half),
        compiler_params=params(),
        cost_estimate=cost(2 * steps * COL_Y * depth * 27 * channels * half, 3 * own.size),
        name="first_inner",
    )(scalars, own, part_a, part_b)


def first_border(halo, scalars, own, cross, mate, parts):
    _, width, channels, depth = own.shape
    whole = pl.BlockSpec((COL_Y, channels, depth), lambda i: (0, 0, 0))
    return pl.pallas_call(
        functools.partial(first_border_kernel, halo),
        grid=(2,),
        out_shape=[shape_of(COL_Y, channels, depth)] * 2,
        in_specs=[SCALARS, ANY, ANY, ANY] + [WHOLE] * 4,
        out_specs=[whole, whole],
        scratch_shapes=first_scratch(6, width, channels, depth, channels),
        compiler_params=params(),
        cost_estimate=cost(4 * COL_Y * depth * 27 * channels * channels, 2 * own.size),
        name="first_border",
    )(scalars, own, cross, mate, *parts)


def second_scratch(slots, width, channels, depth, quarter):
    tall = TAPS * 2 * quarter
    return [
        pltpu.VMEM((slots, width, channels, depth), BF16),
        pltpu.VMEM((tall, 12 * channels), BF16),
        pltpu.VMEM((tall, 9 * channels), BF16),
        pltpu.VMEM((tall, 9 * channels), BF16),
        pltpu.VMEM((2 * quarter, 128), F32),
    ]


def second_inner(halo, scalars, edge_cross, edge_mate, inner_a, inner_b, weights, bias):
    steps, width, half, depth = inner_a.shape
    channels, quarter = 2 * half, weights.shape[1]
    return pl.pallas_call(
        functools.partial(second_inner_kernel, halo),
        grid=(steps,),
        out_shape=shape_of(steps, COL_Y, quarter, depth),
        in_specs=[SCALARS] + [ANY] * 4 + [WHOLE] * 2,
        out_specs=pl.BlockSpec((1, COL_Y, quarter, depth), lambda i: (i, 0, 0, 0)),
        scratch_shapes=second_scratch(COL_Y, width, channels, depth, quarter) + [pltpu.SemaphoreType.DMA((COL_Y,))],
        compiler_params=params(),
        cost_estimate=cost(2 * steps * COL_Y * depth * 27 * channels * quarter, 4 * inner_a.size),
        name="second_inner",
    )(scalars, edge_cross, edge_mate, inner_a, inner_b, weights, bias[None])


def second_border(halo, scalars, cross, mate, edge_cross, edge_mate, inner_a, inner_b, done_inner, weights, bias):
    _, width, half, depth = inner_a.shape
    channels, quarter = 2 * half, weights.shape[1]
    return pl.pallas_call(
        functools.partial(second_border_kernel, halo),
        out_shape=shape_of(1, quarter, COL_Y, COL_Y, depth),
        in_specs=[SCALARS] + [ANY] * 7 + [WHOLE] * 2,
        out_specs=WHOLE,
        scratch_shapes=second_scratch(6, width, channels, depth, quarter)
        + [pltpu.VMEM((COL_Y, COL_Y, quarter, depth), BF16), pltpu.SemaphoreType.DMA((7,))],
        compiler_params=params(),
        cost_estimate=cost(4 * COL_Y * depth * 27 * channels * quarter, 2 * inner_a.size),
        name="second_border",
    )(scalars, cross, mate, edge_cross, edge_mate, inner_a, inner_b, done_inner, weights, bias[None])


def cross_pairs(peers):
    pairs = []
    for i in range(peers):
        to = i + 1 if i % 2 else i - 1
        if 0 <= to < peers and to // COL_Y == i // COL_Y:
            pairs.append((i, to))
    return pairs


def mate_pairs(peers):
    return [(i, i ^ 1) for i in range(peers)]


def x_pairs(peers, by):
    return [(i, i + by * COL_Y) for i in range(peers) if 0 <= i + by * COL_Y < peers]


def far_pairs(peers, chans):
    pairs = []
    for i in range(peers):
        for c in range(chans):
            pairs.append((i * chans + c, i * chans + (c ^ (3 if i % 2 else 2))))
    return pairs


def with_x_borders(low, own, high, peers):
    tall = jnp.concatenate([low[None], own, high[None]], axis=0)
    before = lax.ppermute(tall[:, COL_Y - 1], "space", x_pairs(peers, 1))
    after = lax.ppermute(tall[:, 0], "space", x_pairs(peers, -1))
    tall = jnp.concatenate([before[:, None], tall, after[:, None]], axis=1)
    return tall[0], tall[1:-1], tall[-1]


def on_device(features, column_heights, weight_one, bias_one, weight_two, bias_two):
    column, chan = lax.axis_index("space"), lax.axis_index("chan")
    peers, chans = lax.axis_size("space"), lax.axis_size("chan")
    halo = 1 if peers > COL_Y else 0
    odd = column % 2
    top = column_heights[column] * 8

    own_part = pack(weight_one, bias_one)
    far_part = lax.ppermute(own_part, ("space", "chan"), far_pairs(peers, chans))
    near_part = lax.ppermute(own_part, "chan", [(c, c ^ 1) for c in range(chans)])
    fields, cross, mate = arrange(jnp.stack([top, odd]), features)
    cross = lax.ppermute(cross, "space", cross_pairs(peers))
    mate = lax.ppermute(mate, "space", mate_pairs(peers))
    if halo:
        low, high = jnp.where(odd == 1, mate, cross), jnp.where(odd == 1, cross, mate)
        low, fields, high = with_x_borders(low, fields, high, peers)
        cross, mate = jnp.where(odd == 1, high, low), jnp.where(odd == 1, low, high)

    here = chan % 2
    inner_a = first_inner(halo, jnp.stack([top, here, 1 - here]), fields, own_part, near_part)
    other_part = lax.ppermute(far_part, "space", mate_pairs(peers))
    first_far = jnp.where(odd == 1, 1 - here, here)
    place = chan // 2
    order = [chan, chan ^ 1, chan ^ (2 + odd), chan ^ (3 - odd)]
    edges = first_border(halo, jnp.stack([top, odd] + order), fields, cross, mate, (own_part, near_part, far_part, other_part))
    edge_cross, edge_mate = edges
    cross = lax.ppermute(edge_cross, "space", cross_pairs(peers))
    mate = lax.ppermute(edge_mate, "space", mate_pairs(peers))
    inner_b = first_inner(halo, jnp.stack([top, first_far, 1 - first_far]), fields, far_part, other_part)

    if halo:
        halves = jnp.where(place == 1, jnp.concatenate([inner_b, inner_a], axis=2), jnp.concatenate([inner_a, inner_b], axis=2))
        first, last = jnp.where(odd == 1, edge_mate, edge_cross), jnp.where(odd == 1, edge_cross, edge_mate)
        own = jnp.concatenate([first[None], halves, last[None]], axis=0)
        low, high = jnp.where(odd == 1, mate, cross), jnp.where(odd == 1, cross, mate)
        low, own, high = with_x_borders(low, own, high, peers)
        cross, mate = jnp.where(odd == 1, high, low), jnp.where(odd == 1, low, high)
        edge_cross, edge_mate = jnp.where(odd == 1, own[-1], own[0]), jnp.where(odd == 1, own[0], own[-1])
        half = inner_a.shape[2]
        inner_a = lax.dynamic_slice_in_dim(own[1:-1], place * half, half, 2)
        inner_b = lax.dynamic_slice_in_dim(own[1:-1], (1 - place) * half, half, 2)

    scalars = jnp.stack([top, odd, place])
    done_inner = second_inner(halo, scalars, edge_cross, edge_mate, inner_a, inner_b, weight_two, bias_two)
    return second_border(
        halo, scalars, cross, mate, edge_cross, edge_mate, inner_a, inner_b, done_inner, weight_two, bias_two
    )


def solution(mesh):
    placed = (
        P("space", None, None, None, None),
        P(),
        P(None, "chan", None),
        P("chan"),
        P(None, "chan", None),
        P("chan"),
    )
    return jax.shard_map(
        on_device,
        mesh=mesh,
        in_specs=placed,
        out_specs=P("space", "chan", None, None, None),
        check_vma=False,
    )
```

```python
import functools

import jax
import jax.numpy as jnp
from jax import lax
from jax.experimental import pallas as pl
from jax.experimental.pallas import tpu as pltpu
from jax.sharding import PartitionSpec as P

COL_Y = 8
TAPS = 3
BF16 = jnp.bfloat16
F32 = jnp.float32
ANY = pl.BlockSpec(memory_space=pl.ANY)
WHOLE = pl.BlockSpec(memory_space=pltpu.VMEM)
SCALARS = pl.BlockSpec(memory_space=pltpu.SMEM)


class Place:
    def __init__(self, heights):
        self.heights = heights
        self.column = lax.axis_index("space")
        self.peers = lax.axis_size("space")
        self.odd = lax.rem(self.column, 2)
        chan = lax.axis_index("chan")
        self.half = lax.div(chan, 2)
        near = lax.rem(chan, 2)
        far = jnp.where(self.odd == 1, 1 - near, near)
        self.slots = (near, 1 - near, far, 1 - far)

    def top(self, by_x=0, across=False):
        column, inside = self.column, True
        if across:
            y = lax.rem(column, COL_Y)
            step = jnp.where(self.odd == 1, 1, -1)
            inside = (y + step >= 0) & (y + step < COL_Y)
            column = column + step
        if by_x:
            column = column + by_x * COL_Y
            inside = inside & (column >= 0) & (column < self.peers)
        column = jnp.clip(column, 0, self.peers - 1)
        return jnp.where(inside, self.heights[column] * 8, 0)


def as_column(row):
    size = row.shape[1]
    wide = jnp.broadcast_to(row, (size, size))
    same = lax.broadcasted_iota(jnp.int32, (size, size), 0) == lax.broadcasted_iota(jnp.int32, (size, size), 1)
    return jnp.sum(jnp.where(same, wide, 0.0), axis=1, keepdims=True)


def pack_kernel(weights, bias, packed):
    taps, rows, lanes = weights.shape
    packed[:taps] = weights[...]
    column = as_column(bias[...])
    lane = lax.broadcasted_iota(jnp.int32, (rows, lanes), 1)
    extra = jnp.zeros((rows, lanes), F32)
    for at in range(3):
        piece = column.astype(BF16).astype(F32)
        extra = jnp.where(lane == at, piece, extra)
        column = column - piece
    packed[taps] = extra.astype(BF16)


def arrange_kernel(heights, features, after, fields, cross, mate):
    _, channels, width, _, depth = features.shape
    place = Place(heights)
    group = 256 // COL_Y
    row = lax.broadcasted_iota(jnp.int32, (256, 256), 0)
    column = lax.broadcasted_iota(jnp.int32, (256, 256), 1)
    u = lax.div(row, group)
    y = jnp.where(place.odd == 1, COL_Y - 1 - u, u)
    swap = (column == lax.rem(row, group) * COL_Y + y).astype(F32).astype(BF16)
    live = lax.broadcasted_iota(jnp.int32, (1, depth), 1) < place.top()
    for x in range(width):
        for first in range(0, channels, group):
            tile = features[0, first : first + group, x].reshape(256, depth)
            moved = jnp.dot(swap, tile, preferred_element_type=F32)
            moved = jnp.where(live, moved, 0.0).astype(BF16).reshape(COL_Y, group, depth)
            fields[:, x, first : first + group] = moved
            cross[:, x, first : first + group] = moved[:2]
            mate[x, first : first + group] = moved[COL_Y - 1]


def finish(partial, bias, live_top):
    rows, depth = partial.shape[0] // TAPS, partial.shape[1]
    z = lax.broadcasted_iota(jnp.int32, (rows, depth), 1)
    below = jnp.where(z == 0, 0.0, pltpu.roll(partial[:rows], 1, 1))
    above = jnp.where(z == depth - 1, 0.0, pltpu.roll(partial[2 * rows :], depth - 1, 1))
    total = jnp.maximum(below + partial[rows : 2 * rows] + above + bias, 0.0)
    return jnp.where(z < live_top, total, 0.0).astype(BF16)


def fill_first(parts, slots, odd, matrix, low_matrix, high_matrix, bias):
    quarter, channels = parts[0].shape[1], parts[0].shape[2]
    block = quarter * len(parts)
    for part, slot in zip(parts, slots, strict=True):
        at = slot * quarter
        for k in range(TAPS):
            span = pl.ds(pl.multiple_of(k * block + at, quarter), quarter)
            for j in range(TAPS):
                tap_j = jnp.where(odd == 1, 2 - j, j)
                for i in range(TAPS):
                    tile = part[9 * i + 3 * tap_j + k]
                    matrix[span, pl.ds((j * TAPS + i) * channels, channels)] = tile
                    if i > 0:
                        low_matrix[span, pl.ds((j * 2 + i - 1) * channels, channels)] = tile
                    if i < 2:
                        high_matrix[span, pl.ds((j * 2 + i) * channels, channels)] = tile
        extra = part[27].astype(F32)
        value = extra[:, 0:1] + extra[:, 1:2] + extra[:, 2:3]
        bias[pl.ds(pl.multiple_of(at, quarter), quarter), :] = jnp.broadcast_to(value, (quarter, bias.shape[1]))


def reach(x, width, stored, pad):
    return max(x - 1 + pad, 0), min(x + width + 1 + pad, stored)


def first_row(get, stored, halo, matrices, bias, top):
    for x in range(-halo, COL_Y + halo):
        low, high = reach(x, 1, stored, 2 * halo)
        lhs = matrices[0]
        if high - low == 2:
            lhs = matrices[1] if x == 0 else matrices[2]
        taken = jnp.concatenate([get(j, low, high) for j in range(TAPS)], axis=0)
        partial = jnp.dot(lhs[...], taken, preferred_element_type=F32)
        side = -1 if x < 0 else 1 if x >= COL_Y else 0
        yield x + halo, finish(partial, bias[:, 0:1], top(side))


def span_of(ref, *at):
    *lead, low, high = at
    value = ref[(*lead, slice(low, high))]
    return value.reshape(-1, value.shape[-1])


def first_inner_kernel(halo, heights, own, mate, part_a, part_b, after, out, out_last, matrix, low_matrix, high_matrix, bias, *, far):
    place = Place(heights)
    slots = place.slots[2:] if far else place.slots[:2]
    fill_first([part_a, part_b], slots, place.odd, matrix, low_matrix, high_matrix, bias)
    matrices, width = (matrix, low_matrix, high_matrix), own.shape[1]

    def pair(step, _):
        for more in range(2):
            u = step * 2 + more
            for x, done in first_row(lambda j, a, b: span_of(own, u + j, a, b), width, halo, matrices, bias, place.top):
                out[u, x] = done
        return 0

    lax.fori_loop(0, (COL_Y - 2) // 2, pair, 0)

    def get(j, a, b):
        return span_of(mate, a, b) if j == 2 else span_of(own, COL_Y - 2 + j, a, b)

    for x, done in first_row(get, width, halo, matrices, bias, place.top):
        out_last[x] = done


def fill_second(weights, place, matrix, low_matrix, high_matrix):
    quarter, channels = weights.shape[1], weights.shape[2]
    empty = jnp.zeros((quarter, channels), BF16)
    for k in range(TAPS):
        for to in range(2):
            span = pl.ds((k * 2 + to) * quarter, quarter)
            for j in range(TAPS):
                tap_j = jnp.where(place.odd == 1, 2 - j, j)
                for at in range(4):
                    tile = empty
                    if 0 <= at - to < TAPS:
                        tile = weights[9 * (at - to) + 3 * tap_j + k].astype(F32)
                        tile = jnp.where(place.half == 1, pltpu.roll(tile, channels // 2, 1), tile).astype(BF16)
                    matrix[span, pl.ds((j * 4 + at) * channels, channels)] = tile
                    if at > 0:
                        low_matrix[span, pl.ds((j * 3 + at - 1) * channels, channels)] = tile
                    if at < 3:
                        high_matrix[span, pl.ds((j * 3 + at) * channels, channels)] = tile


def second_row(get, stored, halo, matrices, both, top):
    quarter = both.shape[0] // 2
    for x in range(0, COL_Y, 2):
        low, high = reach(x, 2, stored, halo)
        lhs = matrices[0]
        if high - low == 3:
            lhs = matrices[1] if x == 0 else matrices[2]
        taken = jnp.concatenate([piece for j in range(TAPS) for piece in get(j, low, high)], axis=0)
        partial = jnp.dot(lhs[...], taken, preferred_element_type=F32)
        done = finish(partial, both, top)
        yield x, done[:quarter], done[quarter:]


def halves(ref_a, ref_b, *at):
    *lead, low, high = at
    return [ref[(*lead, x)] for x in range(low, high) for ref in (ref_a, ref_b)]


def fill_bias(bias, both):
    quarter = bias.shape[1]
    column = jnp.broadcast_to(as_column(bias[...]), (quarter, both.shape[1]))
    both[:quarter] = column
    both[quarter:] = column


def second_inner_kernel(halo, heights, inner_a, inner_b, last_a, last_b, mate_a, mate_b, weights, bias, out, matrix, low_matrix, high_matrix, both):
    place = Place(heights)
    fill_second(weights, place, matrix, low_matrix, high_matrix)
    fill_bias(bias, both)
    matrices, width, top = (matrix, low_matrix, high_matrix), inner_a.shape[1], place.top()

    def pair(step, _):
        for more in range(2):
            u = step * 2 + more
            for x, here, beside in second_row(lambda j, a, b: halves(inner_a, inner_b, u + j, a, b), width, halo, matrices, both[:, 0:1], top):
                out[u, x] = here
                out[u, x + 1] = beside
        return 0

    lax.fori_loop(0, 2, pair, 0)

    def row(u, a, b):
        if u < 7:
            return halves(inner_a, inner_b, u - 1, a, b)
        return halves(last_a, last_b, a, b) if u == 7 else halves(mate_a, mate_b, a, b)

    for u in (6, 7):
        for x, here, beside in second_row(lambda j, a, b: row(u - 1 + j, a, b), width, halo, matrices, both[:, 0:1], top):
            out[u - 2, x] = here
            out[u - 2, x + 1] = beside


def last_kernel(halo, heights, own, cross, part_0, part_1, part_2, part_3, inner_a, inner_b, done_inner, weights, bias, out, matrix, low_matrix, high_matrix, bias_one, matrix_two, low_two, high_two, both, edge, done_edge):
    place = Place(heights)
    fill_first([part_0, part_1, part_2, part_3], [place.slots[0], place.slots[1], 2 + place.slots[2], 2 + place.slots[3]], place.odd, matrix, low_matrix, high_matrix, bias_one)
    fill_second(weights, place, matrix_two, low_two, high_two)
    fill_bias(bias, both)
    width = own.shape[1]

    def fields(u, a, b):
        return span_of(own, u, a, b) if u >= 0 else span_of(cross, -1 - u, a, b)

    for u in (-1, 0):
        for x, done in first_row(
            lambda j, a, b: fields(u - 1 + j, a, b),
            width,
            halo,
            (matrix, low_matrix, high_matrix),
            bias_one,
            lambda side: place.top(side, across=u < 0),
        ):
            edge[u + 1, x] = done

    def row(u, a, b):
        return [edge[u + 1, x] for x in range(a, b)] if u < 1 else halves(inner_a, inner_b, u - 1, a, b)

    for u in (0, 1):
        for x, here, beside in second_row(
            lambda j, a, b: row(u - 1 + j, a, b),
            inner_a.shape[1],
            halo,
            (matrix_two, low_two, high_two),
            both[:, 0:1],
            place.top(),
        ):
            done_edge[u, x] = here
            done_edge[u, x + 1] = beside
    quarter, depth = out.shape[1], out.shape[4]
    size = quarter * COL_Y
    at_row = lax.broadcasted_iota(jnp.int32, (size, size), 0)
    at_column = lax.broadcasted_iota(jnp.int32, (size, size), 1)
    y = lax.rem(at_row, COL_Y)
    u = jnp.where(place.odd == 1, COL_Y - 1 - y, y)
    swap = (at_column == u * quarter + lax.div(at_row, COL_Y)).astype(F32).astype(BF16)
    for x in range(COL_Y):
        tile = jnp.concatenate([done_edge[0, x], done_edge[1, x]] + [done_inner[v, x] for v in range(COL_Y - 2)], axis=0)
        moved = jnp.dot(swap, tile, preferred_element_type=F32).astype(BF16)
        out[0, :, x] = moved.reshape(quarter, COL_Y, depth)


def call(kernel, name, inputs, outputs, scratch, flops, *args):
    nbytes = sum(2 * a.size for a in args)
    return pl.pallas_call(
        kernel,
        out_shape=[jax.ShapeDtypeStruct(dims, BF16) for dims in outputs],
        in_specs=inputs,
        out_specs=[WHOLE] * len(outputs),
        scratch_shapes=scratch,
        compiler_params=pltpu.CompilerParams(vmem_limit_bytes=16 * 2**20),
        cost_estimate=pl.CostEstimate(flops=int(flops), bytes_accessed=int(nbytes), transcendentals=0),
        name=name,
    )(*args)


def pack(weights, bias):
    taps, rows, lanes = weights.shape
    return call(pack_kernel, "pack", [WHOLE, WHOLE], [(taps + 1, rows, lanes)], [], 0, weights, bias[None])[0]


def arrange(heights, features, after):
    _, channels, width, _, depth = features.shape
    row = (width, channels, depth)
    outputs = [(COL_Y, *row), (2, *row), row]
    inputs = [SCALARS, WHOLE, ANY]
    return call(arrange_kernel, "arrange", inputs, outputs, [], 512 * features.size, heights, features, after)


def first_scratch(channels, rows):
    wide = TAPS * channels
    return [
        pltpu.VMEM((TAPS * rows, 3 * wide), BF16),
        pltpu.VMEM((TAPS * rows, 2 * wide), BF16),
        pltpu.VMEM((TAPS * rows, 2 * wide), BF16),
        pltpu.VMEM((rows, 128), F32),
    ]


def second_scratch(channels, quarter):
    tall = TAPS * 2 * quarter
    return [
        pltpu.VMEM((tall, 12 * channels), BF16),
        pltpu.VMEM((tall, 9 * channels), BF16),
        pltpu.VMEM((tall, 9 * channels), BF16),
        pltpu.VMEM((2 * quarter, 128), F32),
    ]


def first_inner(halo, far, heights, own, mate, part_a, part_b, after):
    _, _, channels, depth = own.shape
    half, width = 2 * part_a.shape[1], COL_Y + 2 * halo
    kernel = functools.partial(first_inner_kernel, halo, far=far)
    inputs = [SCALARS] + [WHOLE] * 4 + [ANY]
    outputs = [(COL_Y - 2, width, half, depth), (width, half, depth)]
    flops = 2 * (COL_Y - 1) * COL_Y * depth * 27 * channels * half
    name = "first_far" if far else "first_near"
    return call(kernel, name, inputs, outputs, first_scratch(channels, half), flops, heights, own, mate, part_a, part_b, after)


def second_inner(halo, heights, inner_a, inner_b, last_a, last_b, mate_a, mate_b, weights, bias):
    rows, _, half, depth = inner_a.shape
    channels, quarter = 2 * half, weights.shape[1]
    kernel = functools.partial(second_inner_kernel, halo)
    flops = 2 * rows * COL_Y * depth * 27 * channels * quarter
    return call(
        kernel, "second_inner", [SCALARS] + [WHOLE] * 8, [(rows, COL_Y, quarter, depth)], second_scratch(channels, quarter), flops,
        heights, inner_a, inner_b, last_a, last_b, mate_a, mate_b, weights, bias[None],
    )[0]


def last(halo, heights, own, cross, parts, inner_a, inner_b, done_inner, weights, bias):
    _, _, channels, depth = own.shape
    quarter, width = weights.shape[1], COL_Y + 2 * halo
    kernel = functools.partial(last_kernel, halo)
    scratch = first_scratch(channels, channels) + second_scratch(channels, quarter)
    scratch += [pltpu.VMEM((2, width, channels, depth), BF16), pltpu.VMEM((2, COL_Y, quarter, depth), BF16)]
    flops = 4 * COL_Y * depth * 27 * channels * (channels + quarter)
    return call(
        kernel, "last", [SCALARS] + [WHOLE] * 11, [(1, quarter, COL_Y, COL_Y, depth)], scratch, flops,
        heights, own, cross, *parts, inner_a, inner_b, done_inner, weights, bias[None],
    )[0]


def across_pairs(peers):
    pairs = []
    for i in range(peers):
        to = i + 1 if i % 2 else i - 1
        if 0 <= to < peers and to // COL_Y == i // COL_Y:
            pairs.append((i, to))
    return pairs


def to_mate(value):
    return lax.ppermute(value, "space", [(i, i ^ 1) for i in range(lax.axis_size("space"))])


def far_pairs(peers, chans):
    pairs = []
    for i in range(peers):
        for c in range(chans):
            pairs.append((i * chans + c, i * chans + (c ^ (3 if i % 2 else 2))))
    return pairs


def with_x_borders(rows, peers):
    forth = [(i, i + COL_Y) for i in range(peers - COL_Y)]
    back = [(i + COL_Y, i) for i in range(peers - COL_Y)]
    before = lax.ppermute(rows[:, COL_Y - 2 :], "space", forth)
    behind = lax.ppermute(rows[:, :2], "space", back)
    return jnp.concatenate([before, rows, behind], axis=1)


def on_device(features, column_heights, weight_one, bias_one, weight_two, bias_two):
    peers, chans = lax.axis_size("space"), lax.axis_size("chan")
    halo = 1 if peers > COL_Y else 0

    own_part = pack(weight_one, bias_one)
    far_part = lax.ppermute(own_part, ("space", "chan"), far_pairs(peers, chans))
    near_part = lax.ppermute(own_part, "chan", [(c, c ^ 1) for c in range(chans)])
    fields, cross, mate = arrange(column_heights, features, own_part)
    cross = lax.ppermute(cross, "space", across_pairs(peers))
    mate = to_mate(mate)
    if halo:
        fields = with_x_borders(jnp.concatenate([cross, fields, mate[None]], axis=0), peers)
        cross, fields, mate = fields[:2], fields[2:-1], fields[-1]

    inner_a, last_a = first_inner(halo, False, column_heights, fields, mate, own_part, near_part, mate)
    mate_a = to_mate(last_a)
    other_part = to_mate(far_part)
    inner_b, last_b = first_inner(halo, True, column_heights, fields, mate, far_part, other_part, last_a)
    mate_b = to_mate(last_b)
    done_inner = second_inner(
        halo, column_heights, inner_a, inner_b, last_a, last_b, mate_a, mate_b, weight_two, bias_two
    )
    parts = (own_part, near_part, far_part, other_part)
    return last(halo, column_heights, fields, cross, parts, inner_a, inner_b, done_inner, weight_two, bias_two)


def solution(mesh):
    placed = (
        P("space", None, None, None, None),
        P(),
        P(None, "chan", None),
        P("chan"),
        P(None, "chan", None),
        P("chan"),
    )
    return jax.shard_map(
        on_device,
        mesh=mesh,
        in_specs=placed,
        out_specs=P("space", "chan", None, None, None),
        check_vma=False,
    )
```

```python
import functools

import jax
import jax.numpy as jnp
from jax import lax
from jax.experimental import pallas as pl
from jax.experimental.pallas import tpu as pltpu
from jax.sharding import PartitionSpec as P

COL_Y = 8
TAPS = 3
BF16 = jnp.bfloat16
F32 = jnp.float32
ANY = pl.BlockSpec(memory_space=pl.ANY)
WHOLE = pl.BlockSpec(memory_space=pltpu.VMEM)
SCALARS = pl.BlockSpec(memory_space=pltpu.SMEM)


class Place:
    def __init__(self, heights):
        self.heights = heights
        self.column = lax.axis_index("space")
        self.peers = lax.axis_size("space")
        self.odd = lax.rem(self.column, 2)
        chan = lax.axis_index("chan")
        self.half = lax.div(chan, 2)
        near = lax.rem(chan, 2)
        far = jnp.where(self.odd == 1, 1 - near, near)
        self.slots = (near, 1 - near, far, 1 - far)

    def top(self, by_x=0, across=False):
        column, inside = self.column, True
        if across:
            y = lax.rem(column, COL_Y)
            step = jnp.where(self.odd == 1, 1, -1)
            inside = (y + step >= 0) & (y + step < COL_Y)
            column = column + step
        if by_x:
            column = column + by_x * COL_Y
            inside = inside & (column >= 0) & (column < self.peers)
        column = jnp.clip(column, 0, self.peers - 1)
        return jnp.where(inside, self.heights[column] * 8, 0)


def as_column(row):
    size = row.shape[1]
    wide = jnp.broadcast_to(row, (size, size))
    same = lax.broadcasted_iota(jnp.int32, (size, size), 0) == lax.broadcasted_iota(jnp.int32, (size, size), 1)
    return jnp.sum(jnp.where(same, wide, 0.0), axis=1, keepdims=True)


def prepare_kernel(heights, weights, bias, features, packed, fields, cross, mate, bias_here, stored, sems):
    _, channels, width, _, depth = features.shape
    taps, rows, lanes = weights.shape
    copies = [
        pltpu.make_async_copy(bias, bias_here, sems.at[width]),
        pltpu.make_async_copy(weights, packed.at[pl.ds(0, taps)], sems.at[width + 1]),
    ]
    copies += [pltpu.make_async_copy(features.at[0, :, x], stored.at[x], sems.at[x]) for x in range(width)]
    for copy in copies:
        copy.start()
    place = Place(heights)
    group = 256 // COL_Y
    row = lax.broadcasted_iota(jnp.int32, (256, 256), 0)
    column = lax.broadcasted_iota(jnp.int32, (256, 256), 1)
    u = lax.div(row, group)
    y = jnp.where(place.odd == 1, COL_Y - 1 - u, u)
    swap = (column == lax.rem(row, group) * COL_Y + y).astype(F32).astype(BF16)
    live = lax.broadcasted_iota(jnp.int32, (1, depth), 1) < place.top()

    copies[0].wait()
    column = as_column(bias_here[...])
    lane = lax.broadcasted_iota(jnp.int32, (rows, lanes), 1)
    extra = jnp.zeros((rows, lanes), F32)
    for at in range(3):
        piece = column.astype(BF16).astype(F32)
        extra = jnp.where(lane == at, piece, extra)
        column = column - piece
    packed[taps] = extra.astype(BF16)
    copies[1].wait()

    for x in range(width):
        copies[2 + x].wait()
        for first in range(0, channels, group):
            tile = stored[x, first : first + group].reshape(256, depth)
            moved = jnp.dot(swap, tile, preferred_element_type=F32)
            moved = jnp.where(live, moved, 0.0).astype(BF16).reshape(COL_Y, group, depth)
            fields[:, x, first : first + group] = moved
            cross[:, x, first : first + group] = moved[:2]
            mate[x, first : first + group] = moved[COL_Y - 1]


def finish(partial, bias, live_top):
    rows, depth = partial.shape[0] // TAPS, partial.shape[1]
    z = lax.broadcasted_iota(jnp.int32, (rows, depth), 1)
    below = jnp.where(z == 0, 0.0, pltpu.roll(partial[:rows], 1, 1))
    above = jnp.where(z == depth - 1, 0.0, pltpu.roll(partial[2 * rows :], depth - 1, 1))
    total = jnp.maximum(below + partial[rows : 2 * rows] + above + bias, 0.0)
    return jnp.where(z < live_top, total, 0.0).astype(BF16)


def fill_first(parts, slots, odd, matrix, low_matrix, high_matrix, bias):
    quarter, channels = parts[0].shape[1], parts[0].shape[2]
    block = quarter * len(parts)
    for part, slot in zip(parts, slots, strict=True):
        at = slot * quarter
        for k in range(TAPS):
            span = pl.ds(pl.multiple_of(k * block + at, quarter), quarter)
            for j in range(TAPS):
                tap_j = jnp.where(odd == 1, 2 - j, j)
                for i in range(TAPS):
                    tile = part[9 * i + 3 * tap_j + k]
                    matrix[span, pl.ds((j * TAPS + i) * channels, channels)] = tile
                    if i > 0:
                        low_matrix[span, pl.ds((j * 2 + i - 1) * channels, channels)] = tile
                    if i < 2:
                        high_matrix[span, pl.ds((j * 2 + i) * channels, channels)] = tile
        extra = part[27].astype(F32)
        value = extra[:, 0:1] + extra[:, 1:2] + extra[:, 2:3]
        bias[pl.ds(pl.multiple_of(at, quarter), quarter), :] = jnp.broadcast_to(value, (quarter, bias.shape[1]))


def reach(x, width, stored, pad):
    return max(x - 1 + pad, 0), min(x + width + 1 + pad, stored)


def first_row(get, stored, halo, matrices, bias, top):
    for x in range(-halo, COL_Y + halo):
        low, high = reach(x, 1, stored, 2 * halo)
        lhs = matrices[0]
        if high - low == 2:
            lhs = matrices[1] if x == 0 else matrices[2]
        taken = jnp.concatenate([get(j, low, high) for j in range(TAPS)], axis=0)
        partial = jnp.dot(lhs[...], taken, preferred_element_type=F32)
        side = -1 if x < 0 else 1 if x >= COL_Y else 0
        yield x + halo, finish(partial, bias[:, 0:1], top(side))


def span_of(ref, *at):
    *lead, low, high = at
    value = ref[(*lead, slice(low, high))]
    return value.reshape(-1, value.shape[-1])


def first_inner_kernel(halo, heights, own, mate, part_a, part_b, after, out, out_last, matrix, low_matrix, high_matrix, bias, *, far):
    place = Place(heights)
    slots = place.slots[2:] if far else place.slots[:2]
    fill_first([part_a, part_b], slots, place.odd, matrix, low_matrix, high_matrix, bias)
    matrices, width = (matrix, low_matrix, high_matrix), own.shape[1]

    def pair(step, _):
        for more in range(2):
            u = step * 2 + more
            for x, done in first_row(lambda j, a, b: span_of(own, u + j, a, b), width, halo, matrices, bias, place.top):
                out[u, x] = done
        return 0

    lax.fori_loop(0, (COL_Y - 2) // 2, pair, 0)

    def get(j, a, b):
        return span_of(mate, a, b) if j == 2 else span_of(own, COL_Y - 2 + j, a, b)

    for x, done in first_row(get, width, halo, matrices, bias, place.top):
        out_last[x] = done


def fill_second(weights, place, matrix, low_matrix, high_matrix):
    quarter, channels = weights.shape[1], weights.shape[2]
    empty = jnp.zeros((quarter, channels), BF16)
    for k in range(TAPS):
        for to in range(2):
            span = pl.ds((k * 2 + to) * quarter, quarter)
            for j in range(TAPS):
                tap_j = jnp.where(place.odd == 1, 2 - j, j)
                for at in range(4):
                    tile = empty
                    if 0 <= at - to < TAPS:
                        tile = weights[9 * (at - to) + 3 * tap_j + k].astype(F32)
                        tile = jnp.where(place.half == 1, pltpu.roll(tile, channels // 2, 1), tile).astype(BF16)
                    matrix[span, pl.ds((j * 4 + at) * channels, channels)] = tile
                    if at > 0:
                        low_matrix[span, pl.ds((j * 3 + at - 1) * channels, channels)] = tile
                    if at < 3:
                        high_matrix[span, pl.ds((j * 3 + at) * channels, channels)] = tile


def second_row(get, stored, halo, matrices, both, top):
    quarter = both.shape[0] // 2
    for x in range(0, COL_Y, 2):
        low, high = reach(x, 2, stored, halo)
        lhs = matrices[0]
        if high - low == 3:
            lhs = matrices[1] if x == 0 else matrices[2]
        taken = jnp.concatenate([piece for j in range(TAPS) for piece in get(j, low, high)], axis=0)
        partial = jnp.dot(lhs[...], taken, preferred_element_type=F32)
        done = finish(partial, both, top)
        yield x, done[:quarter], done[quarter:]


def halves(ref_a, ref_b, *at):
    *lead, low, high = at
    return [ref[(*lead, x)] for x in range(low, high) for ref in (ref_a, ref_b)]


def fill_bias(bias, both):
    quarter = bias.shape[1]
    column = jnp.broadcast_to(as_column(bias[...]), (quarter, both.shape[1]))
    both[:quarter] = column
    both[quarter:] = column


def fill_kernel(heights, weights, bias, after, matrix, low_matrix, high_matrix, both):
    fill_second(weights, Place(heights), matrix, low_matrix, high_matrix)
    fill_bias(bias, both)


def second_inner_kernel(halo, heights, inner_a, inner_b, last_a, last_b, matrix, low_matrix, high_matrix, both, out):
    place = Place(heights)
    matrices, width, top = (matrix, low_matrix, high_matrix), inner_a.shape[1], place.top()

    def pair(step, _):
        for more in range(2):
            u = step * 2 + more
            for x, here, beside in second_row(lambda j, a, b: halves(inner_a, inner_b, u + j, a, b), width, halo, matrices, both[:, 0:1], top):
                out[u, x] = here
                out[u, x + 1] = beside
        return 0

    lax.fori_loop(0, 2, pair, 0)

    def row(u, a, b):
        return halves(inner_a, inner_b, u - 1, a, b) if u < 7 else halves(last_a, last_b, a, b)

    for x, here, beside in second_row(lambda j, a, b: row(5 + j, a, b), width, halo, matrices, both[:, 0:1], top):
        out[4, x] = here
        out[4, x + 1] = beside


def last_kernel(
    halo, heights, own, cross, part_0, part_1, part_2, part_3, inner_a, inner_b, last_a, last_b, mate_a, mate_b,
    done_inner, matrix_two, low_two, high_two, both, out, matrix, low_matrix, high_matrix, bias_one, edge, done_edge,
):
    place = Place(heights)
    fill_first([part_0, part_1, part_2, part_3], [place.slots[0], place.slots[1], 2 + place.slots[2], 2 + place.slots[3]], place.odd, matrix, low_matrix, high_matrix, bias_one)
    width, depth = own.shape[1], own.shape[3]
    matrices = (matrix, low_matrix, high_matrix)

    def fields(u, a, b):
        return span_of(own, u, a, b) if u >= 0 else span_of(cross, -1 - u, a, b)

    def edge_row(u, levels):
        def top(side):
            return place.top(side, across=u < 0)

        def get(j, a, b):
            return fields(u - 1 + j, a, b)[:, :levels]

        for x, done in first_row(get, width, halo, matrices, bias_one, top):
            edge[u + 1, x, :, :levels] = done
            if levels < depth:
                edge[u + 1, x, :, levels:] = jnp.zeros((done.shape[0], depth - levels), BF16)

    part = depth // 2 if depth % 256 == 0 else depth
    highest = place.top(0, across=True)
    if halo:
        highest = jnp.maximum(highest, jnp.maximum(place.top(-1, across=True), place.top(1, across=True)))
    low = highest < part

    @pl.when(low)
    def _():
        edge_row(-1, part)

    @pl.when(jnp.logical_not(low))
    def _():
        edge_row(-1, depth)

    edge_row(0, depth)

    def row(u, a, b):
        if u < 1:
            return [edge[u + 1, x] for x in range(a, b)]
        if u < 7:
            return halves(inner_a, inner_b, u - 1, a, b)
        return halves(last_a, last_b, a, b) if u == 7 else halves(mate_a, mate_b, a, b)

    for at, u in enumerate((0, 1, 7)):
        for x, here, beside in second_row(
            lambda j, a, b: row(u - 1 + j, a, b),
            inner_a.shape[1],
            halo,
            (matrix_two, low_two, high_two),
            both[:, 0:1],
            place.top(),
        ):
            done_edge[at, x] = here
            done_edge[at, x + 1] = beside
    quarter = out.shape[1]
    size = quarter * COL_Y
    at_row = lax.broadcasted_iota(jnp.int32, (size, size), 0)
    at_column = lax.broadcasted_iota(jnp.int32, (size, size), 1)
    y = lax.rem(at_row, COL_Y)
    u = jnp.where(place.odd == 1, COL_Y - 1 - y, y)
    swap = (at_column == u * quarter + lax.div(at_row, COL_Y)).astype(F32).astype(BF16)
    for x in range(COL_Y):
        tiles = [done_edge[0, x], done_edge[1, x]] + [done_inner[v, x] for v in range(COL_Y - 3)] + [done_edge[2, x]]
        tile = jnp.concatenate(tiles, axis=0)
        moved = jnp.dot(swap, tile, preferred_element_type=F32).astype(BF16)
        out[0, :, x] = moved.reshape(quarter, COL_Y, depth)


def call(kernel, name, inputs, outputs, scratch, flops, *args, kinds=None, vmem=16):
    nbytes = sum(2 * a.size for a in args)
    return pl.pallas_call(
        kernel,
        out_shape=[jax.ShapeDtypeStruct(*each) for each in zip(outputs, kinds or [BF16] * len(outputs))],
        in_specs=inputs,
        out_specs=[WHOLE] * len(outputs),
        scratch_shapes=scratch,
        compiler_params=pltpu.CompilerParams(vmem_limit_bytes=vmem * 2**20),
        cost_estimate=pl.CostEstimate(flops=0, bytes_accessed=0, transcendentals=0),
        name=name,
    )(*args)


def prepare(heights, weights, bias, features):
    _, channels, width, _, depth = features.shape
    taps, rows, lanes = weights.shape
    row = (width, channels, depth)
    outputs = [(taps + 1, rows, lanes), (COL_Y, *row), (2, *row), row]
    scratch = [
        pltpu.VMEM((1, rows), F32),
        pltpu.VMEM((width, channels, COL_Y, depth), BF16),
        pltpu.SemaphoreType.DMA((width + 2,)),
    ]
    inputs = [SCALARS, ANY, ANY, ANY]
    return call(prepare_kernel, "prepare", inputs, outputs, scratch, 0, heights, weights, bias[None], features, vmem=47)


def first_scratch(channels, rows):
    wide = TAPS * channels
    return [
        pltpu.VMEM((TAPS * rows, 3 * wide), BF16),
        pltpu.VMEM((TAPS * rows, 2 * wide), BF16),
        pltpu.VMEM((TAPS * rows, 2 * wide), BF16),
        pltpu.VMEM((rows, 128), F32),
    ]


def fill(heights, weights, bias, after):
    quarter, channels = weights.shape[1], weights.shape[2]
    tall = TAPS * 2 * quarter
    outputs = [(tall, 12 * channels), (tall, 9 * channels), (tall, 9 * channels), (2 * quarter, 128)]
    kinds = [BF16, BF16, BF16, F32]
    return call(fill_kernel, "fill", [SCALARS, WHOLE, WHOLE, ANY], outputs, [], 0, heights, weights, bias[None], after, kinds=kinds)


def first_inner(halo, far, heights, own, mate, part_a, part_b, after):
    _, _, channels, depth = own.shape
    half, width = 2 * part_a.shape[1], COL_Y + 2 * halo
    kernel = functools.partial(first_inner_kernel, halo, far=far)
    inputs = [SCALARS] + [WHOLE] * 4 + [ANY]
    outputs = [(COL_Y - 2, width, half, depth), (width, half, depth)]
    flops = 2 * (COL_Y - 1) * COL_Y * depth * 27 * channels * half
    name = "first_far" if far else "first_near"
    return call(kernel, name, inputs, outputs, first_scratch(channels, half), flops, heights, own, mate, part_a, part_b, after)


def second_inner(halo, heights, inner_a, inner_b, last_a, last_b, matrices):
    rows, _, half, depth = inner_a.shape
    quarter = matrices[-1].shape[0] // 2
    kernel = functools.partial(second_inner_kernel, halo)
    flops = 2 * (rows - 1) * COL_Y * depth * 27 * 2 * half * quarter
    outputs = [(rows - 1, COL_Y, quarter, depth)]
    args = (heights, inner_a, inner_b, last_a, last_b, *matrices)
    return call(kernel, "second_inner", [SCALARS] + [WHOLE] * 8, outputs, [], flops, *args)[0]


def last(halo, heights, own, cross, parts, hidden, done_inner, matrices):
    _, _, channels, depth = own.shape
    quarter, width = matrices[-1].shape[0] // 2, COL_Y + 2 * halo
    kernel = functools.partial(last_kernel, halo)
    scratch = first_scratch(channels, channels)
    scratch += [pltpu.VMEM((2, width, channels, depth), BF16), pltpu.VMEM((3, COL_Y, quarter, depth), BF16)]
    flops = 4 * COL_Y * depth * 27 * channels * (channels + quarter)
    outputs = [(1, quarter, COL_Y, COL_Y, depth)]
    args = (heights, own, cross, *parts, *hidden, done_inner, *matrices)
    return call(kernel, "last", [SCALARS] + [WHOLE] * (len(args) - 1), outputs, scratch, flops, *args)[0]


def across_pairs(peers):
    pairs = []
    for i in range(peers):
        to = i + 1 if i % 2 else i - 1
        if 0 <= to < peers and to // COL_Y == i // COL_Y:
            pairs.append((i, to))
    return pairs


def to_mate(value):
    return lax.ppermute(value, "space", [(i, i ^ 1) for i in range(lax.axis_size("space"))])


def far_pairs(peers, chans):
    pairs = []
    for i in range(peers):
        for c in range(chans):
            pairs.append((i * chans + c, i * chans + (c ^ (3 if i % 2 else 2))))
    return pairs


def with_x_borders(rows, peers):
    forth = [(i, i + COL_Y) for i in range(peers - COL_Y)]
    back = [(i + COL_Y, i) for i in range(peers - COL_Y)]
    before = lax.ppermute(rows[:, COL_Y - 2 :], "space", forth)
    behind = lax.ppermute(rows[:, :2], "space", back)
    return jnp.concatenate([before, rows, behind], axis=1)


def on_device(features, column_heights, weight_one, bias_one, weight_two, bias_two):
    peers, chans = lax.axis_size("space"), lax.axis_size("chan")
    halo = 1 if peers > COL_Y else 0

    own_part, fields, cross, mate = prepare(column_heights, weight_one, bias_one, features)
    far_part = lax.ppermute(own_part, ("space", "chan"), far_pairs(peers, chans))
    near_part = lax.ppermute(own_part, "chan", [(c, c ^ 1) for c in range(chans)])
    cross = lax.ppermute(cross, "space", across_pairs(peers))
    mate = to_mate(mate)
    if halo:
        fields = with_x_borders(jnp.concatenate([cross, fields, mate[None]], axis=0), peers)
        cross, fields, mate = fields[:2], fields[2:-1], fields[-1]

    matrices = fill(column_heights, weight_two, bias_two, mate)
    inner_a, last_a = first_inner(halo, False, column_heights, fields, mate, own_part, near_part, matrices[-1])
    mate_a = to_mate(last_a)
    far_part, last_a = lax.optimization_barrier((far_part, last_a))
    other_part = to_mate(far_part)
    inner_b, last_b = first_inner(halo, True, column_heights, fields, mate, far_part, other_part, last_a)
    mate_b = to_mate(last_b)
    done_inner = second_inner(halo, column_heights, inner_a, inner_b, last_a, last_b, matrices)
    parts = (own_part, near_part, far_part, other_part)
    hidden = (inner_a, inner_b, last_a, last_b, mate_a, mate_b)
    return last(halo, column_heights, fields, cross, parts, hidden, done_inner, matrices)


def solution(mesh):
    placed = (
        P("space", None, None, None, None),
        P(),
        P(None, "chan", None),
        P("chan"),
        P(None, "chan", None),
        P("chan"),
    )
    return jax.shard_map(
        on_device,
        mesh=mesh,
        in_specs=placed,
        out_specs=P("space", "chan", None, None, None),
        check_vma=False,
    )
```

```python
import functools

import jax
import jax.numpy as jnp
from jax import lax
from jax.experimental import pallas as pl
from jax.experimental.pallas import tpu as pltpu
from jax.sharding import PartitionSpec as P

COL_Y = 8
TAPS = 3
BF16 = jnp.bfloat16
F32 = jnp.float32
ANY = pl.BlockSpec(memory_space=pl.ANY)
WHOLE = pl.BlockSpec(memory_space=pltpu.VMEM)
SCALARS = pl.BlockSpec(memory_space=pltpu.SMEM)


class Place:
    def __init__(self, heights):
        self.heights = heights
        self.column = lax.axis_index("space")
        self.peers = lax.axis_size("space")
        self.odd = lax.rem(self.column, 2)
        chan = lax.axis_index("chan")
        self.half = lax.div(chan, 2)
        near = lax.rem(chan, 2)
        far = jnp.where(self.odd == 1, 1 - near, near)
        self.slots = (near, 1 - near, far, 1 - far)

    def top(self, by_x=0, across=False):
        column, inside = self.column, True
        if across:
            y = lax.rem(column, COL_Y)
            step = jnp.where(self.odd == 1, 1, -1)
            inside = (y + step >= 0) & (y + step < COL_Y)
            column = column + step
        if by_x:
            column = column + by_x * COL_Y
            inside = inside & (column >= 0) & (column < self.peers)
        column = jnp.clip(column, 0, self.peers - 1)
        return jnp.where(inside, self.heights[column] * 8, 0)


def as_column(row):
    size = row.shape[1]
    wide = jnp.broadcast_to(row, (size, size))
    same = lax.broadcasted_iota(jnp.int32, (size, size), 0) == lax.broadcasted_iota(jnp.int32, (size, size), 1)
    return jnp.sum(jnp.where(same, wide, 0.0), axis=1, keepdims=True)


def pack_kernel(weights, bias, packed):
    taps, rows, lanes = weights.shape
    packed[:taps] = weights[...]
    column = as_column(bias[...])
    lane = lax.broadcasted_iota(jnp.int32, (rows, lanes), 1)
    extra = jnp.zeros((rows, lanes), F32)
    for at in range(3):
        piece = column.astype(BF16).astype(F32)
        extra = jnp.where(lane == at, piece, extra)
        column = column - piece
    packed[taps] = extra.astype(BF16)


def arrange_kernel(heights, features, after, fields, cross, mate):
    _, channels, width, _, depth = features.shape
    place = Place(heights)
    group = 256 // COL_Y
    row = lax.broadcasted_iota(jnp.int32, (256, 256), 0)
    column = lax.broadcasted_iota(jnp.int32, (256, 256), 1)
    u = lax.div(row, group)
    y = jnp.where(place.odd == 1, COL_Y - 1 - u, u)
    swap = (column == lax.rem(row, group) * COL_Y + y).astype(F32).astype(BF16)
    live = lax.broadcasted_iota(jnp.int32, (1, depth), 1) < place.top()
    for x in range(width):
        for first in range(0, channels, group):
            tile = features[0, first : first + group, x].reshape(256, depth)
            moved = jnp.dot(swap, tile, preferred_element_type=F32)
            moved = jnp.where(live, moved, 0.0).astype(BF16).reshape(COL_Y, group, depth)
            fields[:, x, first : first + group] = moved
            cross[:, x, first : first + group] = moved[:2]
            mate[x, first : first + group] = moved[COL_Y - 1]


def finish(partial, bias, live_top):
    rows, depth = partial.shape[0] // TAPS, partial.shape[1]
    z = lax.broadcasted_iota(jnp.int32, (rows, depth), 1)
    below = jnp.where(z == 0, 0.0, pltpu.roll(partial[:rows], 1, 1))
    above = jnp.where(z == depth - 1, 0.0, pltpu.roll(partial[2 * rows :], depth - 1, 1))
    total = jnp.maximum(below + partial[rows : 2 * rows] + above + bias, 0.0)
    return jnp.where(z < live_top, total, 0.0).astype(BF16)


def fill_first(parts, slots, odd, matrix, low_matrix, high_matrix, bias):
    quarter, channels = parts[0].shape[1], parts[0].shape[2]
    block = quarter * len(parts)
    for part, slot in zip(parts, slots, strict=True):
        at = slot * quarter
        for k in range(TAPS):
            span = pl.ds(pl.multiple_of(k * block + at, quarter), quarter)
            for j in range(TAPS):
                tap_j = jnp.where(odd == 1, 2 - j, j)
                for i in range(TAPS):
                    tile = part[9 * i + 3 * tap_j + k]
                    matrix[span, pl.ds((j * TAPS + i) * channels, channels)] = tile
                    if i > 0:
                        low_matrix[span, pl.ds((j * 2 + i - 1) * channels, channels)] = tile
                    if i < 2:
                        high_matrix[span, pl.ds((j * 2 + i) * channels, channels)] = tile
        extra = part[27].astype(F32)
        value = extra[:, 0:1] + extra[:, 1:2] + extra[:, 2:3]
        bias[pl.ds(pl.multiple_of(at, quarter), quarter), :] = jnp.broadcast_to(value, (quarter, bias.shape[1]))


def reach(x, width, stored, pad):
    return max(x - 1 + pad, 0), min(x + width + 1 + pad, stored)


def first_row(get, stored, halo, matrices, bias, top):
    for x in range(-halo, COL_Y + halo):
        low, high = reach(x, 1, stored, 2 * halo)
        lhs = matrices[0]
        if high - low == 2:
            lhs = matrices[1] if x == 0 else matrices[2]
        taken = jnp.concatenate([get(j, low, high) for j in range(TAPS)], axis=0)
        partial = jnp.dot(lhs[...], taken, preferred_element_type=F32)
        side = -1 if x < 0 else 1 if x >= COL_Y else 0
        yield x + halo, finish(partial, bias[:, 0:1], top(side))


def span_of(ref, *at):
    *lead, low, high = at
    value = ref[(*lead, slice(low, high))]
    return value.reshape(-1, value.shape[-1])


def inner_rows(own, out, halo, matrices, bias, top):
    def pair(step, _):
        for more in range(2):
            u = step * 2 + more
            for x, done in first_row(lambda j, a, b: span_of(own, u + j, a, b), own.shape[1], halo, matrices, bias, top):
                out[u, x] = done
        return 0

    lax.fori_loop(0, (COL_Y - 2) // 2, pair, 0)


def first_near_kernel(halo, heights, own, part_a, part_b, after, out, matrix, low_matrix, high_matrix, bias):
    place = Place(heights)
    fill_first([part_a, part_b], place.slots[:2], place.odd, matrix, low_matrix, high_matrix, bias)
    inner_rows(own, out, halo, (matrix, low_matrix, high_matrix), bias, place.top)


def first_far_kernel(
    halo, heights, own, mate, part_a, part_b, near, low_near, high_near, bias_near, after,
    out, out_last, matrix, low_matrix, high_matrix, bias,
):
    place = Place(heights)
    fill_first([part_a, part_b], place.slots[2:], place.odd, matrix, low_matrix, high_matrix, bias)
    far = (matrix, low_matrix, high_matrix)
    inner_rows(own, out, halo, far, bias, place.top)

    def get(j, a, b):
        return span_of(mate, a, b) if j == 2 else span_of(own, COL_Y - 2 + j, a, b)

    whole_row(get, own.shape[1], halo, ((near, low_near, high_near), bias_near), (far, bias), place.top, out_last)


def whole_row(get, stored, halo, near, far, top, out, *at):
    half = near[1].shape[0]
    levels = None
    for first, (matrices, bias) in ((0, near), (half, far)):
        for x, done in first_row(get, stored, halo, matrices, bias, top):
            levels = done.shape[1]
            out[(*at, x, slice(first, first + half), slice(0, levels))] = done


def fill_second(weights, place, matrix, low_matrix, high_matrix):
    quarter, channels = weights.shape[1], weights.shape[2]
    empty = jnp.zeros((quarter, channels), BF16)
    for k in range(TAPS):
        for to in range(2):
            span = pl.ds((k * 2 + to) * quarter, quarter)
            for j in range(TAPS):
                tap_j = jnp.where(place.odd == 1, 2 - j, j)
                for at in range(4):
                    tile = empty
                    if 0 <= at - to < TAPS:
                        tile = weights[9 * (at - to) + 3 * tap_j + k].astype(F32)
                        tile = jnp.where(place.half == 1, pltpu.roll(tile, channels // 2, 1), tile).astype(BF16)
                    matrix[span, pl.ds((j * 4 + at) * channels, channels)] = tile
                    if at > 0:
                        low_matrix[span, pl.ds((j * 3 + at - 1) * channels, channels)] = tile
                    if at < 3:
                        high_matrix[span, pl.ds((j * 3 + at) * channels, channels)] = tile


def second_row(get, stored, halo, matrices, both, top):
    quarter = both.shape[0] // 2
    for x in range(0, COL_Y, 2):
        low, high = reach(x, 2, stored, halo)
        lhs = matrices[0]
        if high - low == 3:
            lhs = matrices[1] if x == 0 else matrices[2]
        taken = jnp.concatenate([piece for j in range(TAPS) for piece in get(j, low, high)], axis=0)
        partial = jnp.dot(lhs[...], taken, preferred_element_type=F32)
        done = finish(partial, both, top)
        yield x, done[:quarter], done[quarter:]


def halves(ref_a, ref_b, *at):
    *lead, low, high = at
    return [ref[(*lead, x)] for x in range(low, high) for ref in (ref_a, ref_b)]


def fill_bias(bias, both):
    quarter = bias.shape[1]
    column = jnp.broadcast_to(as_column(bias[...]), (quarter, both.shape[1]))
    both[:quarter] = column
    both[quarter:] = column


def fill_kernel(heights, weights, bias, after, matrix, low_matrix, high_matrix, both):
    fill_second(weights, Place(heights), matrix, low_matrix, high_matrix)
    fill_bias(bias, both)


def second_inner_kernel(halo, heights, inner_a, inner_b, row_seven, matrix, low_matrix, high_matrix, both, out):
    place = Place(heights)
    matrices, width, top = (matrix, low_matrix, high_matrix), inner_a.shape[1], place.top()

    def pair(step, _):
        for more in range(2):
            u = step * 2 + more
            for x, here, beside in second_row(lambda j, a, b: halves(inner_a, inner_b, u + j, a, b), width, halo, matrices, both[:, 0:1], top):
                out[u, x] = here
                out[u, x + 1] = beside
        return 0

    lax.fori_loop(0, 2, pair, 0)

    def row(u, a, b):
        return halves(inner_a, inner_b, u - 1, a, b) if u < 7 else [row_seven[x] for x in range(a, b)]

    for x, here, beside in second_row(lambda j, a, b: row(5 + j, a, b), width, halo, matrices, both[:, 0:1], top):
        out[4, x] = here
        out[4, x + 1] = beside


def last_kernel(
    halo, heights, own, cross, near, low_near, high_near, bias_near, far, low_far, high_far, bias_far,
    inner_a, inner_b, row_seven, mate, done_inner, matrix_two, low_two, high_two, both, out, edge, done_edge,
):
    place = Place(heights)
    width, depth = own.shape[1], own.shape[3]
    near, far = ((near, low_near, high_near), bias_near), ((far, low_far, high_far), bias_far)

    def fields(u, a, b):
        return span_of(own, u, a, b) if u >= 0 else span_of(cross, -1 - u, a, b)

    def edge_row(u, levels):
        def top(side):
            return place.top(side, across=u < 0)

        def get(j, a, b):
            return fields(u - 1 + j, a, b)[:, :levels]

        whole_row(get, width, halo, near, far, top, edge, u + 1)
        if levels < depth:
            edge[u + 1, :, :, levels:] = jnp.zeros((*edge.shape[1:3], depth - levels), BF16)

    part = depth // 2 if depth % 256 == 0 else depth
    highest = place.top(0, across=True)
    if halo:
        highest = jnp.maximum(highest, jnp.maximum(place.top(-1, across=True), place.top(1, across=True)))
    low = highest < part

    @pl.when(low)
    def _():
        edge_row(-1, part)

    @pl.when(jnp.logical_not(low))
    def _():
        edge_row(-1, depth)

    edge_row(0, depth)

    def row(u, a, b):
        if u < 1:
            return [edge[u + 1, x] for x in range(a, b)]
        if u < 7:
            return halves(inner_a, inner_b, u - 1, a, b)
        return [(row_seven if u == 7 else mate)[x] for x in range(a, b)]

    for at, u in enumerate((0, 1, 7)):
        for x, here, beside in second_row(
            lambda j, a, b: row(u - 1 + j, a, b),
            inner_a.shape[1],
            halo,
            (matrix_two, low_two, high_two),
            both[:, 0:1],
            place.top(),
        ):
            done_edge[at, x] = here
            done_edge[at, x + 1] = beside
    quarter = out.shape[1]
    size = quarter * COL_Y
    at_row = lax.broadcasted_iota(jnp.int32, (size, size), 0)
    at_column = lax.broadcasted_iota(jnp.int32, (size, size), 1)
    y = lax.rem(at_row, COL_Y)
    u = jnp.where(place.odd == 1, COL_Y - 1 - y, y)
    swap = (at_column == u * quarter + lax.div(at_row, COL_Y)).astype(F32).astype(BF16)
    for x in range(COL_Y):
        tiles = [done_edge[0, x], done_edge[1, x]] + [done_inner[v, x] for v in range(COL_Y - 3)] + [done_edge[2, x]]
        tile = jnp.concatenate(tiles, axis=0)
        moved = jnp.dot(swap, tile, preferred_element_type=F32).astype(BF16)
        out[0, :, x] = moved.reshape(quarter, COL_Y, depth)


SHORT, LONG = 2**6, 2**27


def call(kernel, name, inputs, outputs, scratch, nbytes, *args, kinds=None):
    return pl.pallas_call(
        kernel,
        out_shape=[jax.ShapeDtypeStruct(*each) for each in zip(outputs, kinds or [BF16] * len(outputs))],
        in_specs=inputs,
        out_specs=[WHOLE] * len(outputs),
        scratch_shapes=scratch,
        compiler_params=pltpu.CompilerParams(vmem_limit_bytes=16 * 2**20),
        cost_estimate=pl.CostEstimate(flops=64 * nbytes, bytes_accessed=nbytes, transcendentals=0),
        name=name,
    )(*args)


def pack(weights, bias):
    taps, rows, lanes = weights.shape
    return call(pack_kernel, "pack", [WHOLE, WHOLE], [(taps + 1, rows, lanes)], [], LONG, weights, bias[None])[0]


def arrange(heights, features, after):
    _, channels, width, _, depth = features.shape
    row = (width, channels, depth)
    outputs = [(COL_Y, *row), (2, *row), row]
    return call(arrange_kernel, "arrange", [SCALARS, WHOLE, ANY], outputs, [], SHORT, heights, features, after)


def first_matrices(channels, rows):
    wide = TAPS * channels
    shapes = [(TAPS * rows, 3 * wide), (TAPS * rows, 2 * wide), (TAPS * rows, 2 * wide), (rows, 128)]
    return shapes, [BF16, BF16, BF16, F32]


def fill(heights, weights, bias, after):
    quarter, channels = weights.shape[1], weights.shape[2]
    tall = TAPS * 2 * quarter
    outputs = [(tall, 12 * channels), (tall, 9 * channels), (tall, 9 * channels), (2 * quarter, 128)]
    kinds = [BF16, BF16, BF16, F32]
    return call(fill_kernel, "fill", [SCALARS, WHOLE, WHOLE, ANY], outputs, [], SHORT, heights, weights, bias[None], after, kinds=kinds)


def first_near(halo, heights, own, part_a, part_b, after):
    _, _, channels, depth = own.shape
    half, width = 2 * part_a.shape[1], COL_Y + 2 * halo
    shapes, kinds = first_matrices(channels, half)
    inner, *matrices = call(
        functools.partial(first_near_kernel, halo), "first_near", [SCALARS] + [WHOLE] * 3 + [ANY],
        [(COL_Y - 2, width, half, depth), *shapes], [], LONG, heights, own, part_a, part_b, after, kinds=[BF16, *kinds],
    )
    return inner, matrices


def first_far(halo, heights, own, mate, part_a, part_b, near, after):
    _, _, channels, depth = own.shape
    half, width = 2 * part_a.shape[1], COL_Y + 2 * halo
    shapes, kinds = first_matrices(channels, half)
    inner, row_seven, *matrices = call(
        functools.partial(first_far_kernel, halo), "first_far", [SCALARS] + [WHOLE] * 8 + [ANY],
        [(COL_Y - 2, width, half, depth), (width, channels, depth), *shapes], [], SHORT,
        heights, own, mate, part_a, part_b, *near, after, kinds=[BF16, BF16, *kinds],
    )
    return inner, row_seven, matrices


def second_inner(halo, heights, inner_a, inner_b, row_seven, matrices):
    rows, _, _, depth = inner_a.shape
    quarter = matrices[-1].shape[0] // 2
    outputs = [(rows - 1, COL_Y, quarter, depth)]
    args = (heights, inner_a, inner_b, row_seven, *matrices)
    kernel = functools.partial(second_inner_kernel, halo)
    return call(kernel, "second_inner", [SCALARS] + [WHOLE] * (len(args) - 1), outputs, [], SHORT, *args)[0]


def last(halo, heights, own, cross, near, far, hidden, done_inner, matrices):
    _, _, channels, depth = own.shape
    quarter, width = matrices[-1].shape[0] // 2, COL_Y + 2 * halo
    scratch = [pltpu.VMEM((2, width, channels, depth), BF16), pltpu.VMEM((3, COL_Y, quarter, depth), BF16)]
    outputs = [(1, quarter, COL_Y, COL_Y, depth)]
    args = (heights, own, cross, *near, *far, *hidden, done_inner, *matrices)
    kernel = functools.partial(last_kernel, halo)
    return call(kernel, "last", [SCALARS] + [WHOLE] * (len(args) - 1), outputs, scratch, SHORT, *args)[0]


def across_pairs(peers):
    pairs = []
    for i in range(peers):
        to = i + 1 if i % 2 else i - 1
        if 0 <= to < peers and to // COL_Y == i // COL_Y:
            pairs.append((i, to))
    return pairs


def to_mate(value):
    return lax.ppermute(value, "space", [(i, i ^ 1) for i in range(lax.axis_size("space"))])


def far_pairs(peers, chans):
    pairs = []
    for i in range(peers):
        for c in range(chans):
            pairs.append((i * chans + c, i * chans + (c ^ (3 if i % 2 else 2))))
    return pairs


def with_x_borders(rows, peers):
    forth = [(i, i + COL_Y) for i in range(peers - COL_Y)]
    back = [(i + COL_Y, i) for i in range(peers - COL_Y)]
    before = lax.ppermute(rows[:, COL_Y - 2 :], "space", forth)
    behind = lax.ppermute(rows[:, :2], "space", back)
    return jnp.concatenate([before, rows, behind], axis=1)


def on_device(features, column_heights, weight_one, bias_one, weight_two, bias_two):
    peers, chans = lax.axis_size("space"), lax.axis_size("chan")
    halo = 1 if peers > COL_Y else 0

    own_part = pack(weight_one, bias_one)
    near_part = lax.ppermute(own_part, "chan", [(c, c ^ 1) for c in range(chans)])
    far_part = lax.ppermute(own_part, ("space", "chan"), far_pairs(peers, chans))
    fields, cross, mate = arrange(column_heights, features, own_part)
    cross = lax.ppermute(cross, "space", across_pairs(peers))
    mate = to_mate(mate)
    if halo:
        fields = with_x_borders(jnp.concatenate([cross, fields, mate[None]], axis=0), peers)
        cross, fields, mate = fields[:2], fields[2:-1], fields[-1]

    matrices = fill(column_heights, weight_two, bias_two, own_part)
    inner_a, near = first_near(halo, column_heights, fields, own_part, near_part, matrices[-1])
    far_part, inner_a = lax.optimization_barrier((far_part, inner_a))
    other_part = to_mate(far_part)
    inner_b, row_seven, far = first_far(halo, column_heights, fields, mate, far_part, other_part, near, inner_a)
    mate = to_mate(row_seven)
    done_inner = second_inner(halo, column_heights, inner_a, inner_b, row_seven, matrices)
    hidden = (inner_a, inner_b, row_seven, mate)
    return last(halo, column_heights, fields, cross, near, far, hidden, done_inner, matrices)


def solution(mesh):
    placed = (
        P("space", None, None, None, None),
        P(),
        P(None, "chan", None),
        P("chan"),
        P(None, "chan", None),
        P("chan"),
    )
    return jax.shard_map(
        on_device,
        mesh=mesh,
        in_specs=placed,
        out_specs=P("space", "chan", None, None, None),
        check_vma=False,
    )
```

```python
import functools

import jax
import jax.numpy as jnp
from jax import lax
from jax.experimental import pallas as pl
from jax.experimental.pallas import tpu as pltpu
from jax.sharding import PartitionSpec as P

COL_Y = 8
TAPS = 3
BF16 = jnp.bfloat16
F32 = jnp.float32
ANY = pl.BlockSpec(memory_space=pl.ANY)
WHOLE = pl.BlockSpec(memory_space=pltpu.VMEM)
SCALARS = pl.BlockSpec(memory_space=pltpu.SMEM)


class Place:
    def __init__(self, heights):
        self.heights = heights
        self.column = lax.axis_index("space")
        self.peers = lax.axis_size("space")
        self.odd = lax.rem(self.column, 2)
        chan = lax.axis_index("chan")
        self.half = lax.div(chan, 2)
        near = lax.rem(chan, 2)
        far = jnp.where(self.odd == 1, 1 - near, near)
        self.slots = (near, 1 - near, far, 1 - far)

    def top(self, by_x=0, across=False):
        column, inside = self.column, True
        if across:
            y = lax.rem(column, COL_Y)
            step = jnp.where(self.odd == 1, 1, -1)
            inside = (y + step >= 0) & (y + step < COL_Y)
            column = column + step
        if by_x:
            column = column + by_x * COL_Y
            inside = inside & (column >= 0) & (column < self.peers)
        column = jnp.clip(column, 0, self.peers - 1)
        return jnp.where(inside, self.heights[column] * 8, 0)


def as_column(row):
    size = row.shape[1]
    wide = jnp.broadcast_to(row, (size, size))
    same = lax.broadcasted_iota(jnp.int32, (size, size), 0) == lax.broadcasted_iota(jnp.int32, (size, size), 1)
    return jnp.sum(jnp.where(same, wide, 0.0), axis=1, keepdims=True)


def order_kernel(swap):
    odd = lax.rem(lax.axis_index("space"), 2)
    group = swap.shape[0] // COL_Y
    row = lax.broadcasted_iota(jnp.int32, swap.shape, 0)
    column = lax.broadcasted_iota(jnp.int32, swap.shape, 1)
    u = lax.div(row, group)
    y = jnp.where(odd == 1, COL_Y - 1 - u, u)
    swap[...] = (column == lax.rem(row, group) * COL_Y + y).astype(F32).astype(BF16)


def arrange_kernel(heights, features, swap, fields, cross, mate):
    _, channels, width, _, depth = features.shape
    place = Place(heights)
    group = 256 // COL_Y
    live = lax.broadcasted_iota(jnp.int32, (1, depth), 1) < place.top()
    for x in range(width):
        for first in range(0, channels, group):
            tile = features[0, first : first + group, x].reshape(256, depth)
            moved = jnp.dot(swap[...], tile, preferred_element_type=F32)
            moved = jnp.where(live, moved, 0.0).astype(BF16).reshape(COL_Y, group, depth)
            fields[:, x, first : first + group] = moved
            cross[:, x, first : first + group] = moved[:2]
            mate[x, first : first + group] = moved[COL_Y - 1]


def finish(partial, bias, live_top, columns=1):
    rows, lanes = partial.shape[0] // TAPS, partial.shape[1]
    depth = lanes // columns
    z = lax.broadcasted_iota(jnp.int32, (rows, lanes), 1)
    if columns > 1:
        z = lax.rem(z, depth)
    below = jnp.where(z == 0, 0.0, pltpu.roll(partial[:rows], 1, 1))
    above = jnp.where(z == depth - 1, 0.0, pltpu.roll(partial[2 * rows :], lanes - 1, 1))
    total = jnp.maximum(below + partial[rows : 2 * rows] + above + bias, 0.0)
    return jnp.where(z < live_top, total, 0.0).astype(BF16)


def fill_first(parts, biases, slots, odd, matrix, low_matrix, high_matrix, bias):
    quarter, channels = parts[0].shape[1], parts[0].shape[2]
    block = quarter * len(parts)
    for part, given, slot in zip(parts, biases, slots, strict=True):
        at = slot * quarter
        for k in range(TAPS):
            span = pl.ds(pl.multiple_of(k * block + at, quarter), quarter)
            for j in range(TAPS):
                tap_j = jnp.where(odd == 1, 2 - j, j)
                for i in range(TAPS):
                    tile = part[9 * i + 3 * tap_j + k]
                    matrix[span, pl.ds((j * TAPS + i) * channels, channels)] = tile
                    if i > 0:
                        low_matrix[span, pl.ds((j * 2 + i - 1) * channels, channels)] = tile
                    if i < 2:
                        high_matrix[span, pl.ds((j * 2 + i) * channels, channels)] = tile
        value = as_column(given[...])
        bias[pl.ds(pl.multiple_of(at, quarter), quarter), :] = jnp.broadcast_to(value, (quarter, bias.shape[1]))


def reach(x, width, stored, pad):
    return max(x - 1 + pad, 0), min(x + width + 1 + pad, stored)


def first_row(get, stored, halo, matrices, bias, top):
    for x in range(-halo, COL_Y + halo):
        low, high = reach(x, 1, stored, 2 * halo)
        lhs = matrices[0]
        if high - low == 2:
            lhs = matrices[1] if x == 0 else matrices[2]
        taken = jnp.concatenate([get(j, low, high) for j in range(TAPS)], axis=0)
        partial = jnp.dot(lhs[...], taken, preferred_element_type=F32)
        side = -1 if x < 0 else 1 if x >= COL_Y else 0
        yield x + halo, finish(partial, bias[:, 0:1], top(side))


def first_row_low(get, stored, halo, matrices, bias, top, levels):
    channels = matrices[0].shape[1] // TAPS**2

    def field(j, x):
        return get(j, x, x + 1)[:, :levels] if 0 <= x < stored else jnp.zeros((channels, levels), BF16)

    for x in range(-halo, COL_Y + halo, 2):
        at = x + 2 * halo
        taken = [
            jnp.concatenate([field(j, at + more + i - 1) for j in range(TAPS) for i in range(TAPS)], axis=0) for more in range(2)
        ]
        partial = jnp.dot(matrices[0][...], jnp.concatenate(taken, axis=1), preferred_element_type=F32)
        sides = [-1 if each < 0 else 1 if each >= COL_Y else 0 for each in (x, x + 1)]
        tops = jnp.where(lax.broadcasted_iota(jnp.int32, (1, 2 * levels), 1) < levels, top(sides[0]), top(sides[1]))
        done = finish(partial, bias[:, 0:1], tops, columns=2)
        yield x + halo, done[:, :levels]
        yield x + halo + 1, done[:, levels:]


def span_of(ref, *at):
    *lead, low, high = at
    value = ref[(*lead, slice(low, high))]
    return value.reshape(-1, value.shape[-1])


def inner_rows(own, out, halo, matrices, bias, top):
    def pair(step, _):
        for more in range(2):
            u = step * 2 + more
            for x, done in first_row(lambda j, a, b: span_of(own, u + j, a, b), own.shape[1], halo, matrices, bias, top):
                out[u, x] = done
        return 0

    lax.fori_loop(0, (COL_Y - 2) // 2, pair, 0)


def first_near_kernel(halo, heights, own, part_a, part_b, bias_a, bias_b, bias_c, bias_d, out, matrix, low_matrix, high_matrix, bias):
    place = Place(heights)
    fill_first([part_a, part_b], [bias_a, bias_b], place.slots[:2], place.odd, matrix, low_matrix, high_matrix, bias)
    inner_rows(own, out, halo, (matrix, low_matrix, high_matrix), bias, place.top)


def first_far_kernel(
    halo, heights, own, mate, part_a, part_b, bias_a, bias_b, near, low_near, high_near, bias_near, after,
    out, out_last, matrix, low_matrix, high_matrix, bias,
):
    place = Place(heights)
    fill_first([part_a, part_b], [bias_a, bias_b], place.slots[2:], place.odd, matrix, low_matrix, high_matrix, bias)
    far = (matrix, low_matrix, high_matrix)
    inner_rows(own, out, halo, far, bias, place.top)

    def get(j, a, b):
        return span_of(mate, a, b) if j == 2 else span_of(own, COL_Y - 2 + j, a, b)

    whole_row(get, own.shape[1], halo, ((near, low_near, high_near), bias_near), (far, bias), place.top, out_last)


def whole_row(get, stored, halo, near, far, top, out, *at, levels=None):
    half = near[1].shape[0]
    for first, (matrices, bias) in ((0, near), (half, far)):
        if levels is None:
            for x, done in first_row(get, stored, halo, matrices, bias, top):
                out[(*at, x, slice(first, first + half))] = done
        else:
            for x, done in first_row_low(get, stored, halo, matrices, bias, top, levels):
                out[(*at, x, slice(first, first + half), slice(0, levels))] = done


def fill_second(weights, place, matrix, low_matrix, high_matrix):
    quarter, channels = weights.shape[1], weights.shape[2]
    empty = jnp.zeros((quarter, channels), BF16)
    for k in range(TAPS):
        for to in range(2):
            span = pl.ds((k * 2 + to) * quarter, quarter)
            for j in range(TAPS):
                tap_j = jnp.where(place.odd == 1, 2 - j, j)
                for at in range(4):
                    tile = empty
                    if 0 <= at - to < TAPS:
                        tile = weights[9 * (at - to) + 3 * tap_j + k].astype(F32)
                        tile = jnp.where(place.half == 1, pltpu.roll(tile, channels // 2, 1), tile).astype(BF16)
                    matrix[span, pl.ds((j * 4 + at) * channels, channels)] = tile
                    if at > 0:
                        low_matrix[span, pl.ds((j * 3 + at - 1) * channels, channels)] = tile
                    if at < 3:
                        high_matrix[span, pl.ds((j * 3 + at) * channels, channels)] = tile


def second_row(get, stored, halo, matrices, both, top):
    quarter = both.shape[0] // 2
    for x in range(0, COL_Y, 2):
        low, high = reach(x, 2, stored, halo)
        lhs = matrices[0]
        if high - low == 3:
            lhs = matrices[1] if x == 0 else matrices[2]
        taken = jnp.concatenate([piece for j in range(TAPS) for piece in get(j, low, high)], axis=0)
        partial = jnp.dot(lhs[...], taken, preferred_element_type=F32)
        done = finish(partial, both, top)
        yield x, done[:quarter], done[quarter:]


def halves(ref_a, ref_b, *at):
    *lead, low, high = at
    return [ref[(*lead, x)] for x in range(low, high) for ref in (ref_a, ref_b)]


def fill_bias(bias, both):
    quarter = bias.shape[1]
    column = jnp.broadcast_to(as_column(bias[...]), (quarter, both.shape[1]))
    both[:quarter] = column
    both[quarter:] = column


def fill_kernel(heights, weights, bias, after, matrix, low_matrix, high_matrix, both):
    fill_second(weights, Place(heights), matrix, low_matrix, high_matrix)
    fill_bias(bias, both)


def second_inner_kernel(halo, heights, inner_a, inner_b, row_seven, matrix, low_matrix, high_matrix, both, out):
    place = Place(heights)
    matrices, width, top = (matrix, low_matrix, high_matrix), inner_a.shape[1], place.top()

    def pair(step, _):
        for more in range(2):
            u = step * 2 + more
            for x, here, beside in second_row(lambda j, a, b: halves(inner_a, inner_b, u + j, a, b), width, halo, matrices, both[:, 0:1], top):
                out[u, x] = here
                out[u, x + 1] = beside
        return 0

    lax.fori_loop(0, 2, pair, 0)

    def row(u, a, b):
        return halves(inner_a, inner_b, u - 1, a, b) if u < 7 else [row_seven[x] for x in range(a, b)]

    for x, here, beside in second_row(lambda j, a, b: row(5 + j, a, b), width, halo, matrices, both[:, 0:1], top):
        out[4, x] = here
        out[4, x + 1] = beside


def last_kernel(
    halo, heights, own, cross, near, low_near, high_near, bias_near, far, low_far, high_far, bias_far,
    inner_a, inner_b, row_seven, mate, done_inner, matrix_two, low_two, high_two, both, out, edge, done_edge, result, sems,
):
    place = Place(heights)
    width, depth = own.shape[1], own.shape[3]
    near, far = ((near, low_near, high_near), bias_near), ((far, low_far, high_far), bias_far)

    def fields(u, a, b):
        return span_of(own, u, a, b) if u >= 0 else span_of(cross, -1 - u, a, b)

    def edge_row(u, levels=None):
        def top(side):
            return place.top(side, across=u < 0)

        whole_row(lambda j, a, b: fields(u - 1 + j, a, b), width, halo, near, far, top, edge, u + 1, levels=levels)

    part = 128
    needed = jnp.minimum(place.top(0, across=True), place.top() + 1)
    if halo:
        wide = jnp.maximum(place.top(-1, across=True), place.top(1, across=True))
        needed = jnp.maximum(needed, jnp.minimum(wide, place.top() + 1))
    low = needed < part if depth > part else False

    @pl.when(low)
    def _():
        edge_row(-1, part)
        edge[0, :, :, part:] = jnp.zeros((*edge.shape[1:3], depth - part), BF16)

    @pl.when(jnp.logical_not(low))
    def _():
        edge_row(-1)

    edge_row(0)

    def row(u, a, b):
        if u < 1:
            return [edge[u + 1, x] for x in range(a, b)]
        if u < 7:
            return halves(inner_a, inner_b, u - 1, a, b)
        return [(row_seven if u == 7 else mate)[x] for x in range(a, b)]

    for at, u in enumerate((0, 1, 7)):
        for x, here, beside in second_row(
            lambda j, a, b: row(u - 1 + j, a, b),
            inner_a.shape[1],
            halo,
            (matrix_two, low_two, high_two),
            both[:, 0:1],
            place.top(),
        ):
            done_edge[at, x] = here
            done_edge[at, x + 1] = beside
    quarter = out.shape[1]
    size = quarter * COL_Y
    at_row = lax.broadcasted_iota(jnp.int32, (size, size), 0)
    at_column = lax.broadcasted_iota(jnp.int32, (size, size), 1)
    y = lax.rem(at_row, COL_Y)
    u = jnp.where(place.odd == 1, COL_Y - 1 - y, y)
    swap = (at_column == u * quarter + lax.div(at_row, COL_Y)).astype(F32).astype(BF16)
    for x in range(COL_Y):
        tiles = [done_edge[0, x], done_edge[1, x]] + [done_inner[v, x] for v in range(COL_Y - 3)] + [done_edge[2, x]]
        tile = jnp.concatenate(tiles, axis=0)
        moved = jnp.dot(swap, tile, preferred_element_type=F32).astype(BF16)
        result[x] = moved.reshape(quarter, COL_Y, depth)
        pltpu.make_async_copy(result.at[x], out.at[0, :, x], sems.at[x]).start()
    for x in range(COL_Y):
        pltpu.make_async_copy(result.at[x], out.at[0, :, x], sems.at[x]).wait()


SHORT, LONG = 2**6, 2**27


def call(kernel, name, inputs, outputs, scratch, nbytes, *args, kinds=None, place=WHOLE):
    return pl.pallas_call(
        kernel,
        out_shape=[jax.ShapeDtypeStruct(*each) for each in zip(outputs, kinds or [BF16] * len(outputs))],
        in_specs=inputs,
        out_specs=[place] * len(outputs),
        scratch_shapes=scratch,
        compiler_params=pltpu.CompilerParams(vmem_limit_bytes=16 * 2**20),
        cost_estimate=pl.CostEstimate(flops=64 * nbytes, bytes_accessed=nbytes, transcendentals=0),
        name=name,
    )(*args)


def arrange(heights, features):
    _, channels, width, _, depth = features.shape
    row = (width, channels, depth)
    outputs = [(COL_Y, *row), (2, *row), row]
    swap = call(order_kernel, "order", [], [(256, 256)], [], LONG)[0]
    return call(arrange_kernel, "arrange", [SCALARS, WHOLE, WHOLE], outputs, [], SHORT, heights, features, swap)


def first_matrices(channels, rows):
    wide = TAPS * channels
    shapes = [(TAPS * rows, 3 * wide), (TAPS * rows, 2 * wide), (TAPS * rows, 2 * wide), (rows, 128)]
    return shapes, [BF16, BF16, BF16, F32]


def fill(heights, weights, bias, after):
    quarter, channels = weights.shape[1], weights.shape[2]
    tall = TAPS * 2 * quarter
    outputs = [(tall, 12 * channels), (tall, 9 * channels), (tall, 9 * channels), (2 * quarter, 128)]
    kinds = [BF16, BF16, BF16, F32]
    return call(fill_kernel, "fill", [SCALARS, WHOLE, WHOLE, ANY], outputs, [], SHORT, heights, weights, bias[None], after, kinds=kinds)


def first_near(halo, heights, own, part_a, part_b, biases):
    _, _, channels, depth = own.shape
    half, width = 2 * part_a.shape[1], COL_Y + 2 * halo
    shapes, kinds = first_matrices(channels, half)
    inner, *matrices = call(
        functools.partial(first_near_kernel, halo), "first_near", [SCALARS] + [WHOLE] * 7,
        [(COL_Y - 2, width, half, depth), *shapes], [], LONG, heights, own, part_a, part_b, *biases, kinds=[BF16, *kinds],
    )
    return inner, matrices


def first_far(halo, heights, own, mate, part_a, part_b, bias_a, bias_b, near, after):
    _, _, channels, depth = own.shape
    half, width = 2 * part_a.shape[1], COL_Y + 2 * halo
    shapes, kinds = first_matrices(channels, half)
    inner, row_seven, *matrices = call(
        functools.partial(first_far_kernel, halo), "first_far", [SCALARS] + [WHOLE] * 10 + [ANY],
        [(COL_Y - 2, width, half, depth), (width, channels, depth), *shapes], [], SHORT,
        heights, own, mate, part_a, part_b, bias_a, bias_b, *near, after, kinds=[BF16, BF16, *kinds],
    )
    return inner, row_seven, matrices


def second_inner(halo, heights, inner_a, inner_b, row_seven, matrices):
    rows, _, _, depth = inner_a.shape
    quarter = matrices[-1].shape[0] // 2
    outputs = [(rows - 1, COL_Y, quarter, depth)]
    args = (heights, inner_a, inner_b, row_seven, *matrices)
    kernel = functools.partial(second_inner_kernel, halo)
    return call(kernel, "second_inner", [SCALARS] + [WHOLE] * (len(args) - 1), outputs, [], SHORT, *args)[0]


def last(halo, heights, own, cross, near, far, hidden, done_inner, matrices):
    _, _, channels, depth = own.shape
    quarter, width = matrices[-1].shape[0] // 2, COL_Y + 2 * halo
    scratch = [pltpu.VMEM((2, width, channels, depth), BF16), pltpu.VMEM((3, COL_Y, quarter, depth), BF16)]
    scratch += [pltpu.VMEM((COL_Y, quarter, COL_Y, depth), BF16), pltpu.SemaphoreType.DMA((COL_Y,))]
    outputs = [(1, quarter, COL_Y, COL_Y, depth)]
    args = (heights, own, cross, *near, *far, *hidden, done_inner, *matrices)
    kernel = functools.partial(last_kernel, halo)
    return call(kernel, "last", [SCALARS] + [WHOLE] * (len(args) - 1), outputs, scratch, SHORT, *args, place=ANY)[0]


def across_pairs(peers):
    pairs = []
    for i in range(peers):
        to = i + 1 if i % 2 else i - 1
        if 0 <= to < peers and to // COL_Y == i // COL_Y:
            pairs.append((i, to))
    return pairs


def to_mate(value):
    return lax.ppermute(value, "space", [(i, i ^ 1) for i in range(lax.axis_size("space"))])


def far_pairs(peers, chans, even, odd):
    return [(i * chans + c, i * chans + (c ^ (odd if i % 2 else even))) for i in range(peers) for c in range(chans)]


def with_x_borders(rows, peers):
    forth = [(i, i + COL_Y) for i in range(peers - COL_Y)]
    back = [(i + COL_Y, i) for i in range(peers - COL_Y)]
    before = lax.ppermute(rows[:, COL_Y - 2 :], "space", forth)
    behind = lax.ppermute(rows[:, :2], "space", back)
    return jnp.concatenate([before, rows, behind], axis=1)


def on_device(features, column_heights, weight_one, bias_one, weight_two, bias_two):
    peers, chans = lax.axis_size("space"), lax.axis_size("chan")
    halo = 1 if peers > COL_Y else 0

    near_pairs, distant_pairs = [(c, c ^ 1) for c in range(chans)], far_pairs(peers, chans, 2, 3)
    near_part = lax.ppermute(weight_one, "chan", near_pairs)
    far_part = lax.ppermute(weight_one, ("space", "chan"), distant_pairs)
    own_bias = bias_one[None]
    near_bias = lax.ppermute(own_bias, "chan", near_pairs)
    far_bias = lax.ppermute(own_bias, ("space", "chan"), distant_pairs)
    other_bias = lax.ppermute(own_bias, ("space", "chan"), far_pairs(peers, chans, 3, 2))
    fields, cross, mate = arrange(column_heights, features)
    cross = lax.ppermute(cross, "space", across_pairs(peers))
    mate = to_mate(mate)
    if halo:
        fields = with_x_borders(jnp.concatenate([cross, fields, mate[None]], axis=0), peers)
        cross, fields, mate = fields[:2], fields[2:-1], fields[-1]

    inner_a, near = first_near(halo, column_heights, fields, weight_one, near_part, (own_bias, near_bias, far_bias, other_bias))
    far_part, inner_a = lax.optimization_barrier((far_part, inner_a))
    other_part = to_mate(far_part)
    matrices = fill(column_heights, weight_two, bias_two, inner_a)
    inner_b, row_seven, far = first_far(
        halo, column_heights, fields, mate, far_part, other_part, far_bias, other_bias, near, matrices[-1]
    )
    mate = to_mate(row_seven)
    done_inner = second_inner(halo, column_heights, inner_a, inner_b, row_seven, matrices)
    hidden = (inner_a, inner_b, row_seven, mate)
    return last(halo, column_heights, fields, cross, near, far, hidden, done_inner, matrices)


def solution(mesh):
    placed = (
        P("space", None, None, None, None),
        P(),
        P(None, "chan", None),
        P("chan"),
        P(None, "chan", None),
        P("chan"),
    )
    return jax.shard_map(
        on_device,
        mesh=mesh,
        in_specs=placed,
        out_specs=P("space", "chan", None, None, None),
        check_vma=False,
    )
```

```python
import functools

import jax
import jax.numpy as jnp
from jax import lax
from jax.experimental import pallas as pl
from jax.experimental.pallas import tpu as pltpu
from jax.sharding import PartitionSpec as P

COL_Y = 8
TAPS = 3
BF16 = jnp.bfloat16
F32 = jnp.float32
ANY = pl.BlockSpec(memory_space=pl.ANY)
WHOLE = pl.BlockSpec(memory_space=pltpu.VMEM)
SCALARS = pl.BlockSpec(memory_space=pltpu.SMEM)


class Place:
    def __init__(self, heights):
        self.heights = heights
        self.column = lax.axis_index("space")
        self.peers = lax.axis_size("space")
        self.odd = lax.rem(self.column, 2)
        chan = lax.axis_index("chan")
        self.half = lax.div(chan, 2)
        near = lax.rem(chan, 2)
        far = jnp.where(self.odd == 1, 1 - near, near)
        self.slots = (near, 1 - near, far, 1 - far)

    def top(self, by_x=0, across=False):
        column, inside = self.column, True
        if across:
            y = lax.rem(column, COL_Y)
            step = jnp.where(self.odd == 1, 1, -1)
            inside = (y + step >= 0) & (y + step < COL_Y)
            column = column + step
        if by_x:
            column = column + by_x * COL_Y
            inside = inside & (column >= 0) & (column < self.peers)
        column = jnp.clip(column, 0, self.peers - 1)
        return jnp.where(inside, self.heights[column] * 8, 0)


def as_column(row):
    size = row.shape[1]
    wide = jnp.broadcast_to(row, (size, size))
    same = lax.broadcasted_iota(jnp.int32, (size, size), 0) == lax.broadcasted_iota(jnp.int32, (size, size), 1)
    return jnp.sum(jnp.where(same, wide, 0.0), axis=1, keepdims=True)


def order_kernel(swap):
    odd = lax.rem(lax.axis_index("space"), 2)
    group = swap.shape[0] // COL_Y
    row = lax.broadcasted_iota(jnp.int32, swap.shape, 0)
    column = lax.broadcasted_iota(jnp.int32, swap.shape, 1)
    u = lax.div(row, group)
    y = jnp.where(odd == 1, COL_Y - 1 - u, u)
    swap[...] = (column == lax.rem(row, group) * COL_Y + y).astype(F32).astype(BF16)


def pack_kernel(weights, bias, after, packed):
    taps, rows, lanes = weights.shape
    packed[:taps] = weights[...]
    column = as_column(bias[...])
    lane = lax.broadcasted_iota(jnp.int32, (rows, lanes), 1)
    extra = jnp.zeros((rows, lanes), F32)
    for at in range(3):
        piece = column.astype(BF16).astype(F32)
        extra = jnp.where(lane == at, piece, extra)
        column = column - piece
    packed[taps] = extra.astype(BF16)


def arrange_kernel(heights, features, swap, after, fields, cross, mate):
    _, channels, width, _, depth = features.shape
    place = Place(heights)
    group = 256 // COL_Y
    live = lax.broadcasted_iota(jnp.int32, (1, depth), 1) < place.top()
    for x in range(width):
        for first in range(0, channels, group):
            tile = features[0, first : first + group, x].reshape(256, depth)
            moved = jnp.dot(swap[...], tile, preferred_element_type=F32)
            moved = jnp.where(live, moved, 0.0).astype(BF16).reshape(COL_Y, group, depth)
            fields[:, x, first : first + group] = moved
            cross[:, x, first : first + group] = moved[:2]
            mate[x, first : first + group] = moved[COL_Y - 1]


def finish(partial, bias, live_top, columns=1):
    rows, lanes = partial.shape[0] // TAPS, partial.shape[1]
    depth = lanes // columns
    z = lax.broadcasted_iota(jnp.int32, (rows, lanes), 1)
    if columns > 1:
        z = lax.rem(z, depth)
    below = jnp.where(z == 0, 0.0, pltpu.roll(partial[:rows], 1, 1))
    above = jnp.where(z == depth - 1, 0.0, pltpu.roll(partial[2 * rows :], lanes - 1, 1))
    total = jnp.maximum(below + partial[rows : 2 * rows] + above + bias, 0.0)
    return jnp.where(z < live_top, total, 0.0).astype(BF16)


def fill_first(parts, slots, odd, matrix, low_matrix, high_matrix, bias):
    quarter, channels = parts[0].shape[1], parts[0].shape[2]
    block = quarter * len(parts)
    for part, slot in zip(parts, slots, strict=True):
        at = slot * quarter
        for k in range(TAPS):
            span = pl.ds(pl.multiple_of(k * block + at, quarter), quarter)
            for j in range(TAPS):
                tap_j = jnp.where(odd == 1, 2 - j, j)
                for i in range(TAPS):
                    tile = part[9 * i + 3 * tap_j + k]
                    matrix[span, pl.ds((j * TAPS + i) * channels, channels)] = tile
                    if i > 0:
                        low_matrix[span, pl.ds((j * 2 + i - 1) * channels, channels)] = tile
                    if i < 2:
                        high_matrix[span, pl.ds((j * 2 + i) * channels, channels)] = tile
        extra = part[27].astype(F32)
        value = extra[:, 0:1] + extra[:, 1:2] + extra[:, 2:3]
        bias[pl.ds(pl.multiple_of(at, quarter), quarter), :] = jnp.broadcast_to(value, (quarter, bias.shape[1]))


def reach(x, width, stored, pad):
    return max(x - 1 + pad, 0), min(x + width + 1 + pad, stored)


def first_row(get, stored, halo, matrices, bias, top):
    for x in range(-halo, COL_Y + halo):
        low, high = reach(x, 1, stored, 2 * halo)
        lhs = matrices[0]
        if high - low == 2:
            lhs = matrices[1] if x == 0 else matrices[2]
        taken = jnp.concatenate([get(j, low, high) for j in range(TAPS)], axis=0)
        partial = jnp.dot(lhs[...], taken, preferred_element_type=F32)
        side = -1 if x < 0 else 1 if x >= COL_Y else 0
        yield x + halo, finish(partial, bias[:, 0:1], top(side))


def first_row_low(get, stored, halo, matrices, bias, top, levels):
    channels = matrices[0].shape[1] // TAPS**2

    def field(j, x):
        return get(j, x, x + 1)[:, :levels] if 0 <= x < stored else jnp.zeros((channels, levels), BF16)

    for x in range(-halo, COL_Y + halo, 2):
        at = x + 2 * halo
        taken = [
            jnp.concatenate([field(j, at + more + i - 1) for j in range(TAPS) for i in range(TAPS)], axis=0) for more in range(2)
        ]
        partial = jnp.dot(matrices[0][...], jnp.concatenate(taken, axis=1), preferred_element_type=F32)
        sides = [-1 if each < 0 else 1 if each >= COL_Y else 0 for each in (x, x + 1)]
        tops = jnp.where(lax.broadcasted_iota(jnp.int32, (1, 2 * levels), 1) < levels, top(sides[0]), top(sides[1]))
        done = finish(partial, bias[:, 0:1], tops, columns=2)
        yield x + halo, done[:, :levels]
        yield x + halo + 1, done[:, levels:]


def span_of(ref, *at):
    *lead, low, high = at
    value = ref[(*lead, slice(low, high))]
    return value.reshape(-1, value.shape[-1])


def inner_rows(own, out, halo, matrices, bias, top):
    def pair(step, _):
        for more in range(2):
            u = step * 2 + more
            for x, done in first_row(lambda j, a, b: span_of(own, u + j, a, b), own.shape[1], halo, matrices, bias, top):
                out[u, x] = done
        return 0

    lax.fori_loop(0, (COL_Y - 2) // 2, pair, 0)


def first_near_kernel(halo, heights, own, part_a, part_b, out, matrix, low_matrix, high_matrix, bias):
    place = Place(heights)
    fill_first([part_a, part_b], place.slots[:2], place.odd, matrix, low_matrix, high_matrix, bias)
    inner_rows(own, out, halo, (matrix, low_matrix, high_matrix), bias, place.top)


def first_far_kernel(
    halo, heights, own, mate, part_a, part_b, near, low_near, high_near, bias_near, after,
    out, out_last, matrix, low_matrix, high_matrix, bias,
):
    place = Place(heights)
    fill_first([part_a, part_b], place.slots[2:], place.odd, matrix, low_matrix, high_matrix, bias)
    far = (matrix, low_matrix, high_matrix)
    inner_rows(own, out, halo, far, bias, place.top)

    def get(j, a, b):
        return span_of(mate, a, b) if j == 2 else span_of(own, COL_Y - 2 + j, a, b)

    whole_row(get, own.shape[1], halo, ((near, low_near, high_near), bias_near), (far, bias), place.top, out_last)


def whole_row(get, stored, halo, near, far, top, out, *at, levels=None):
    half = near[1].shape[0]
    for first, (matrices, bias) in ((0, near), (half, far)):
        if levels is None:
            for x, done in first_row(get, stored, halo, matrices, bias, top):
                out[(*at, x, slice(first, first + half))] = done
        else:
            for x, done in first_row_low(get, stored, halo, matrices, bias, top, levels):
                out[(*at, x, slice(first, first + half), slice(0, levels))] = done


def fill_second(weights, place, matrix, low_matrix, high_matrix):
    quarter, channels = weights.shape[1], weights.shape[2]
    empty = jnp.zeros((quarter, channels), BF16)
    for k in range(TAPS):
        for to in range(2):
            span = pl.ds((k * 2 + to) * quarter, quarter)
            for j in range(TAPS):
                tap_j = jnp.where(place.odd == 1, 2 - j, j)
                for at in range(4):
                    tile = empty
                    if 0 <= at - to < TAPS:
                        tile = weights[9 * (at - to) + 3 * tap_j + k].astype(F32)
                        tile = jnp.where(place.half == 1, pltpu.roll(tile, channels // 2, 1), tile).astype(BF16)
                    matrix[span, pl.ds((j * 4 + at) * channels, channels)] = tile
                    if at > 0:
                        low_matrix[span, pl.ds((j * 3 + at - 1) * channels, channels)] = tile
                    if at < 3:
                        high_matrix[span, pl.ds((j * 3 + at) * channels, channels)] = tile


def second_row(get, stored, halo, matrices, both, top):
    quarter = both.shape[0] // 2
    for x in range(0, COL_Y, 2):
        low, high = reach(x, 2, stored, halo)
        lhs = matrices[0]
        if high - low == 3:
            lhs = matrices[1] if x == 0 else matrices[2]
        taken = jnp.concatenate([piece for j in range(TAPS) for piece in get(j, low, high)], axis=0)
        partial = jnp.dot(lhs[...], taken, preferred_element_type=F32)
        done = finish(partial, both, top)
        yield x, done[:quarter], done[quarter:]


def halves(ref_a, ref_b, *at):
    *lead, low, high = at
    return [ref[(*lead, x)] for x in range(low, high) for ref in (ref_a, ref_b)]


def fill_bias(bias, both):
    quarter = bias.shape[1]
    column = jnp.broadcast_to(as_column(bias[...]), (quarter, both.shape[1]))
    both[:quarter] = column
    both[quarter:] = column


def fill_kernel(heights, weights, bias, after, matrix, low_matrix, high_matrix, both):
    fill_second(weights, Place(heights), matrix, low_matrix, high_matrix)
    fill_bias(bias, both)


def second_inner_kernel(halo, heights, inner_a, inner_b, row_seven, matrix, low_matrix, high_matrix, both, out):
    place = Place(heights)
    matrices, width, top = (matrix, low_matrix, high_matrix), inner_a.shape[1], place.top()

    def pair(step, _):
        for more in range(2):
            u = step * 2 + more
            for x, here, beside in second_row(lambda j, a, b: halves(inner_a, inner_b, u + j, a, b), width, halo, matrices, both[:, 0:1], top):
                out[u, x] = here
                out[u, x + 1] = beside
        return 0

    lax.fori_loop(0, 2, pair, 0)

    def row(u, a, b):
        return halves(inner_a, inner_b, u - 1, a, b) if u < 7 else [row_seven[x] for x in range(a, b)]

    for x, here, beside in second_row(lambda j, a, b: row(5 + j, a, b), width, halo, matrices, both[:, 0:1], top):
        out[4, x] = here
        out[4, x + 1] = beside


def last_kernel(
    halo, heights, own, cross, near, low_near, high_near, bias_near, far, low_far, high_far, bias_far,
    inner_a, inner_b, row_seven, mate, done_inner, matrix_two, low_two, high_two, both, out, edge, done_edge, result, sems,
):
    place = Place(heights)
    width, depth = own.shape[1], own.shape[3]
    near, far = ((near, low_near, high_near), bias_near), ((far, low_far, high_far), bias_far)

    def fields(u, a, b):
        return span_of(own, u, a, b) if u >= 0 else span_of(cross, -1 - u, a, b)

    def edge_row(u, levels=None):
        def top(side):
            return place.top(side, across=u < 0)

        whole_row(lambda j, a, b: fields(u - 1 + j, a, b), width, halo, near, far, top, edge, u + 1, levels=levels)

    part = 128
    needed = jnp.minimum(place.top(0, across=True), place.top() + 1)
    if halo:
        wide = jnp.maximum(place.top(-1, across=True), place.top(1, across=True))
        needed = jnp.maximum(needed, jnp.minimum(wide, place.top() + 1))
    low = needed < part if depth > part else False

    @pl.when(low)
    def _():
        edge_row(-1, part)
        edge[0, :, :, part:] = jnp.zeros((*edge.shape[1:3], depth - part), BF16)

    @pl.when(jnp.logical_not(low))
    def _():
        edge_row(-1)

    edge_row(0)

    def row(u, a, b):
        if u < 1:
            return [edge[u + 1, x] for x in range(a, b)]
        if u < 7:
            return halves(inner_a, inner_b, u - 1, a, b)
        return [(row_seven if u == 7 else mate)[x] for x in range(a, b)]

    for at, u in enumerate((0, 1, 7)):
        for x, here, beside in second_row(
            lambda j, a, b: row(u - 1 + j, a, b),
            inner_a.shape[1],
            halo,
            (matrix_two, low_two, high_two),
            both[:, 0:1],
            place.top(),
        ):
            done_edge[at, x] = here
            done_edge[at, x + 1] = beside
    quarter = out.shape[1]
    size = quarter * COL_Y
    at_row = lax.broadcasted_iota(jnp.int32, (size, size), 0)
    at_column = lax.broadcasted_iota(jnp.int32, (size, size), 1)
    y = lax.rem(at_row, COL_Y)
    u = jnp.where(place.odd == 1, COL_Y - 1 - y, y)
    swap = (at_column == u * quarter + lax.div(at_row, COL_Y)).astype(F32).astype(BF16)
    for x in range(COL_Y):
        tiles = [done_edge[0, x], done_edge[1, x]] + [done_inner[v, x] for v in range(COL_Y - 3)] + [done_edge[2, x]]
        tile = jnp.concatenate(tiles, axis=0)
        moved = jnp.dot(swap, tile, preferred_element_type=F32).astype(BF16)
        result[x] = moved.reshape(quarter, COL_Y, depth)
        pltpu.make_async_copy(result.at[x], out.at[0, :, x], sems.at[x]).start()
    for x in range(COL_Y):
        pltpu.make_async_copy(result.at[x], out.at[0, :, x], sems.at[x]).wait()


SHORT, LONG = 2**6, 2**27


def call(kernel, name, inputs, outputs, scratch, nbytes, *args, kinds=None, place=WHOLE):
    return pl.pallas_call(
        kernel,
        out_shape=[jax.ShapeDtypeStruct(*each) for each in zip(outputs, kinds or [BF16] * len(outputs))],
        in_specs=inputs,
        out_specs=[place] * len(outputs),
        scratch_shapes=scratch,
        compiler_params=pltpu.CompilerParams(vmem_limit_bytes=16 * 2**20),
        cost_estimate=pl.CostEstimate(flops=64 * nbytes, bytes_accessed=nbytes, transcendentals=0),
        name=name,
    )(*args)


def order():
    return call(order_kernel, "order", [], [(256, 256)], [], LONG)[0]


def pack(weights, bias, after):
    taps, rows, lanes = weights.shape
    outputs = [(taps + 1, rows, lanes)]
    return call(pack_kernel, "pack", [WHOLE, WHOLE, ANY], outputs, [], LONG, weights, bias[None], after)[0]


def arrange(heights, features, swap, after):
    _, channels, width, _, depth = features.shape
    row = (width, channels, depth)
    outputs = [(COL_Y, *row), (2, *row), row]
    return call(arrange_kernel, "arrange", [SCALARS, WHOLE, WHOLE, ANY], outputs, [], SHORT, heights, features, swap, after)


def first_matrices(channels, rows):
    wide = TAPS * channels
    shapes = [(TAPS * rows, 3 * wide), (TAPS * rows, 2 * wide), (TAPS * rows, 2 * wide), (rows, 128)]
    return shapes, [BF16, BF16, BF16, F32]


def fill(heights, weights, bias, after):
    quarter, channels = weights.shape[1], weights.shape[2]
    tall = TAPS * 2 * quarter
    outputs = [(tall, 12 * channels), (tall, 9 * channels), (tall, 9 * channels), (2 * quarter, 128)]
    kinds = [BF16, BF16, BF16, F32]
    return call(fill_kernel, "fill", [SCALARS, WHOLE, WHOLE, ANY], outputs, [], SHORT, heights, weights, bias[None], after, kinds=kinds)


def first_near(halo, heights, own, part_a, part_b):
    _, _, channels, depth = own.shape
    half, width = 2 * part_a.shape[1], COL_Y + 2 * halo
    shapes, kinds = first_matrices(channels, half)
    inner, *matrices = call(
        functools.partial(first_near_kernel, halo), "first_near", [SCALARS] + [WHOLE] * 3,
        [(COL_Y - 2, width, half, depth), *shapes], [], LONG, heights, own, part_a, part_b, kinds=[BF16, *kinds],
    )
    return inner, matrices


def first_far(halo, heights, own, mate, part_a, part_b, near, after):
    _, _, channels, depth = own.shape
    half, width = 2 * part_a.shape[1], COL_Y + 2 * halo
    shapes, kinds = first_matrices(channels, half)
    inner, row_seven, *matrices = call(
        functools.partial(first_far_kernel, halo), "first_far", [SCALARS] + [WHOLE] * 8 + [ANY],
        [(COL_Y - 2, width, half, depth), (width, channels, depth), *shapes], [], SHORT,
        heights, own, mate, part_a, part_b, *near, after, kinds=[BF16, BF16, *kinds],
    )
    return inner, row_seven, matrices


def second_inner(halo, heights, inner_a, inner_b, row_seven, matrices):
    rows, _, _, depth = inner_a.shape
    quarter = matrices[-1].shape[0] // 2
    outputs = [(rows - 1, COL_Y, quarter, depth)]
    args = (heights, inner_a, inner_b, row_seven, *matrices)
    kernel = functools.partial(second_inner_kernel, halo)
    return call(kernel, "second_inner", [SCALARS] + [WHOLE] * (len(args) - 1), outputs, [], SHORT, *args)[0]


def last(halo, heights, own, cross, near, far, hidden, done_inner, matrices):
    _, _, channels, depth = own.shape
    quarter, width = matrices[-1].shape[0] // 2, COL_Y + 2 * halo
    scratch = [pltpu.VMEM((2, width, channels, depth), BF16), pltpu.VMEM((3, COL_Y, quarter, depth), BF16)]
    scratch += [pltpu.VMEM((COL_Y, quarter, COL_Y, depth), BF16), pltpu.SemaphoreType.DMA((COL_Y,))]
    outputs = [(1, quarter, COL_Y, COL_Y, depth)]
    args = (heights, own, cross, *near, *far, *hidden, done_inner, *matrices)
    kernel = functools.partial(last_kernel, halo)
    return call(kernel, "last", [SCALARS] + [WHOLE] * (len(args) - 1), outputs, scratch, SHORT, *args, place=ANY)[0]


def across_pairs(peers):
    pairs = []
    for i in range(peers):
        to = i + 1 if i % 2 else i - 1
        if 0 <= to < peers and to // COL_Y == i // COL_Y:
            pairs.append((i, to))
    return pairs


def to_mate(value):
    return lax.ppermute(value, "space", [(i, i ^ 1) for i in range(lax.axis_size("space"))])


def far_pairs(peers, chans):
    return [(i * chans + c, i * chans + (c ^ (3 if i % 2 else 2))) for i in range(peers) for c in range(chans)]


def with_x_borders(rows, peers):
    forth = [(i, i + COL_Y) for i in range(peers - COL_Y)]
    back = [(i + COL_Y, i) for i in range(peers - COL_Y)]
    before = lax.ppermute(rows[:, COL_Y - 2 :], "space", forth)
    behind = lax.ppermute(rows[:, :2], "space", back)
    return jnp.concatenate([before, rows, behind], axis=1)


def on_device(features, column_heights, weight_one, bias_one, weight_two, bias_two):
    peers, chans = lax.axis_size("space"), lax.axis_size("chan")
    halo = 1 if peers > COL_Y else 0

    swap = order()
    own_part = pack(weight_one, bias_one, swap)
    near_part = lax.ppermute(own_part, "chan", [(c, c ^ 1) for c in range(chans)])
    far_part = lax.ppermute(own_part, ("space", "chan"), far_pairs(peers, chans))
    fields, cross, mate = arrange(column_heights, features, swap, own_part)
    cross = lax.ppermute(cross, "space", across_pairs(peers))
    mate = to_mate(mate)
    if halo:
        fields = with_x_borders(jnp.concatenate([cross, fields, mate[None]], axis=0), peers)
        cross, fields, mate = fields[:2], fields[2:-1], fields[-1]

    inner_a, near = first_near(halo, column_heights, fields, own_part, near_part)
    far_part, inner_a = lax.optimization_barrier((far_part, inner_a))
    other_part = to_mate(far_part)
    matrices = fill(column_heights, weight_two, bias_two, inner_a)
    inner_b, row_seven, far = first_far(halo, column_heights, fields, mate, far_part, other_part, near, matrices[-1])
    mate = to_mate(row_seven)
    done_inner = second_inner(halo, column_heights, inner_a, inner_b, row_seven, matrices)
    hidden = (inner_a, inner_b, row_seven, mate)
    return last(halo, column_heights, fields, cross, near, far, hidden, done_inner, matrices)


def solution(mesh):
    placed = (
        P("space", None, None, None, None),
        P(),
        P(None, "chan", None),
        P("chan"),
        P(None, "chan", None),
        P("chan"),
    )
    return jax.shard_map(
        on_device,
        mesh=mesh,
        in_specs=placed,
        out_specs=P("space", "chan", None, None, None),
        check_vma=False,
    )
```

```python
import functools

import jax
import jax.numpy as jnp
from jax import lax
from jax.experimental import pallas as pl
from jax.experimental.pallas import tpu as pltpu
from jax.sharding import PartitionSpec as P

COL_Y = 8
TAPS = 3
BF16 = jnp.bfloat16
F32 = jnp.float32
ANY = pl.BlockSpec(memory_space=pl.ANY)
WHOLE = pl.BlockSpec(memory_space=pltpu.VMEM)
SCALARS = pl.BlockSpec(memory_space=pltpu.SMEM)


class Place:
    def __init__(self, heights):
        self.heights = heights
        self.column = lax.axis_index("space")
        self.peers = lax.axis_size("space")
        self.odd = lax.rem(self.column, 2)
        chan = lax.axis_index("chan")
        self.half = lax.div(chan, 2)
        near = lax.rem(chan, 2)
        far = jnp.where(self.odd == 1, 1 - near, near)
        self.slots = (near, 1 - near, far, 1 - far)

    def top(self, by_x=0, across=False):
        column, inside = self.column, True
        if across:
            y = lax.rem(column, COL_Y)
            step = jnp.where(self.odd == 1, 1, -1)
            inside = (y + step >= 0) & (y + step < COL_Y)
            column = column + step
        if by_x:
            column = column + by_x * COL_Y
            inside = inside & (column >= 0) & (column < self.peers)
        column = jnp.clip(column, 0, self.peers - 1)
        return jnp.where(inside, self.heights[column] * 8, 0)


def as_column(row):
    size = row.shape[1]
    wide = jnp.broadcast_to(row, (size, size))
    same = lax.broadcasted_iota(jnp.int32, (size, size), 0) == lax.broadcasted_iota(jnp.int32, (size, size), 1)
    return jnp.sum(jnp.where(same, wide, 0.0), axis=1, keepdims=True)


def order_kernel(swap):
    odd = lax.rem(lax.axis_index("space"), 2)
    group = swap.shape[0] // COL_Y
    row = lax.broadcasted_iota(jnp.int32, swap.shape, 0)
    column = lax.broadcasted_iota(jnp.int32, swap.shape, 1)
    u = lax.div(row, group)
    y = jnp.where(odd == 1, COL_Y - 1 - u, u)
    swap[...] = (column == lax.rem(row, group) * COL_Y + y).astype(F32).astype(BF16)


def pack_kernel(weights, bias, after, packed):
    taps, rows, lanes = weights.shape
    packed[:taps] = weights[...]
    column = as_column(bias[...])
    lane = lax.broadcasted_iota(jnp.int32, (rows, lanes), 1)
    extra = jnp.zeros((rows, lanes), F32)
    for at in range(3):
        piece = column.astype(BF16).astype(F32)
        extra = jnp.where(lane == at, piece, extra)
        column = column - piece
    packed[taps] = extra.astype(BF16)


def arrange_kernel(heights, features, swap, after, fields, cross, mate):
    _, channels, width, _, depth = features.shape
    place = Place(heights)
    group = 256 // COL_Y
    live = lax.broadcasted_iota(jnp.int32, (1, depth), 1) < place.top()
    for x in range(width):
        for first in range(0, channels, group):
            tile = features[0, first : first + group, x].reshape(256, depth)
            moved = jnp.dot(swap[...], tile, preferred_element_type=F32)
            moved = jnp.where(live, moved, 0.0).astype(BF16).reshape(COL_Y, group, depth)
            fields[:, x, first : first + group] = moved
            cross[:, x, first : first + group] = moved[:2]
            mate[x, first : first + group] = moved[COL_Y - 1]


def finish(partial, bias, live_top, columns=1):
    rows, lanes = partial.shape[0] // TAPS, partial.shape[1]
    depth = lanes // columns
    z = lax.broadcasted_iota(jnp.int32, (rows, lanes), 1)
    if columns > 1:
        z = lax.rem(z, depth)
    below = jnp.where(z == 0, 0.0, pltpu.roll(partial[:rows], 1, 1))
    above = jnp.where(z == depth - 1, 0.0, pltpu.roll(partial[2 * rows :], lanes - 1, 1))
    total = jnp.maximum(below + partial[rows : 2 * rows] + above + bias, 0.0)
    return jnp.where(z < live_top, total, 0.0).astype(BF16)


def fill_first(parts, slots, odd, matrix, low_matrix, high_matrix, bias):
    quarter, channels = parts[0].shape[1], parts[0].shape[2]
    block = quarter * len(parts)
    for part, slot in zip(parts, slots, strict=True):
        at = slot * quarter
        for k in range(TAPS):
            span = pl.ds(pl.multiple_of(k * block + at, quarter), quarter)
            for j in range(TAPS):
                tap_j = jnp.where(odd == 1, 2 - j, j)
                for i in range(TAPS):
                    tile = part[9 * i + 3 * tap_j + k]
                    matrix[span, pl.ds((j * TAPS + i) * channels, channels)] = tile
                    if i > 0:
                        low_matrix[span, pl.ds((j * 2 + i - 1) * channels, channels)] = tile
                    if i < 2:
                        high_matrix[span, pl.ds((j * 2 + i) * channels, channels)] = tile
        extra = part[27].astype(F32)
        value = extra[:, 0:1] + extra[:, 1:2] + extra[:, 2:3]
        bias[pl.ds(pl.multiple_of(at, quarter), quarter), :] = jnp.broadcast_to(value, (quarter, bias.shape[1]))


def reach(x, width, stored, pad):
    return max(x - 1 + pad, 0), min(x + width + 1 + pad, stored)


def first_row(get, stored, halo, matrices, bias, top):
    for x in range(-halo, COL_Y + halo):
        low, high = reach(x, 1, stored, 2 * halo)
        lhs = matrices[0]
        if high - low == 2:
            lhs = matrices[1] if x == 0 else matrices[2]
        taken = jnp.concatenate([get(j, low, high) for j in range(TAPS)], axis=0)
        partial = jnp.dot(lhs[...], taken, preferred_element_type=F32)
        side = -1 if x < 0 else 1 if x >= COL_Y else 0
        yield x + halo, finish(partial, bias[:, 0:1], top(side))


def first_row_low(get, stored, halo, matrices, bias, top, levels):
    channels = matrices[0].shape[1] // TAPS**2

    def field(j, x):
        return get(j, x, x + 1)[:, :levels] if 0 <= x < stored else jnp.zeros((channels, levels), BF16)

    for x in range(-halo, COL_Y + halo, 2):
        at = x + 2 * halo
        taken = [
            jnp.concatenate([field(j, at + more + i - 1) for j in range(TAPS) for i in range(TAPS)], axis=0) for more in range(2)
        ]
        partial = jnp.dot(matrices[0][...], jnp.concatenate(taken, axis=1), preferred_element_type=F32)
        sides = [-1 if each < 0 else 1 if each >= COL_Y else 0 for each in (x, x + 1)]
        tops = jnp.where(lax.broadcasted_iota(jnp.int32, (1, 2 * levels), 1) < levels, top(sides[0]), top(sides[1]))
        done = finish(partial, bias[:, 0:1], tops, columns=2)
        yield x + halo, done[:, :levels]
        yield x + halo + 1, done[:, levels:]


def span_of(ref, *at):
    *lead, low, high = at
    value = ref[(*lead, slice(low, high))]
    return value.reshape(-1, value.shape[-1])


def inner_rows(own, out, halo, matrices, bias, top):
    def pair(step, _):
        for more in range(2):
            u = step * 2 + more
            for x, done in first_row(lambda j, a, b: span_of(own, u + j, a, b), own.shape[1], halo, matrices, bias, top):
                out[u, x] = done
        return 0

    lax.fori_loop(0, (COL_Y - 2) // 2, pair, 0)


def first_near_kernel(halo, heights, own, part_a, part_b, out, matrix, low_matrix, high_matrix, bias):
    place = Place(heights)
    fill_first([part_a, part_b], place.slots[:2], place.odd, matrix, low_matrix, high_matrix, bias)
    inner_rows(own, out, halo, (matrix, low_matrix, high_matrix), bias, place.top)


def first_far_kernel(
    halo, heights, own, mate, part_a, part_b, near, low_near, high_near, bias_near, after,
    out, out_last, matrix, low_matrix, high_matrix, bias,
):
    place = Place(heights)
    fill_first([part_a, part_b], place.slots[2:], place.odd, matrix, low_matrix, high_matrix, bias)
    far = (matrix, low_matrix, high_matrix)
    inner_rows(own, out, halo, far, bias, place.top)

    def get(j, a, b):
        return span_of(mate, a, b) if j == 2 else span_of(own, COL_Y - 2 + j, a, b)

    whole_row(get, own.shape[1], halo, ((near, low_near, high_near), bias_near), (far, bias), place.top, out_last)


class Joined:
    def __init__(self, near, far):
        self.near, self.far = near, far
        self.shape = (2 * near.shape[0], near.shape[1])

    def __getitem__(self, _):
        rows = self.near.shape[0] // TAPS
        pieces = [ref[k * rows : (k + 1) * rows] for k in range(TAPS) for ref in (self.near, self.far)]
        return jnp.concatenate(pieces, axis=0)


def whole_row(get, stored, halo, near, far, top, out, *at, levels=None):
    matrices = [Joined(*each) for each in zip(near[0], far[0], strict=True)]
    bias = jnp.concatenate([near[1][...], far[1][...]], axis=0)
    if levels is None:
        for x, done in first_row(get, stored, halo, matrices, bias, top):
            out[(*at, x)] = done
    else:
        for x, done in first_row_low(get, stored, halo, matrices, bias, top, levels):
            out[(*at, x, slice(None), slice(0, levels))] = done


def fill_second(weights, place, matrix, low_matrix, high_matrix):
    quarter, channels = weights.shape[1], weights.shape[2]
    empty = jnp.zeros((quarter, channels), BF16)
    for k in range(TAPS):
        for to in range(2):
            span = pl.ds((k * 2 + to) * quarter, quarter)
            for j in range(TAPS):
                tap_j = jnp.where(place.odd == 1, 2 - j, j)
                for at in range(4):
                    tile = empty
                    if 0 <= at - to < TAPS:
                        tile = weights[9 * (at - to) + 3 * tap_j + k].astype(F32)
                        tile = jnp.where(place.half == 1, pltpu.roll(tile, channels // 2, 1), tile).astype(BF16)
                    matrix[span, pl.ds((j * 4 + at) * channels, channels)] = tile
                    if at > 0:
                        low_matrix[span, pl.ds((j * 3 + at - 1) * channels, channels)] = tile
                    if at < 3:
                        high_matrix[span, pl.ds((j * 3 + at) * channels, channels)] = tile


def second_row(get, stored, halo, matrices, both, top):
    quarter = both.shape[0] // 2
    for x in range(0, COL_Y, 2):
        low, high = reach(x, 2, stored, halo)
        lhs = matrices[0]
        if high - low == 3:
            lhs = matrices[1] if x == 0 else matrices[2]
        taken = jnp.concatenate([piece for j in range(TAPS) for piece in get(j, low, high)], axis=0)
        partial = jnp.dot(lhs[...], taken, preferred_element_type=F32)
        done = finish(partial, both, top)
        yield x, done[:quarter], done[quarter:]


def halves(ref_a, ref_b, *at):
    *lead, low, high = at
    return [ref[(*lead, x)] for x in range(low, high) for ref in (ref_a, ref_b)]


def fill_bias(bias, both):
    quarter = bias.shape[1]
    column = jnp.broadcast_to(as_column(bias[...]), (quarter, both.shape[1]))
    both[:quarter] = column
    both[quarter:] = column


def fill_kernel(heights, weights, bias, after, matrix, low_matrix, high_matrix, both):
    fill_second(weights, Place(heights), matrix, low_matrix, high_matrix)
    fill_bias(bias, both)


def second_inner_kernel(halo, heights, inner_a, inner_b, row_seven, matrix, low_matrix, high_matrix, both, out):
    place = Place(heights)
    matrices, width, top = (matrix, low_matrix, high_matrix), inner_a.shape[1], place.top()

    def row(u, a, b):
        return halves(inner_a, inner_b, u - 1, a, b) if u < 7 else [row_seven[x] for x in range(a, b)]

    for u in range(2, 7):
        for x, here, beside in second_row(lambda j, a, b: row(u - 1 + j, a, b), width, halo, matrices, both[:, 0:1], top):
            out[u - 2, x] = here
            out[u - 2, x + 1] = beside


def last_kernel(
    halo, heights, own, cross, near, low_near, high_near, bias_near, far, low_far, high_far, bias_far,
    inner_a, inner_b, row_seven, mate, done_inner, matrix_two, low_two, high_two, both, out, edge, done_edge, result, sems,
):
    place = Place(heights)
    width, depth = own.shape[1], own.shape[3]
    near, far = ((near, low_near, high_near), bias_near), ((far, low_far, high_far), bias_far)

    def fields(u, a, b):
        return span_of(own, u, a, b) if u >= 0 else span_of(cross, -1 - u, a, b)

    def edge_row(u, levels=None):
        def top(side):
            return place.top(side, across=u < 0)

        whole_row(lambda j, a, b: fields(u - 1 + j, a, b), width, halo, near, far, top, edge, u + 1, levels=levels)

    part = 128
    needed = jnp.minimum(place.top(0, across=True), place.top() + 1)
    if halo:
        wide = jnp.maximum(place.top(-1, across=True), place.top(1, across=True))
        needed = jnp.maximum(needed, jnp.minimum(wide, place.top() + 1))
    low = needed < part if depth > part else False

    @pl.when(low)
    def _():
        edge_row(-1, part)
        edge[0, :, :, part:] = jnp.zeros((*edge.shape[1:3], depth - part), BF16)

    @pl.when(jnp.logical_not(low))
    def _():
        edge_row(-1)

    edge_row(0)

    def row(u, a, b):
        if u < 1:
            return [edge[u + 1, x] for x in range(a, b)]
        if u < 7:
            return halves(inner_a, inner_b, u - 1, a, b)
        return [(row_seven if u == 7 else mate)[x] for x in range(a, b)]

    for at, u in enumerate((0, 1, 7)):
        for x, here, beside in second_row(
            lambda j, a, b: row(u - 1 + j, a, b),
            inner_a.shape[1],
            halo,
            (matrix_two, low_two, high_two),
            both[:, 0:1],
            place.top(),
        ):
            done_edge[at, x] = here
            done_edge[at, x + 1] = beside
    quarter = out.shape[1]
    size = quarter * COL_Y
    at_row = lax.broadcasted_iota(jnp.int32, (size, size), 0)
    at_column = lax.broadcasted_iota(jnp.int32, (size, size), 1)
    y = lax.rem(at_row, COL_Y)
    u = jnp.where(place.odd == 1, COL_Y - 1 - y, y)
    swap = (at_column == u * quarter + lax.div(at_row, COL_Y)).astype(F32).astype(BF16)
    for x in range(COL_Y):
        tiles = [done_edge[0, x], done_edge[1, x]] + [done_inner[v, x] for v in range(COL_Y - 3)] + [done_edge[2, x]]
        tile = jnp.concatenate(tiles, axis=0)
        moved = jnp.dot(swap, tile, preferred_element_type=F32).astype(BF16)
        result[x] = moved.reshape(quarter, COL_Y, depth)
        pltpu.make_async_copy(result.at[x], out.at[0, :, x], sems.at[x]).start()
    for x in range(COL_Y):
        pltpu.make_async_copy(result.at[x], out.at[0, :, x], sems.at[x]).wait()


SHORT, LONG = 2**6, 2**27


def call(kernel, name, inputs, outputs, scratch, nbytes, *args, kinds=None, place=WHOLE):
    return pl.pallas_call(
        kernel,
        out_shape=[jax.ShapeDtypeStruct(*each) for each in zip(outputs, kinds or [BF16] * len(outputs))],
        in_specs=inputs,
        out_specs=[place] * len(outputs),
        scratch_shapes=scratch,
        compiler_params=pltpu.CompilerParams(vmem_limit_bytes=16 * 2**20),
        cost_estimate=pl.CostEstimate(flops=64 * nbytes, bytes_accessed=nbytes, transcendentals=0),
        name=name,
    )(*args)


def order():
    return call(order_kernel, "order", [], [(256, 256)], [], LONG)[0]


def pack(weights, bias, after):
    taps, rows, lanes = weights.shape
    outputs = [(taps + 1, rows, lanes)]
    return call(pack_kernel, "pack", [WHOLE, WHOLE, ANY], outputs, [], LONG, weights, bias[None], after)[0]


def arrange(heights, features, swap, after):
    _, channels, width, _, depth = features.shape
    row = (width, channels, depth)
    outputs = [(COL_Y, *row), (2, *row), row]
    return call(arrange_kernel, "arrange", [SCALARS, WHOLE, WHOLE, ANY], outputs, [], SHORT, heights, features, swap, after)


def first_matrices(channels, rows):
    wide = TAPS * channels
    shapes = [(TAPS * rows, 3 * wide), (TAPS * rows, 2 * wide), (TAPS * rows, 2 * wide), (rows, 128)]
    return shapes, [BF16, BF16, BF16, F32]


def fill(heights, weights, bias, after):
    quarter, channels = weights.shape[1], weights.shape[2]
    tall = TAPS * 2 * quarter
    outputs = [(tall, 12 * channels), (tall, 9 * channels), (tall, 9 * channels), (2 * quarter, 128)]
    kinds = [BF16, BF16, BF16, F32]
    return call(fill_kernel, "fill", [SCALARS, WHOLE, WHOLE, ANY], outputs, [], SHORT, heights, weights, bias[None], after, kinds=kinds)


def first_near(halo, heights, own, part_a, part_b):
    _, _, channels, depth = own.shape
    half, width = 2 * part_a.shape[1], COL_Y + 2 * halo
    shapes, kinds = first_matrices(channels, half)
    inner, *matrices = call(
        functools.partial(first_near_kernel, halo), "first_near", [SCALARS] + [WHOLE] * 3,
        [(COL_Y - 2, width, half, depth), *shapes], [], LONG, heights, own, part_a, part_b, kinds=[BF16, *kinds],
    )
    return inner, matrices


def first_far(halo, heights, own, mate, part_a, part_b, near, after):
    _, _, channels, depth = own.shape
    half, width = 2 * part_a.shape[1], COL_Y + 2 * halo
    shapes, kinds = first_matrices(channels, half)
    inner, row_seven, *matrices = call(
        functools.partial(first_far_kernel, halo), "first_far", [SCALARS] + [WHOLE] * 8 + [ANY],
        [(COL_Y - 2, width, half, depth), (width, channels, depth), *shapes], [], SHORT,
        heights, own, mate, part_a, part_b, *near, after, kinds=[BF16, BF16, *kinds],
    )
    return inner, row_seven, matrices


def second_inner(halo, heights, inner_a, inner_b, row_seven, matrices):
    rows, _, _, depth = inner_a.shape
    quarter = matrices[-1].shape[0] // 2
    outputs = [(rows - 1, COL_Y, quarter, depth)]
    args = (heights, inner_a, inner_b, row_seven, *matrices)
    kernel = functools.partial(second_inner_kernel, halo)
    return call(kernel, "second_inner", [SCALARS] + [WHOLE] * (len(args) - 1), outputs, [], SHORT, *args)[0]


def last(halo, heights, own, cross, near, far, hidden, done_inner, matrices):
    _, _, channels, depth = own.shape
    quarter, width = matrices[-1].shape[0] // 2, COL_Y + 2 * halo
    scratch = [pltpu.VMEM((2, width, channels, depth), BF16), pltpu.VMEM((3, COL_Y, quarter, depth), BF16)]
    scratch += [pltpu.VMEM((COL_Y, quarter, COL_Y, depth), BF16), pltpu.SemaphoreType.DMA((COL_Y,))]
    outputs = [(1, quarter, COL_Y, COL_Y, depth)]
    args = (heights, own, cross, *near, *far, *hidden, done_inner, *matrices)
    kernel = functools.partial(last_kernel, halo)
    return call(kernel, "last", [SCALARS] + [WHOLE] * (len(args) - 1), outputs, scratch, SHORT, *args, place=ANY)[0]


def across_pairs(peers):
    pairs = []
    for i in range(peers):
        to = i + 1 if i % 2 else i - 1
        if 0 <= to < peers and to // COL_Y == i // COL_Y:
            pairs.append((i, to))
    return pairs


def to_mate(value):
    return lax.ppermute(value, "space", [(i, i ^ 1) for i in range(lax.axis_size("space"))])


def far_pairs(peers, chans):
    return [(i * chans + c, i * chans + (c ^ (3 if i % 2 else 2))) for i in range(peers) for c in range(chans)]


def with_x_borders(rows, peers):
    forth = [(i, i + COL_Y) for i in range(peers - COL_Y)]
    back = [(i + COL_Y, i) for i in range(peers - COL_Y)]
    before = lax.ppermute(rows[:, COL_Y - 2 :], "space", forth)
    behind = lax.ppermute(rows[:, :2], "space", back)
    return jnp.concatenate([before, rows, behind], axis=1)


def on_device(features, column_heights, weight_one, bias_one, weight_two, bias_two):
    peers, chans = lax.axis_size("space"), lax.axis_size("chan")
    halo = 1 if peers > COL_Y else 0

    swap = order()
    own_part = pack(weight_one, bias_one, swap)
    near_part = lax.ppermute(own_part, "chan", [(c, c ^ 1) for c in range(chans)])
    fields, cross, mate = arrange(column_heights, features, swap, own_part)
    sent_part, cross = lax.optimization_barrier((own_part, cross))
    far_part = lax.ppermute(sent_part, ("space", "chan"), far_pairs(peers, chans))
    cross = lax.ppermute(cross, "space", across_pairs(peers))
    near_part, mate = lax.optimization_barrier((near_part, mate))
    mate = to_mate(mate)
    if halo:
        fields = with_x_borders(jnp.concatenate([cross, fields, mate[None]], axis=0), peers)
        cross, fields, mate = fields[:2], fields[2:-1], fields[-1]

    inner_a, near = first_near(halo, column_heights, fields, own_part, near_part)
    far_part, inner_a = lax.optimization_barrier((far_part, inner_a))
    other_part = to_mate(far_part)
    matrices = fill(column_heights, weight_two, bias_two, inner_a)
    inner_b, row_seven, far = first_far(halo, column_heights, fields, mate, far_part, other_part, near, matrices[-1])
    mate = to_mate(row_seven)
    done_inner = second_inner(halo, column_heights, inner_a, inner_b, row_seven, matrices)
    hidden = (inner_a, inner_b, row_seven, mate)
    return last(halo, column_heights, fields, cross, near, far, hidden, done_inner, matrices)


def solution(mesh):
    placed = (
        P("space", None, None, None, None),
        P(),
        P(None, "chan", None),
        P("chan"),
        P(None, "chan", None),
        P("chan"),
    )
    return jax.shard_map(
        on_device,
        mesh=mesh,
        in_specs=placed,
        out_specs=P("space", "chan", None, None, None),
        check_vma=False,
    )
```

```python
import functools

import jax
import jax.numpy as jnp
from jax import lax
from jax.experimental import pallas as pl
from jax.experimental.pallas import tpu as pltpu
from jax.sharding import PartitionSpec as P

COL_Y = 8
TAPS = 3
BF16 = jnp.bfloat16
F32 = jnp.float32
ANY = pl.BlockSpec(memory_space=pl.ANY)
WHOLE = pl.BlockSpec(memory_space=pltpu.VMEM)
SCALARS = pl.BlockSpec(memory_space=pltpu.SMEM)


class Place:
    def __init__(self, heights):
        self.heights = heights
        self.column = lax.axis_index("space")
        self.peers = lax.axis_size("space")
        self.odd = lax.rem(self.column, 2)
        chan = lax.axis_index("chan")
        self.half = lax.div(chan, 2)
        near = lax.rem(chan, 2)
        far = jnp.where(self.odd == 1, 1 - near, near)
        self.slots = (near, 1 - near, far, 1 - far)

    def top(self, by_x=0, across=False):
        column, inside = self.column, True
        if across:
            y = lax.rem(column, COL_Y)
            step = jnp.where(self.odd == 1, 1, -1)
            inside = (y + step >= 0) & (y + step < COL_Y)
            column = column + step
        if by_x:
            column = column + by_x * COL_Y
            inside = inside & (column >= 0) & (column < self.peers)
        column = jnp.clip(column, 0, self.peers - 1)
        return jnp.where(inside, self.heights[column] * 8, 0)


def as_column(row):
    size = row.shape[1]
    wide = jnp.broadcast_to(row, (size, size))
    same = lax.broadcasted_iota(jnp.int32, (size, size), 0) == lax.broadcasted_iota(jnp.int32, (size, size), 1)
    return jnp.sum(jnp.where(same, wide, 0.0), axis=1, keepdims=True)


def order_kernel(swap):
    odd = lax.rem(lax.axis_index("space"), 2)
    group = swap.shape[0] // COL_Y
    row = lax.broadcasted_iota(jnp.int32, swap.shape, 0)
    column = lax.broadcasted_iota(jnp.int32, swap.shape, 1)
    u = lax.div(row, group)
    y = jnp.where(odd == 1, COL_Y - 1 - u, u)
    swap[...] = (column == lax.rem(row, group) * COL_Y + y).astype(F32).astype(BF16)


def pack_kernel(weights, bias, after, packed):
    taps, rows, lanes = weights.shape
    packed[:taps] = weights[...]
    column = as_column(bias[...])
    lane = lax.broadcasted_iota(jnp.int32, (rows, lanes), 1)
    extra = jnp.zeros((rows, lanes), F32)
    for at in range(3):
        piece = column.astype(BF16).astype(F32)
        extra = jnp.where(lane == at, piece, extra)
        column = column - piece
    packed[taps] = extra.astype(BF16)


def arrange_kernel(heights, features, swap, after, fields, cross, mate):
    _, channels, width, _, depth = features.shape
    place = Place(heights)
    group = 256 // COL_Y
    live = lax.broadcasted_iota(jnp.int32, (1, depth), 1) < place.top()
    for x in range(width):
        for first in range(0, channels, group):
            tile = features[0, first : first + group, x].reshape(256, depth)
            moved = jnp.dot(swap[...], tile, preferred_element_type=F32)
            moved = jnp.where(live, moved, 0.0).astype(BF16).reshape(COL_Y, group, depth)
            fields[:, x, first : first + group] = moved
            cross[:, x, first : first + group] = moved[:2]
            mate[x, first : first + group] = moved[COL_Y - 1]


def finish(partial, bias, live_top, columns=1):
    rows, lanes = partial.shape[0] // TAPS, partial.shape[1]
    depth = lanes // columns
    z = lax.broadcasted_iota(jnp.int32, (rows, lanes), 1)
    if columns > 1:
        z = lax.rem(z, depth)
    below = jnp.where(z == 0, 0.0, pltpu.roll(partial[:rows], 1, 1))
    above = jnp.where(z == depth - 1, 0.0, pltpu.roll(partial[2 * rows :], lanes - 1, 1))
    total = jnp.maximum(below + partial[rows : 2 * rows] + above + bias, 0.0)
    return jnp.where(z < live_top, total, 0.0).astype(BF16)


def fill_first(parts, slots, odd, matrix, low_matrix, high_matrix, bias):
    quarter, channels = parts[0].shape[1], parts[0].shape[2]
    block = quarter * len(parts)
    for part, slot in zip(parts, slots, strict=True):
        at = slot * quarter
        for k in range(TAPS):
            span = pl.ds(pl.multiple_of(k * block + at, quarter), quarter)
            for j in range(TAPS):
                tap_j = jnp.where(odd == 1, 2 - j, j)
                for i in range(TAPS):
                    tile = part[9 * i + 3 * tap_j + k]
                    matrix[span, pl.ds((j * TAPS + i) * channels, channels)] = tile
                    if i > 0:
                        low_matrix[span, pl.ds((j * 2 + i - 1) * channels, channels)] = tile
                    if i < 2:
                        high_matrix[span, pl.ds((j * 2 + i) * channels, channels)] = tile
        extra = part[27].astype(F32)
        value = extra[:, 0:1] + extra[:, 1:2] + extra[:, 2:3]
        bias[pl.ds(pl.multiple_of(at, quarter), quarter), :] = jnp.broadcast_to(value, (quarter, bias.shape[1]))


def reach(x, width, stored, pad):
    return max(x - 1 + pad, 0), min(x + width + 1 + pad, stored)


def first_row(get, stored, halo, matrices, bias, top):
    for x in range(-halo, COL_Y + halo):
        low, high = reach(x, 1, stored, 2 * halo)
        lhs = matrices[0]
        if high - low == 2:
            lhs = matrices[1] if x == 0 else matrices[2]
        taken = jnp.concatenate([get(j, low, high) for j in range(TAPS)], axis=0)
        partial = jnp.dot(lhs[...], taken, preferred_element_type=F32)
        side = -1 if x < 0 else 1 if x >= COL_Y else 0
        yield x + halo, finish(partial, bias[:, 0:1], top(side))


def first_row_low(get, stored, halo, matrices, bias, top, levels):
    channels = matrices[0].shape[1] // TAPS**2

    def field(j, x):
        return get(j, x, x + 1)[:, :levels] if 0 <= x < stored else jnp.zeros((channels, levels), BF16)

    for x in range(-halo, COL_Y + halo, 2):
        at = x + 2 * halo
        taken = [
            jnp.concatenate([field(j, at + more + i - 1) for j in range(TAPS) for i in range(TAPS)], axis=0) for more in range(2)
        ]
        partial = jnp.dot(matrices[0][...], jnp.concatenate(taken, axis=1), preferred_element_type=F32)
        sides = [-1 if each < 0 else 1 if each >= COL_Y else 0 for each in (x, x + 1)]
        tops = jnp.where(lax.broadcasted_iota(jnp.int32, (1, 2 * levels), 1) < levels, top(sides[0]), top(sides[1]))
        done = finish(partial, bias[:, 0:1], tops, columns=2)
        yield x + halo, done[:, :levels]
        yield x + halo + 1, done[:, levels:]


def span_of(ref, *at):
    *lead, low, high = at
    value = ref[(*lead, slice(low, high))]
    return value.reshape(-1, value.shape[-1])


def inner_rows(own, out, halo, matrices, bias, top):
    def pair(step, _):
        for more in range(2):
            u = step * 2 + more
            for x, done in first_row(lambda j, a, b: span_of(own, u + j, a, b), own.shape[1], halo, matrices, bias, top):
                out[u, x] = done
        return 0

    lax.fori_loop(0, (COL_Y - 2) // 2, pair, 0)


def first_near_kernel(halo, heights, own, part_a, part_b, out, matrix, low_matrix, high_matrix, bias):
    place = Place(heights)
    fill_first([part_a, part_b], place.slots[:2], place.odd, matrix, low_matrix, high_matrix, bias)
    inner_rows(own, out, halo, (matrix, low_matrix, high_matrix), bias, place.top)


def first_far_kernel(
    halo, heights, own, mate, part_a, part_b, near, low_near, high_near, bias_near, after,
    out, out_last, matrix, low_matrix, high_matrix, bias,
):
    place = Place(heights)
    fill_first([part_a, part_b], place.slots[2:], place.odd, matrix, low_matrix, high_matrix, bias)
    far = (matrix, low_matrix, high_matrix)
    inner_rows(own, out, halo, far, bias, place.top)

    def get(j, a, b):
        return span_of(mate, a, b) if j == 2 else span_of(own, COL_Y - 2 + j, a, b)

    whole_row(get, own.shape[1], halo, ((near, low_near, high_near), bias_near), (far, bias), place.top, out_last)


class Joined:
    def __init__(self, near, far):
        self.near, self.far = near, far
        self.shape = (2 * near.shape[0], near.shape[1])

    def __getitem__(self, _):
        rows = self.near.shape[0] // TAPS
        pieces = [ref[k * rows : (k + 1) * rows] for k in range(TAPS) for ref in (self.near, self.far)]
        return jnp.concatenate(pieces, axis=0)


def whole_row(get, stored, halo, near, far, top, out, *at, levels=None):
    matrices = [Joined(*each) for each in zip(near[0], far[0], strict=True)]
    bias = jnp.concatenate([near[1][...], far[1][...]], axis=0)
    if levels is None:
        for x, done in first_row(get, stored, halo, matrices, bias, top):
            out[(*at, x)] = done
    else:
        for x, done in first_row_low(get, stored, halo, matrices, bias, top, levels):
            out[(*at, x, slice(None), slice(0, levels))] = done


def fill_second(weights, place, matrix, low_matrix, high_matrix):
    quarter, channels = weights.shape[1], weights.shape[2]
    empty = jnp.zeros((quarter, channels), BF16)
    for k in range(TAPS):
        for to in range(2):
            span = pl.ds((k * 2 + to) * quarter, quarter)
            for j in range(TAPS):
                tap_j = jnp.where(place.odd == 1, 2 - j, j)
                for at in range(4):
                    tile = empty
                    if 0 <= at - to < TAPS:
                        tile = weights[9 * (at - to) + 3 * tap_j + k].astype(F32)
                        tile = jnp.where(place.half == 1, pltpu.roll(tile, channels // 2, 1), tile).astype(BF16)
                    matrix[span, pl.ds((j * 4 + at) * channels, channels)] = tile
                    if at > 0:
                        low_matrix[span, pl.ds((j * 3 + at - 1) * channels, channels)] = tile
                    if at < 3:
                        high_matrix[span, pl.ds((j * 3 + at) * channels, channels)] = tile


def second_row(get, stored, halo, matrices, both, top):
    quarter = both.shape[0] // 2
    for x in range(0, COL_Y, 2):
        low, high = reach(x, 2, stored, halo)
        lhs = matrices[0]
        if high - low == 3:
            lhs = matrices[1] if x == 0 else matrices[2]
        taken = jnp.concatenate([piece for j in range(TAPS) for piece in get(j, low, high)], axis=0)
        partial = jnp.dot(lhs[...], taken, preferred_element_type=F32)
        done = finish(partial, both, top)
        yield x, done[:quarter], done[quarter:]


def halves(ref_a, ref_b, *at):
    *lead, low, high = at
    return [ref[(*lead, x)] for x in range(low, high) for ref in (ref_a, ref_b)]


def fill_bias(bias, both):
    quarter = bias.shape[1]
    column = jnp.broadcast_to(as_column(bias[...]), (quarter, both.shape[1]))
    both[:quarter] = column
    both[quarter:] = column


def fill_kernel(heights, weights, bias, after, matrix, low_matrix, high_matrix, both):
    fill_second(weights, Place(heights), matrix, low_matrix, high_matrix)
    fill_bias(bias, both)


def second_inner_kernel(halo, heights, inner_a, inner_b, row_seven, matrix, low_matrix, high_matrix, both, out):
    place = Place(heights)
    matrices, width, top = (matrix, low_matrix, high_matrix), inner_a.shape[1], place.top()

    def row(u, a, b):
        return halves(inner_a, inner_b, u - 1, a, b) if u < 7 else [row_seven[x] for x in range(a, b)]

    for u in range(2, 7):
        for x, here, beside in second_row(lambda j, a, b: row(u - 1 + j, a, b), width, halo, matrices, both[:, 0:1], top):
            out[u - 2, x] = here
            out[u - 2, x + 1] = beside


def last_kernel(
    halo, heights, own, cross, near, low_near, high_near, bias_near, far, low_far, high_far, bias_far,
    inner_a, inner_b, row_seven, mate, done_inner, matrix_two, low_two, high_two, both, out, edge, done_edge, result, sems,
):
    place = Place(heights)
    width, depth = own.shape[1], own.shape[3]
    near, far = ((near, low_near, high_near), bias_near), ((far, low_far, high_far), bias_far)

    def fields(u, a, b):
        return span_of(own, u, a, b) if u >= 0 else span_of(cross, -1 - u, a, b)

    def edge_row(u, levels=None):
        def top(side):
            return place.top(side, across=u < 0)

        whole_row(lambda j, a, b: fields(u - 1 + j, a, b), width, halo, near, far, top, edge, u + 1, levels=levels)

    part = 128
    needed = jnp.minimum(place.top(0, across=True), place.top() + 1)
    if halo:
        wide = jnp.maximum(place.top(-1, across=True), place.top(1, across=True))
        needed = jnp.maximum(needed, jnp.minimum(wide, place.top() + 1))
    low = needed < part if depth > part else False

    @pl.when(low)
    def _():
        edge_row(-1, part)
        edge[0, :, :, part:] = jnp.zeros((*edge.shape[1:3], depth - part), BF16)

    @pl.when(jnp.logical_not(low))
    def _():
        edge_row(-1)

    edge_row(0)

    def row(u, a, b):
        if u < 1:
            return [edge[u + 1, x] for x in range(a, b)]
        if u < 7:
            return halves(inner_a, inner_b, u - 1, a, b)
        return [(row_seven if u == 7 else mate)[x] for x in range(a, b)]

    for at, u in enumerate((0, 1, 7)):
        for x, here, beside in second_row(
            lambda j, a, b: row(u - 1 + j, a, b),
            inner_a.shape[1],
            halo,
            (matrix_two, low_two, high_two),
            both[:, 0:1],
            place.top(),
        ):
            done_edge[at, x] = here
            done_edge[at, x + 1] = beside
    quarter = out.shape[1]
    size = quarter * COL_Y
    at_row = lax.broadcasted_iota(jnp.int32, (size, size), 0)
    at_column = lax.broadcasted_iota(jnp.int32, (size, size), 1)
    y = lax.rem(at_row, COL_Y)
    u = jnp.where(place.odd == 1, COL_Y - 1 - y, y)
    swap = (at_column == u * quarter + lax.div(at_row, COL_Y)).astype(F32).astype(BF16)
    for x in range(COL_Y):
        tiles = [done_edge[0, x], done_edge[1, x]] + [done_inner[v, x] for v in range(COL_Y - 3)] + [done_edge[2, x]]
        tile = jnp.concatenate(tiles, axis=0)
        moved = jnp.dot(swap, tile, preferred_element_type=F32).astype(BF16)
        result[x] = moved.reshape(quarter, COL_Y, depth)
        pltpu.make_async_copy(result.at[x], out.at[0, :, x], sems.at[x]).start()
    for x in range(COL_Y):
        pltpu.make_async_copy(result.at[x], out.at[0, :, x], sems.at[x]).wait()


SHORT, MIDDLE, LONG = 2**6, 2**25, 2**27


def call(kernel, name, inputs, outputs, scratch, nbytes, *args, kinds=None, place=WHOLE):
    return pl.pallas_call(
        kernel,
        out_shape=[jax.ShapeDtypeStruct(*each) for each in zip(outputs, kinds or [BF16] * len(outputs))],
        in_specs=inputs,
        out_specs=[place] * len(outputs),
        scratch_shapes=scratch,
        compiler_params=pltpu.CompilerParams(vmem_limit_bytes=16 * 2**20),
        cost_estimate=pl.CostEstimate(flops=64 * nbytes, bytes_accessed=nbytes, transcendentals=0),
        name=name,
    )(*args)


def order():
    return call(order_kernel, "order", [], [(256, 256)], [], LONG)[0]


def pack(weights, bias, after):
    taps, rows, lanes = weights.shape
    outputs = [(taps + 1, rows, lanes)]
    return call(pack_kernel, "pack", [WHOLE, WHOLE, ANY], outputs, [], LONG, weights, bias[None], after)[0]


def arrange(heights, features, swap, after):
    _, channels, width, _, depth = features.shape
    row = (width, channels, depth)
    outputs = [(COL_Y, *row), (2, *row), row]
    return call(arrange_kernel, "arrange", [SCALARS, WHOLE, WHOLE, ANY], outputs, [], SHORT, heights, features, swap, after)


def first_matrices(channels, rows):
    wide = TAPS * channels
    shapes = [(TAPS * rows, 3 * wide), (TAPS * rows, 2 * wide), (TAPS * rows, 2 * wide), (rows, 128)]
    return shapes, [BF16, BF16, BF16, F32]


def fill(heights, weights, bias, after):
    quarter, channels = weights.shape[1], weights.shape[2]
    tall = TAPS * 2 * quarter
    outputs = [(tall, 12 * channels), (tall, 9 * channels), (tall, 9 * channels), (2 * quarter, 128)]
    kinds = [BF16, BF16, BF16, F32]
    return call(fill_kernel, "fill", [SCALARS, WHOLE, WHOLE, ANY], outputs, [], SHORT, heights, weights, bias[None], after, kinds=kinds)


def first_near(halo, heights, own, part_a, part_b):
    _, _, channels, depth = own.shape
    half, width = 2 * part_a.shape[1], COL_Y + 2 * halo
    shapes, kinds = first_matrices(channels, half)
    inner, *matrices = call(
        functools.partial(first_near_kernel, halo), "first_near", [SCALARS] + [WHOLE] * 3,
        [(COL_Y - 2, width, half, depth), *shapes], [], MIDDLE, heights, own, part_a, part_b, kinds=[BF16, *kinds],
    )
    return inner, matrices


def first_far(halo, heights, own, mate, part_a, part_b, near, after):
    _, _, channels, depth = own.shape
    half, width = 2 * part_a.shape[1], COL_Y + 2 * halo
    shapes, kinds = first_matrices(channels, half)
    inner, row_seven, *matrices = call(
        functools.partial(first_far_kernel, halo), "first_far", [SCALARS] + [WHOLE] * 8 + [ANY],
        [(COL_Y - 2, width, half, depth), (width, channels, depth), *shapes], [], SHORT,
        heights, own, mate, part_a, part_b, *near, after, kinds=[BF16, BF16, *kinds],
    )
    return inner, row_seven, matrices


def second_inner(halo, heights, inner_a, inner_b, row_seven, matrices):
    rows, _, _, depth = inner_a.shape
    quarter = matrices[-1].shape[0] // 2
    outputs = [(rows - 1, COL_Y, quarter, depth)]
    args = (heights, inner_a, inner_b, row_seven, *matrices)
    kernel = functools.partial(second_inner_kernel, halo)
    return call(kernel, "second_inner", [SCALARS] + [WHOLE] * (len(args) - 1), outputs, [], SHORT, *args)[0]


def last(halo, heights, own, cross, near, far, hidden, done_inner, matrices):
    _, _, channels, depth = own.shape
    quarter, width = matrices[-1].shape[0] // 2, COL_Y + 2 * halo
    scratch = [pltpu.VMEM((2, width, channels, depth), BF16), pltpu.VMEM((3, COL_Y, quarter, depth), BF16)]
    scratch += [pltpu.VMEM((COL_Y, quarter, COL_Y, depth), BF16), pltpu.SemaphoreType.DMA((COL_Y,))]
    outputs = [(1, quarter, COL_Y, COL_Y, depth)]
    args = (heights, own, cross, *near, *far, *hidden, done_inner, *matrices)
    kernel = functools.partial(last_kernel, halo)
    return call(kernel, "last", [SCALARS] + [WHOLE] * (len(args) - 1), outputs, scratch, SHORT, *args, place=ANY)[0]


def across_pairs(peers):
    pairs = []
    for i in range(peers):
        to = i + 1 if i % 2 else i - 1
        if 0 <= to < peers and to // COL_Y == i // COL_Y:
            pairs.append((i, to))
    return pairs


def to_mate(value):
    return lax.ppermute(value, "space", [(i, i ^ 1) for i in range(lax.axis_size("space"))])


def far_pairs(peers, chans):
    return [(i * chans + c, i * chans + (c ^ (3 if i % 2 else 2))) for i in range(peers) for c in range(chans)]


def with_x_borders(rows, peers):
    forth = [(i, i + COL_Y) for i in range(peers - COL_Y)]
    back = [(i + COL_Y, i) for i in range(peers - COL_Y)]
    before = lax.ppermute(rows[:, COL_Y - 2 :], "space", forth)
    behind = lax.ppermute(rows[:, :2], "space", back)
    return jnp.concatenate([before, rows, behind], axis=1)


def on_device(features, column_heights, weight_one, bias_one, weight_two, bias_two):
    peers, chans = lax.axis_size("space"), lax.axis_size("chan")
    halo = 1 if peers > COL_Y else 0

    swap = order()
    own_part = pack(weight_one, bias_one, swap)
    near_part = lax.ppermute(own_part, "chan", [(c, c ^ 1) for c in range(chans)])
    fields, cross, mate = arrange(column_heights, features, swap, own_part)
    sent_part, cross = lax.optimization_barrier((own_part, cross))
    far_part = lax.ppermute(sent_part, ("space", "chan"), far_pairs(peers, chans))
    cross = lax.ppermute(cross, "space", across_pairs(peers))
    mate = to_mate(mate)
    if halo:
        fields = with_x_borders(jnp.concatenate([cross, fields, mate[None]], axis=0), peers)
        cross, fields, mate = fields[:2], fields[2:-1], fields[-1]

    inner_a, near = first_near(halo, column_heights, fields, own_part, near_part)
    far_part, inner_a = lax.optimization_barrier((far_part, inner_a))
    other_part = to_mate(far_part)
    matrices = fill(column_heights, weight_two, bias_two, inner_a)
    inner_b, row_seven, far = first_far(halo, column_heights, fields, mate, far_part, other_part, near, matrices[-1])
    mate = to_mate(row_seven)
    done_inner = second_inner(halo, column_heights, inner_a, inner_b, row_seven, matrices)
    hidden = (inner_a, inner_b, row_seven, mate)
    return last(halo, column_heights, fields, cross, near, far, hidden, done_inner, matrices)


def solution(mesh):
    placed = (
        P("space", None, None, None, None),
        P(),
        P(None, "chan", None),
        P("chan"),
        P(None, "chan", None),
        P("chan"),
    )
    return jax.shard_map(
        on_device,
        mesh=mesh,
        in_specs=placed,
        out_specs=P("space", "chan", None, None, None),
        check_vma=False,
    )
```

```python
import functools

import jax
import jax.numpy as jnp
from jax import lax
from jax.experimental import pallas as pl
from jax.experimental.pallas import tpu as pltpu
from jax.sharding import PartitionSpec as P

COL_Y = 8
TAPS = 3
BF16 = jnp.bfloat16
F32 = jnp.float32
ANY = pl.BlockSpec(memory_space=pl.ANY)
WHOLE = pl.BlockSpec(memory_space=pltpu.VMEM)
SCALARS = pl.BlockSpec(memory_space=pltpu.SMEM)


class Place:
    def __init__(self, heights):
        self.heights = heights
        self.column = lax.axis_index("space")
        self.peers = lax.axis_size("space")
        self.odd = lax.rem(self.column, 2)
        chan = lax.axis_index("chan")
        self.half = lax.div(chan, 2)
        near = lax.rem(chan, 2)
        far = jnp.where(self.odd == 1, 1 - near, near)
        self.slots = (near, 1 - near, far, 1 - far)

    def top(self, by_x=0, across=False):
        column, inside = self.column, True
        if across:
            y = lax.rem(column, COL_Y)
            step = jnp.where(self.odd == 1, 1, -1)
            inside = (y + step >= 0) & (y + step < COL_Y)
            column = column + step
        if by_x:
            column = column + by_x * COL_Y
            inside = inside & (column >= 0) & (column < self.peers)
        column = jnp.clip(column, 0, self.peers - 1)
        return jnp.where(inside, self.heights[column] * 8, 0)


def as_column(row):
    size = row.shape[1]
    wide = jnp.broadcast_to(row, (size, size))
    same = lax.broadcasted_iota(jnp.int32, (size, size), 0) == lax.broadcasted_iota(jnp.int32, (size, size), 1)
    return jnp.sum(jnp.where(same, wide, 0.0), axis=1, keepdims=True)


def order_kernel(swap):
    odd = lax.rem(lax.axis_index("space"), 2)
    group = swap.shape[0] // COL_Y
    row = lax.broadcasted_iota(jnp.int32, swap.shape, 0)
    column = lax.broadcasted_iota(jnp.int32, swap.shape, 1)
    u = lax.div(row, group)
    y = jnp.where(odd == 1, COL_Y - 1 - u, u)
    swap[...] = (column == lax.rem(row, group) * COL_Y + y).astype(F32).astype(BF16)


def pack_kernel(weights, bias, after, packed):
    taps, rows, lanes = weights.shape
    packed[:taps] = weights[...]
    column = as_column(bias[...])
    lane = lax.broadcasted_iota(jnp.int32, (rows, lanes), 1)
    extra = jnp.zeros((rows, lanes), F32)
    for at in range(3):
        piece = column.astype(BF16).astype(F32)
        extra = jnp.where(lane == at, piece, extra)
        column = column - piece
    packed[taps] = extra.astype(BF16)


def arrange_kernel(heights, features, swap, after, fields, cross, mate):
    _, channels, width, _, depth = features.shape
    place = Place(heights)
    group = 256 // COL_Y
    live = lax.broadcasted_iota(jnp.int32, (1, depth), 1) < place.top()
    for x in range(width):
        for first in range(0, channels, group):
            tile = features[0, first : first + group, x].reshape(256, depth)
            moved = jnp.dot(swap[...], tile, preferred_element_type=F32)
            moved = jnp.where(live, moved, 0.0).astype(BF16).reshape(COL_Y, group, depth)
            fields[:, x, first : first + group] = moved
            cross[:, x, first : first + group] = moved[:2]
            mate[x, first : first + group] = moved[COL_Y - 1]


def finish(partial, bias, live_top):
    rows, depth = partial.shape[0] // TAPS, partial.shape[1]
    z = lax.broadcasted_iota(jnp.int32, (rows, depth), 1)
    below = jnp.where(z == 0, 0.0, pltpu.roll(partial[:rows], 1, 1))
    above = jnp.where(z == depth - 1, 0.0, pltpu.roll(partial[2 * rows :], depth - 1, 1))
    total = jnp.maximum(below + partial[rows : 2 * rows] + above + bias, 0.0)
    return jnp.where(z < live_top, total, 0.0).astype(BF16)


def fill_first(parts, slots, odd, matrix, low_matrix, high_matrix, bias):
    quarter, channels = parts[0].shape[1], parts[0].shape[2]
    block = quarter * len(parts)
    for part, slot in zip(parts, slots, strict=True):
        at = slot * quarter
        for k in range(TAPS):
            span = pl.ds(pl.multiple_of(k * block + at, quarter), quarter)
            for j in range(TAPS):
                tap_j = jnp.where(odd == 1, 2 - j, j)
                for i in range(TAPS):
                    tile = part[9 * i + 3 * tap_j + k]
                    matrix[span, pl.ds((j * TAPS + i) * channels, channels)] = tile
                    if i > 0:
                        low_matrix[span, pl.ds((j * 2 + i - 1) * channels, channels)] = tile
                    if i < 2:
                        high_matrix[span, pl.ds((j * 2 + i) * channels, channels)] = tile
        extra = part[27].astype(F32)
        value = extra[:, 0:1] + extra[:, 1:2] + extra[:, 2:3]
        bias[pl.ds(pl.multiple_of(at, quarter), quarter), :] = jnp.broadcast_to(value, (quarter, bias.shape[1]))


def reach(x, width, stored, pad):
    return max(x - 1 + pad, 0), min(x + width + 1 + pad, stored)


def first_sums(get, stored, halo, matrices, taps=range(TAPS)):
    for x in range(-halo, COL_Y + halo):
        low, high = reach(x, 1, stored, 2 * halo)
        lhs = matrices[0]
        if high - low == 2:
            lhs = matrices[1] if x == 0 else matrices[2]
        wide = lhs.shape[1] // TAPS
        taken = jnp.concatenate([get(j, low, high) for j in taps], axis=0)
        columns = slice(taps[0] * wide, (taps[-1] + 1) * wide)
        yield x, jnp.dot(lhs[:, columns], taken, preferred_element_type=F32)


def first_row(get, stored, halo, matrices, bias, top):
    for x, partial in first_sums(get, stored, halo, matrices):
        yield x + halo, finish(partial, bias[:, 0:1], top(side_of(x)))


def side_of(x):
    return -1 if x < 0 else 1 if x >= COL_Y else 0


def span_of(ref, *at):
    *lead, low, high = at
    value = ref[(*lead, slice(low, high))]
    return value.reshape(-1, value.shape[-1])


def inner_rows(own, out, halo, matrices, bias, top):
    def pair(step, _):
        for more in range(2):
            u = step * 2 + more
            for x, done in first_row(lambda j, a, b: span_of(own, u + j, a, b), own.shape[1], halo, matrices, bias, top):
                out[u, x] = done
        return 0

    lax.fori_loop(0, (COL_Y - 2) // 2, pair, 0)


def first_near_kernel(halo, heights, own, part_a, part_b, out, matrix, low_matrix, high_matrix, bias):
    place = Place(heights)
    fill_first([part_a, part_b], place.slots[:2], place.odd, matrix, low_matrix, high_matrix, bias)
    inner_rows(own, out, halo, (matrix, low_matrix, high_matrix), bias, place.top)


def first_far_kernel(
    halo, heights, own, mate, part_a, part_b, near, low_near, high_near, bias_near, after,
    out, out_last, matrix, low_matrix, high_matrix, bias,
):
    place = Place(heights)
    fill_first([part_a, part_b], place.slots[2:], place.odd, matrix, low_matrix, high_matrix, bias)
    far = (matrix, low_matrix, high_matrix)
    inner_rows(own, out, halo, far, bias, place.top)

    def get(j, a, b):
        return span_of(mate, a, b) if j == 2 else span_of(own, COL_Y - 2 + j, a, b)

    matrices, biases = join(((near, low_near, high_near), bias_near), (far, bias))
    for x, done in first_row(get, own.shape[1], halo, matrices, biases, place.top):
        out_last[x] = done


class Joined:
    def __init__(self, near, far):
        self.near, self.far = near, far
        self.shape = (2 * near.shape[0], near.shape[1])

    def __getitem__(self, at):
        columns = at[1]
        rows = self.near.shape[0] // TAPS
        pieces = [ref[k * rows : (k + 1) * rows, columns] for k in range(TAPS) for ref in (self.near, self.far)]
        return jnp.concatenate(pieces, axis=0)


def join(near, far):
    return [Joined(*each) for each in zip(near[0], far[0], strict=True)], jnp.concatenate([near[1][...], far[1][...]], axis=0)


def fill_second(weights, place, matrix, low_matrix, high_matrix):
    quarter, channels = weights.shape[1], weights.shape[2]
    empty = jnp.zeros((quarter, channels), BF16)
    for k in range(TAPS):
        for to in range(2):
            span = pl.ds((k * 2 + to) * quarter, quarter)
            for j in range(TAPS):
                tap_j = jnp.where(place.odd == 1, 2 - j, j)
                for at in range(4):
                    tile = empty
                    if 0 <= at - to < TAPS:
                        tile = weights[9 * (at - to) + 3 * tap_j + k].astype(F32)
                        tile = jnp.where(place.half == 1, pltpu.roll(tile, channels // 2, 1), tile).astype(BF16)
                    matrix[span, pl.ds((j * 4 + at) * channels, channels)] = tile
                    if at > 0:
                        low_matrix[span, pl.ds((j * 3 + at - 1) * channels, channels)] = tile
                    if at < 3:
                        high_matrix[span, pl.ds((j * 3 + at) * channels, channels)] = tile


def second_row(get, stored, halo, matrices, both, top):
    quarter = both.shape[0] // 2
    for x in range(0, COL_Y, 2):
        low, high = reach(x, 2, stored, halo)
        lhs = matrices[0]
        if high - low == 3:
            lhs = matrices[1] if x == 0 else matrices[2]
        taken = jnp.concatenate([piece for j in range(TAPS) for piece in get(j, low, high)], axis=0)
        partial = jnp.dot(lhs[...], taken, preferred_element_type=F32)
        done = finish(partial, both, top)
        yield x, done[:quarter], done[quarter:]


def halves(ref_a, ref_b, *at):
    *lead, low, high = at
    return [ref[(*lead, x)] for x in range(low, high) for ref in (ref_a, ref_b)]


def fill_bias(bias, both):
    quarter = bias.shape[1]
    column = jnp.broadcast_to(as_column(bias[...]), (quarter, both.shape[1]))
    both[:quarter] = column
    both[quarter:] = column


def fill_kernel(heights, weights, bias, after, matrix, low_matrix, high_matrix, both):
    fill_second(weights, Place(heights), matrix, low_matrix, high_matrix)
    fill_bias(bias, both)


def second_inner_kernel(halo, heights, inner_a, inner_b, row_seven, matrix, low_matrix, high_matrix, both, out):
    place = Place(heights)
    matrices, width, top = (matrix, low_matrix, high_matrix), inner_a.shape[1], place.top()

    def row(u, a, b):
        return halves(inner_a, inner_b, u - 1, a, b) if u < 7 else [row_seven[x] for x in range(a, b)]

    for u in range(2, 7):
        for x, here, beside in second_row(lambda j, a, b: row(u - 1 + j, a, b), width, halo, matrices, both[:, 0:1], top):
            out[u - 2, x] = here
            out[u - 2, x + 1] = beside


def ahead_kernel(
    halo, heights, own, near, low_near, high_near, bias_near, far, low_far, high_far, bias_far,
    inner_a, inner_b, row_seven, mate, matrix_two, low_two, high_two, both, done_seven, sums_before, sums_zero,
):
    matrices, _ = join(((near, low_near, high_near), bias_near), ((far, low_far, high_far), bias_far))
    width = own.shape[1]
    for x, sums in first_sums(lambda j, a, b: span_of(own, j - 2, a, b), width, halo, matrices, (2,)):
        sums_before[x + halo] = sums
    for x, sums in first_sums(lambda j, a, b: span_of(own, j - 1, a, b), width, halo, matrices, (1, 2)):
        sums_zero[x + halo] = sums

    def get(j, a, b):
        return halves(inner_a, inner_b, 5, a, b) if j == 0 else [(row_seven if j == 1 else mate)[x] for x in range(a, b)]

    two = (matrix_two, low_two, high_two)
    for x, here, beside in second_row(get, inner_a.shape[1], halo, two, both[:, 0:1], Place(heights).top()):
        done_seven[x] = here
        done_seven[x + 1] = beside


def last_kernel(
    halo, heights, cross, near, low_near, high_near, bias_near, far, low_far, high_far, bias_far, sums_before, sums_zero,
    inner_a, inner_b, done_inner, done_seven, matrix_two, low_two, high_two, both, out, edge, done_edge, result, sems,
):
    place = Place(heights)
    width, depth = cross.shape[1], cross.shape[3]
    matrices, biases = join(((near, low_near, high_near), bias_near), ((far, low_far, high_far), bias_far))
    for u, sums_own, taps in ((-1, sums_before, (0, 1)), (0, sums_zero, (0,))):
        for x, sums in first_sums(lambda j, a, b: span_of(cross, -u - j, a, b), width, halo, matrices, taps):
            top = place.top(side_of(x), across=u < 0)
            edge[u + 1, x + halo] = finish(sums + sums_own[x + halo], biases[:, 0:1], top)

    def row(u, a, b):
        return [edge[u + 1, x] for x in range(a, b)] if u < 1 else halves(inner_a, inner_b, u - 1, a, b)

    two = (matrix_two, low_two, high_two)
    for u in (0, 1):
        for x, here, beside in second_row(
            lambda j, a, b: row(u - 1 + j, a, b), inner_a.shape[1], halo, two, both[:, 0:1], place.top()
        ):
            done_edge[u, x] = here
            done_edge[u, x + 1] = beside
    quarter = out.shape[1]
    size = quarter * COL_Y
    at_row = lax.broadcasted_iota(jnp.int32, (size, size), 0)
    at_column = lax.broadcasted_iota(jnp.int32, (size, size), 1)
    y = lax.rem(at_row, COL_Y)
    u = jnp.where(place.odd == 1, COL_Y - 1 - y, y)
    swap = (at_column == u * quarter + lax.div(at_row, COL_Y)).astype(F32).astype(BF16)
    for x in range(COL_Y):
        tiles = [done_edge[0, x], done_edge[1, x]] + [done_inner[v, x] for v in range(COL_Y - 3)] + [done_seven[x]]
        tile = jnp.concatenate(tiles, axis=0)
        moved = jnp.dot(swap, tile, preferred_element_type=F32).astype(BF16)
        result[x] = moved.reshape(quarter, COL_Y, depth)
        pltpu.make_async_copy(result.at[x], out.at[0, :, x], sems.at[x]).start()
    for x in range(COL_Y):
        pltpu.make_async_copy(result.at[x], out.at[0, :, x], sems.at[x]).wait()


SHORT, LONG = 2**6, 2**27


def call(kernel, name, inputs, outputs, scratch, nbytes, *args, kinds=None, place=WHOLE):
    return pl.pallas_call(
        kernel,
        out_shape=[jax.ShapeDtypeStruct(*each) for each in zip(outputs, kinds or [BF16] * len(outputs))],
        in_specs=inputs,
        out_specs=[place] * len(outputs),
        scratch_shapes=scratch,
        compiler_params=pltpu.CompilerParams(vmem_limit_bytes=16 * 2**20),
        cost_estimate=pl.CostEstimate(flops=64 * nbytes, bytes_accessed=nbytes, transcendentals=0),
        name=name,
    )(*args)


def order():
    return call(order_kernel, "order", [], [(256, 256)], [], LONG)[0]


def pack(weights, bias, after):
    taps, rows, lanes = weights.shape
    outputs = [(taps + 1, rows, lanes)]
    return call(pack_kernel, "pack", [WHOLE, WHOLE, ANY], outputs, [], LONG, weights, bias[None], after)[0]


def arrange(heights, features, swap, after):
    _, channels, width, _, depth = features.shape
    row = (width, channels, depth)
    outputs = [(COL_Y, *row), (2, *row), row]
    return call(arrange_kernel, "arrange", [SCALARS, WHOLE, WHOLE, ANY], outputs, [], SHORT, heights, features, swap, after)


def first_matrices(channels, rows):
    wide = TAPS * channels
    shapes = [(TAPS * rows, 3 * wide), (TAPS * rows, 2 * wide), (TAPS * rows, 2 * wide), (rows, 128)]
    return shapes, [BF16, BF16, BF16, F32]


def fill(heights, weights, bias, after):
    quarter, channels = weights.shape[1], weights.shape[2]
    tall = TAPS * 2 * quarter
    outputs = [(tall, 12 * channels), (tall, 9 * channels), (tall, 9 * channels), (2 * quarter, 128)]
    kinds = [BF16, BF16, BF16, F32]
    return call(fill_kernel, "fill", [SCALARS, WHOLE, WHOLE, ANY], outputs, [], SHORT, heights, weights, bias[None], after, kinds=kinds)


def first_near(halo, heights, own, part_a, part_b):
    _, _, channels, depth = own.shape
    half, width = 2 * part_a.shape[1], COL_Y + 2 * halo
    shapes, kinds = first_matrices(channels, half)
    inner, *matrices = call(
        functools.partial(first_near_kernel, halo), "first_near", [SCALARS] + [WHOLE] * 3,
        [(COL_Y - 2, width, half, depth), *shapes], [], LONG, heights, own, part_a, part_b, kinds=[BF16, *kinds],
    )
    return inner, matrices


def first_far(halo, heights, own, mate, part_a, part_b, near, after):
    _, _, channels, depth = own.shape
    half, width = 2 * part_a.shape[1], COL_Y + 2 * halo
    shapes, kinds = first_matrices(channels, half)
    inner, row_seven, *matrices = call(
        functools.partial(first_far_kernel, halo), "first_far", [SCALARS] + [WHOLE] * 8 + [ANY],
        [(COL_Y - 2, width, half, depth), (width, channels, depth), *shapes], [], SHORT,
        heights, own, mate, part_a, part_b, *near, after, kinds=[BF16, BF16, *kinds],
    )
    return inner, row_seven, matrices


def second_inner(halo, heights, inner_a, inner_b, row_seven, matrices):
    rows, _, _, depth = inner_a.shape
    quarter = matrices[-1].shape[0] // 2
    outputs = [(rows - 1, COL_Y, quarter, depth)]
    args = (heights, inner_a, inner_b, row_seven, *matrices)
    kernel = functools.partial(second_inner_kernel, halo)
    return call(kernel, "second_inner", [SCALARS] + [WHOLE] * (len(args) - 1), outputs, [], SHORT, *args)[0]


def ahead(halo, heights, own, near, far, hidden, matrices):
    _, _, channels, depth = own.shape
    quarter, width = matrices[-1].shape[0] // 2, COL_Y + 2 * halo
    sums = (width, TAPS * channels, depth)
    args = (heights, own, *near, *far, *hidden, *matrices)
    kernel = functools.partial(ahead_kernel, halo)
    outputs, kinds = [(COL_Y, quarter, depth), sums, sums], [BF16, F32, F32]
    return call(kernel, "ahead", [SCALARS] + [WHOLE] * (len(args) - 1), outputs, [], SHORT, *args, kinds=kinds)


def last(halo, heights, cross, near, far, sums, inner, done, matrices):
    _, _, channels, depth = cross.shape
    quarter, width = matrices[-1].shape[0] // 2, COL_Y + 2 * halo
    scratch = [pltpu.VMEM((2, width, channels, depth), BF16), pltpu.VMEM((2, COL_Y, quarter, depth), BF16)]
    scratch += [pltpu.VMEM((COL_Y, quarter, COL_Y, depth), BF16), pltpu.SemaphoreType.DMA((COL_Y,))]
    outputs = [(1, quarter, COL_Y, COL_Y, depth)]
    args = (heights, cross, *near, *far, *sums, *inner, *done, *matrices)
    kernel = functools.partial(last_kernel, halo)
    return call(kernel, "last", [SCALARS] + [WHOLE] * (len(args) - 1), outputs, scratch, SHORT, *args, place=ANY)[0]


def across_pairs(peers):
    pairs = []
    for i in range(peers):
        to = i + 1 if i % 2 else i - 1
        if 0 <= to < peers and to // COL_Y == i // COL_Y:
            pairs.append((i, to))
    return pairs


def to_mate(value):
    return lax.ppermute(value, "space", [(i, i ^ 1) for i in range(lax.axis_size("space"))])


def far_pairs(peers, chans):
    return [(i * chans + c, i * chans + (c ^ (3 if i % 2 else 2))) for i in range(peers) for c in range(chans)]


def with_x_borders(rows, peers):
    forth = [(i, i + COL_Y) for i in range(peers - COL_Y)]
    back = [(i + COL_Y, i) for i in range(peers - COL_Y)]
    before = lax.ppermute(rows[:, COL_Y - 2 :], "space", forth)
    behind = lax.ppermute(rows[:, :2], "space", back)
    return jnp.concatenate([before, rows, behind], axis=1)


def on_device(features, column_heights, weight_one, bias_one, weight_two, bias_two):
    peers, chans = lax.axis_size("space"), lax.axis_size("chan")
    halo = 1 if peers > COL_Y else 0

    swap = order()
    own_part = pack(weight_one, bias_one, swap)
    near_part = lax.ppermute(own_part, "chan", [(c, c ^ 1) for c in range(chans)])
    fields, cross, mate = arrange(column_heights, features, swap, own_part)
    far_part = lax.ppermute(own_part, ("space", "chan"), far_pairs(peers, chans))
    cross = lax.ppermute(cross, "space", across_pairs(peers))
    near_part, mate = lax.optimization_barrier((near_part, mate))
    mate = to_mate(mate)
    if halo:
        fields = with_x_borders(jnp.concatenate([cross, fields, mate[None]], axis=0), peers)
        cross, fields, mate = fields[:2], fields[2:-1], fields[-1]

    inner_a, near = first_near(halo, column_heights, fields, own_part, near_part)
    far_part, inner_a = lax.optimization_barrier((far_part, inner_a))
    other_part = to_mate(far_part)
    matrices = fill(column_heights, weight_two, bias_two, inner_a)
    inner_b, row_seven, far = first_far(halo, column_heights, fields, mate, far_part, other_part, near, matrices[-1])
    mate = to_mate(row_seven)
    done_inner = second_inner(halo, column_heights, inner_a, inner_b, row_seven, matrices)
    done_seven, *sums = ahead(halo, column_heights, fields, near, far, (inner_a, inner_b, row_seven, mate), matrices)
    done = (done_inner, done_seven)
    return last(halo, column_heights, cross, near, far, sums, (inner_a, inner_b), done, matrices)


def solution(mesh):
    placed = (
        P("space", None, None, None, None),
        P(),
        P(None, "chan", None),
        P("chan"),
        P(None, "chan", None),
        P("chan"),
    )
    return jax.shard_map(
        on_device,
        mesh=mesh,
        in_specs=placed,
        out_specs=P("space", "chan", None, None, None),
        check_vma=False,
    )
```

```python
import functools

import jax
import jax.numpy as jnp
from jax import lax
from jax.experimental import pallas as pl
from jax.experimental.pallas import tpu as pltpu
from jax.sharding import PartitionSpec as P

COL_Y = 8
TAPS = 3
BF16 = jnp.bfloat16
F32 = jnp.float32
ANY = pl.BlockSpec(memory_space=pl.ANY)
WHOLE = pl.BlockSpec(memory_space=pltpu.VMEM)
SCALARS = pl.BlockSpec(memory_space=pltpu.SMEM)


class Place:
    def __init__(self, heights):
        self.heights = heights
        self.column = lax.axis_index("space")
        self.peers = lax.axis_size("space")
        self.odd = lax.rem(self.column, 2)
        chan = lax.axis_index("chan")
        self.half = lax.div(chan, 2)
        near = lax.rem(chan, 2)
        far = jnp.where(self.odd == 1, 1 - near, near)
        self.slots = (near, 1 - near, far, 1 - far)

    def top(self, by_x=0, across=False):
        column, inside = self.column, True
        if across:
            y = lax.rem(column, COL_Y)
            step = jnp.where(self.odd == 1, 1, -1)
            inside = (y + step >= 0) & (y + step < COL_Y)
            column = column + step
        if by_x:
            column = column + by_x * COL_Y
            inside = inside & (column >= 0) & (column < self.peers)
        column = jnp.clip(column, 0, self.peers - 1)
        return jnp.where(inside, self.heights[column] * 8, 0)


def as_column(row):
    size = row.shape[1]
    wide = jnp.broadcast_to(row, (size, size))
    same = lax.broadcasted_iota(jnp.int32, (size, size), 0) == lax.broadcasted_iota(jnp.int32, (size, size), 1)
    return jnp.sum(jnp.where(same, wide, 0.0), axis=1, keepdims=True)


def order_kernel(swap):
    odd = lax.rem(lax.axis_index("space"), 2)
    group = swap.shape[0] // COL_Y
    row = lax.broadcasted_iota(jnp.int32, swap.shape, 0)
    column = lax.broadcasted_iota(jnp.int32, swap.shape, 1)
    u = lax.div(row, group)
    y = jnp.where(odd == 1, COL_Y - 1 - u, u)
    swap[...] = (column == lax.rem(row, group) * COL_Y + y).astype(F32).astype(BF16)


def pack_kernel(weights, bias, after, packed):
    taps, rows, lanes = weights.shape
    packed[:taps] = weights[...]
    column = as_column(bias[...])
    lane = lax.broadcasted_iota(jnp.int32, (rows, lanes), 1)
    extra = jnp.zeros((rows, lanes), F32)
    for at in range(3):
        piece = column.astype(BF16).astype(F32)
        extra = jnp.where(lane == at, piece, extra)
        column = column - piece
    packed[taps] = extra.astype(BF16)


def arrange_kernel(heights, features, swap, after, fields, cross, mate):
    _, channels, width, _, depth = features.shape
    place = Place(heights)
    group = 256 // COL_Y
    live = lax.broadcasted_iota(jnp.int32, (1, depth), 1) < place.top()
    for x in range(width):
        for first in range(0, channels, group):
            tile = features[0, first : first + group, x].reshape(256, depth)
            moved = jnp.dot(swap[...], tile, preferred_element_type=F32)
            moved = jnp.where(live, moved, 0.0).astype(BF16).reshape(COL_Y, group, depth)
            fields[:, x, first : first + group] = moved
            cross[:, x, first : first + group] = moved[:2]
            mate[x, first : first + group] = moved[COL_Y - 1]


def finish(partial, bias, live_top):
    rows, depth = partial.shape[0] // TAPS, partial.shape[1]
    z = lax.broadcasted_iota(jnp.int32, (rows, depth), 1)
    below = jnp.where(z == 0, 0.0, pltpu.roll(partial[:rows], 1, 1))
    above = jnp.where(z == depth - 1, 0.0, pltpu.roll(partial[2 * rows :], depth - 1, 1))
    total = jnp.maximum(below + partial[rows : 2 * rows] + above + bias, 0.0)
    return jnp.where(z < live_top, total, 0.0).astype(BF16)


def fill_first(parts, slots, odd, matrix, low_matrix, high_matrix, bias):
    quarter, channels = parts[0].shape[1], parts[0].shape[2]
    block = quarter * len(parts)
    for part, slot in zip(parts, slots, strict=True):
        at = slot * quarter
        for k in range(TAPS):
            span = pl.ds(pl.multiple_of(k * block + at, quarter), quarter)
            for j in range(TAPS):
                tap_j = jnp.where(odd == 1, 2 - j, j)
                for i in range(TAPS):
                    tile = part[9 * i + 3 * tap_j + k]
                    matrix[span, pl.ds((j * TAPS + i) * channels, channels)] = tile
                    if i > 0:
                        low_matrix[span, pl.ds((j * 2 + i - 1) * channels, channels)] = tile
                    if i < 2:
                        high_matrix[span, pl.ds((j * 2 + i) * channels, channels)] = tile
        extra = part[27].astype(F32)
        value = extra[:, 0:1] + extra[:, 1:2] + extra[:, 2:3]
        bias[pl.ds(pl.multiple_of(at, quarter), quarter), :] = jnp.broadcast_to(value, (quarter, bias.shape[1]))


def reach(x, width, stored, pad):
    return max(x - 1 + pad, 0), min(x + width + 1 + pad, stored)


def first_sums(get, stored, halo, matrices, taps=range(TAPS)):
    for x in range(-halo, COL_Y + halo):
        low, high = reach(x, 1, stored, 2 * halo)
        lhs = matrices[0]
        if high - low == 2:
            lhs = matrices[1] if x == 0 else matrices[2]
        wide = lhs.shape[1] // TAPS
        taken = jnp.concatenate([get(j, low, high) for j in taps], axis=0)
        columns = slice(taps[0] * wide, (taps[-1] + 1) * wide)
        yield x, jnp.dot(lhs[:, columns], taken, preferred_element_type=F32)


def first_row(get, stored, halo, matrices, bias, top):
    for x, partial in first_sums(get, stored, halo, matrices):
        yield x + halo, finish(partial, bias[:, 0:1], top(side_of(x)))


def side_of(x):
    return -1 if x < 0 else 1 if x >= COL_Y else 0


def span_of(ref, *at):
    *lead, low, high = at
    value = ref[(*lead, slice(low, high))]
    return value.reshape(-1, value.shape[-1])


def inner_rows(own, out, halo, matrices, bias, top):
    def pair(step, _):
        for more in range(2):
            u = step * 2 + more
            for x, done in first_row(lambda j, a, b: span_of(own, u + j, a, b), own.shape[1], halo, matrices, bias, top):
                out[u, x] = done
        return 0

    lax.fori_loop(0, (COL_Y - 2) // 2, pair, 0)


def first_near_kernel(halo, heights, own, part_a, part_b, out, matrix, low_matrix, high_matrix, bias):
    place = Place(heights)
    fill_first([part_a, part_b], place.slots[:2], place.odd, matrix, low_matrix, high_matrix, bias)
    inner_rows(own, out, halo, (matrix, low_matrix, high_matrix), bias, place.top)


def first_far_kernel(
    halo, heights, own, mate, part_a, part_b, near, low_near, high_near, bias_near, after,
    out, out_last, matrix, low_matrix, high_matrix, bias,
):
    place = Place(heights)
    fill_first([part_a, part_b], place.slots[2:], place.odd, matrix, low_matrix, high_matrix, bias)
    far = (matrix, low_matrix, high_matrix)
    inner_rows(own, out, halo, far, bias, place.top)

    def get(j, a, b):
        return span_of(mate, a, b) if j == 2 else span_of(own, COL_Y - 2 + j, a, b)

    matrices, biases = join(((near, low_near, high_near), bias_near), (far, bias))
    for x, done in first_row(get, own.shape[1], halo, matrices, biases, place.top):
        out_last[x] = done


class Joined:
    def __init__(self, near, far):
        self.near, self.far = near, far
        self.shape = (2 * near.shape[0], near.shape[1])

    def __getitem__(self, at):
        columns = at[1]
        rows = self.near.shape[0] // TAPS
        pieces = [ref[k * rows : (k + 1) * rows, columns] for k in range(TAPS) for ref in (self.near, self.far)]
        return jnp.concatenate(pieces, axis=0)


def join(near, far):
    return [Joined(*each) for each in zip(near[0], far[0], strict=True)], jnp.concatenate([near[1][...], far[1][...]], axis=0)


def fill_second(weights, place, matrix, low_matrix, high_matrix):
    quarter, channels = weights.shape[1], weights.shape[2]
    empty = jnp.zeros((quarter, channels), BF16)
    for k in range(TAPS):
        for to in range(2):
            span = pl.ds((k * 2 + to) * quarter, quarter)
            for j in range(TAPS):
                tap_j = jnp.where(place.odd == 1, 2 - j, j)
                for at in range(4):
                    tile = empty
                    if 0 <= at - to < TAPS:
                        tile = weights[9 * (at - to) + 3 * tap_j + k].astype(F32)
                        tile = jnp.where(place.half == 1, pltpu.roll(tile, channels // 2, 1), tile).astype(BF16)
                    matrix[span, pl.ds((j * 4 + at) * channels, channels)] = tile
                    if at > 0:
                        low_matrix[span, pl.ds((j * 3 + at - 1) * channels, channels)] = tile
                    if at < 3:
                        high_matrix[span, pl.ds((j * 3 + at) * channels, channels)] = tile


def second_row(get, stored, halo, matrices, both, top):
    quarter = both.shape[0] // 2
    for x in range(0, COL_Y, 2):
        low, high = reach(x, 2, stored, halo)
        lhs = matrices[0]
        if high - low == 3:
            lhs = matrices[1] if x == 0 else matrices[2]
        taken = jnp.concatenate([piece for j in range(TAPS) for piece in get(j, low, high)], axis=0)
        partial = jnp.dot(lhs[...], taken, preferred_element_type=F32)
        done = finish(partial, both, top)
        yield x, done[:quarter], done[quarter:]


def halves(ref_a, ref_b, *at):
    *lead, low, high = at
    return [ref[(*lead, x)] for x in range(low, high) for ref in (ref_a, ref_b)]


def fill_bias(bias, both):
    quarter = bias.shape[1]
    column = jnp.broadcast_to(as_column(bias[...]), (quarter, both.shape[1]))
    both[:quarter] = column
    both[quarter:] = column


def fill_kernel(heights, weights, bias, after, matrix, low_matrix, high_matrix, both):
    fill_second(weights, Place(heights), matrix, low_matrix, high_matrix)
    fill_bias(bias, both)


def second_inner_kernel(
    halo, heights, own, near, low_near, high_near, bias_near, far, low_far, high_far, bias_far,
    inner_a, inner_b, row_seven, matrix, low_matrix, high_matrix, both, out, sums_before, sums_zero,
):
    top = Place(heights).top()
    two = (matrix, low_matrix, high_matrix)

    def row(u, a, b):
        return halves(inner_a, inner_b, u - 1, a, b) if u < 7 else [row_seven[x] for x in range(a, b)]

    for u in range(2, 7):
        for x, here, beside in second_row(lambda j, a, b: row(u - 1 + j, a, b), inner_a.shape[1], halo, two, both[:, 0:1], top):
            out[u - 2, x] = here
            out[u - 2, x + 1] = beside

    matrices, _ = join(((near, low_near, high_near), bias_near), ((far, low_far, high_far), bias_far))
    width = own.shape[1]
    for x, sums in first_sums(lambda j, a, b: span_of(own, j - 2, a, b), width, halo, matrices, (2,)):
        sums_before[x + halo] = sums
    for x, sums in first_sums(lambda j, a, b: span_of(own, j - 1, a, b), width, halo, matrices, (1, 2)):
        sums_zero[x + halo] = sums


def last_kernel(
    halo, heights, own, cross, near, low_near, high_near, bias_near, far, low_far, high_far, bias_far, sums_before, sums_zero,
    inner_a, inner_b, row_seven, mate, done_inner, matrix_two, low_two, high_two, both, out, edge, done_edge, result, sems,
):
    place = Place(heights)
    width, depth = cross.shape[1], cross.shape[3]
    matrices, biases = join(((near, low_near, high_near), bias_near), ((far, low_far, high_far), bias_far))
    for u, sums_own, taps in ((-1, sums_before, (0, 1)), (0, sums_zero, (0,))):
        for x, sums in first_sums(lambda j, a, b: span_of(cross, -u - j, a, b), width, halo, matrices, taps):
            top = place.top(side_of(x), across=u < 0)
            edge[u + 1, x + halo] = finish(sums + sums_own[x + halo], biases[:, 0:1], top)

    def row(u, a, b):
        if 0 < u < 7:
            return halves(inner_a, inner_b, u - 1, a, b)
        return [edge[u + 1, x] if u < 1 else (row_seven if u == 7 else mate)[x] for x in range(a, b)]

    two = (matrix_two, low_two, high_two)
    for at, u in enumerate((0, 1, 7)):
        for x, here, beside in second_row(
            lambda j, a, b: row(u - 1 + j, a, b), inner_a.shape[1], halo, two, both[:, 0:1], place.top()
        ):
            done_edge[at, x] = here
            done_edge[at, x + 1] = beside
    quarter = out.shape[1]
    size = quarter * COL_Y
    at_row = lax.broadcasted_iota(jnp.int32, (size, size), 0)
    at_column = lax.broadcasted_iota(jnp.int32, (size, size), 1)
    y = lax.rem(at_row, COL_Y)
    u = jnp.where(place.odd == 1, COL_Y - 1 - y, y)
    swap = (at_column == u * quarter + lax.div(at_row, COL_Y)).astype(F32).astype(BF16)
    for x in range(COL_Y):
        tiles = [done_edge[0, x], done_edge[1, x]] + [done_inner[v, x] for v in range(COL_Y - 3)] + [done_edge[2, x]]
        tile = jnp.concatenate(tiles, axis=0)
        moved = jnp.dot(swap, tile, preferred_element_type=F32).astype(BF16)
        result[x] = moved.reshape(quarter, COL_Y, depth)
        pltpu.make_async_copy(result.at[x], out.at[0, :, x], sems.at[x]).start()
    for x in range(COL_Y):
        pltpu.make_async_copy(result.at[x], out.at[0, :, x], sems.at[x]).wait()


SHORT, LONG = 2**6, 2**27


def call(kernel, name, inputs, outputs, scratch, nbytes, *args, kinds=None, place=WHOLE):
    return pl.pallas_call(
        kernel,
        out_shape=[jax.ShapeDtypeStruct(*each) for each in zip(outputs, kinds or [BF16] * len(outputs))],
        in_specs=inputs,
        out_specs=[place] * len(outputs),
        scratch_shapes=scratch,
        compiler_params=pltpu.CompilerParams(vmem_limit_bytes=16 * 2**20),
        cost_estimate=pl.CostEstimate(flops=64 * nbytes, bytes_accessed=nbytes, transcendentals=0),
        name=name,
    )(*args)


def order():
    return call(order_kernel, "order", [], [(256, 256)], [], LONG)[0]


def pack(weights, bias, after):
    taps, rows, lanes = weights.shape
    outputs = [(taps + 1, rows, lanes)]
    return call(pack_kernel, "pack", [WHOLE, WHOLE, ANY], outputs, [], LONG, weights, bias[None], after)[0]


def arrange(heights, features, swap, after):
    _, channels, width, _, depth = features.shape
    row = (width, channels, depth)
    outputs = [(COL_Y, *row), (2, *row), row]
    return call(arrange_kernel, "arrange", [SCALARS, WHOLE, WHOLE, ANY], outputs, [], SHORT, heights, features, swap, after)


def first_matrices(channels, rows):
    wide = TAPS * channels
    shapes = [(TAPS * rows, 3 * wide), (TAPS * rows, 2 * wide), (TAPS * rows, 2 * wide), (rows, 128)]
    return shapes, [BF16, BF16, BF16, F32]


def fill(heights, weights, bias, after):
    quarter, channels = weights.shape[1], weights.shape[2]
    tall = TAPS * 2 * quarter
    outputs = [(tall, 12 * channels), (tall, 9 * channels), (tall, 9 * channels), (2 * quarter, 128)]
    kinds = [BF16, BF16, BF16, F32]
    return call(fill_kernel, "fill", [SCALARS, WHOLE, WHOLE, ANY], outputs, [], SHORT, heights, weights, bias[None], after, kinds=kinds)


def first_near(halo, heights, own, part_a, part_b):
    _, _, channels, depth = own.shape
    half, width = 2 * part_a.shape[1], COL_Y + 2 * halo
    shapes, kinds = first_matrices(channels, half)
    inner, *matrices = call(
        functools.partial(first_near_kernel, halo), "first_near", [SCALARS] + [WHOLE] * 3,
        [(COL_Y - 2, width, half, depth), *shapes], [], LONG, heights, own, part_a, part_b, kinds=[BF16, *kinds],
    )
    return inner, matrices


def first_far(halo, heights, own, mate, part_a, part_b, near, after):
    _, _, channels, depth = own.shape
    half, width = 2 * part_a.shape[1], COL_Y + 2 * halo
    shapes, kinds = first_matrices(channels, half)
    inner, row_seven, *matrices = call(
        functools.partial(first_far_kernel, halo), "first_far", [SCALARS] + [WHOLE] * 8 + [ANY],
        [(COL_Y - 2, width, half, depth), (width, channels, depth), *shapes], [], SHORT,
        heights, own, mate, part_a, part_b, *near, after, kinds=[BF16, BF16, *kinds],
    )
    return inner, row_seven, matrices


def second_inner(halo, heights, own, near, far, inner_a, inner_b, row_seven, matrices):
    rows, _, _, depth = inner_a.shape
    channels, width = own.shape[2], COL_Y + 2 * halo
    quarter = matrices[-1].shape[0] // 2
    sums = (width, TAPS * channels, depth)
    outputs, kinds = [(rows - 1, COL_Y, quarter, depth), sums, sums], [BF16, F32, F32]
    args = (heights, own, *near, *far, inner_a, inner_b, row_seven, *matrices)
    kernel = functools.partial(second_inner_kernel, halo)
    done, *sums = call(kernel, "second_inner", [SCALARS] + [WHOLE] * (len(args) - 1), outputs, [], SHORT, *args, kinds=kinds)
    return done, sums


def last(halo, heights, own, cross, near, far, sums, hidden, done_inner, matrices):
    _, _, channels, depth = cross.shape
    quarter, width = matrices[-1].shape[0] // 2, COL_Y + 2 * halo
    scratch = [pltpu.VMEM((2, width, channels, depth), BF16), pltpu.VMEM((3, COL_Y, quarter, depth), BF16)]
    scratch += [pltpu.VMEM((COL_Y, quarter, COL_Y, depth), BF16), pltpu.SemaphoreType.DMA((COL_Y,))]
    outputs = [(1, quarter, COL_Y, COL_Y, depth)]
    args = (heights, own, cross, *near, *far, *sums, *hidden, done_inner, *matrices)
    kernel = functools.partial(last_kernel, halo)
    return call(kernel, "last", [SCALARS] + [WHOLE] * (len(args) - 1), outputs, scratch, SHORT, *args, place=ANY)[0]


def across_pairs(peers):
    pairs = []
    for i in range(peers):
        to = i + 1 if i % 2 else i - 1
        if 0 <= to < peers and to // COL_Y == i // COL_Y:
            pairs.append((i, to))
    return pairs


def to_mate(value):
    return lax.ppermute(value, "space", [(i, i ^ 1) for i in range(lax.axis_size("space"))])


def far_pairs(peers, chans):
    return [(i * chans + c, i * chans + (c ^ (3 if i % 2 else 2))) for i in range(peers) for c in range(chans)]


def with_x_borders(rows, peers):
    forth = [(i, i + COL_Y) for i in range(peers - COL_Y)]
    back = [(i + COL_Y, i) for i in range(peers - COL_Y)]
    before = lax.ppermute(rows[:, COL_Y - 2 :], "space", forth)
    behind = lax.ppermute(rows[:, :2], "space", back)
    return jnp.concatenate([before, rows, behind], axis=1)


def on_device(features, column_heights, weight_one, bias_one, weight_two, bias_two):
    peers, chans = lax.axis_size("space"), lax.axis_size("chan")
    halo = 1 if peers > COL_Y else 0

    swap = order()
    own_part = pack(weight_one, bias_one, swap)
    near_part = lax.ppermute(own_part, "chan", [(c, c ^ 1) for c in range(chans)])
    fields, cross, mate = arrange(column_heights, features, swap, own_part)
    sent_part, cross = lax.optimization_barrier((own_part, cross))
    far_part = lax.ppermute(sent_part, ("space", "chan"), far_pairs(peers, chans))
    cross = lax.ppermute(cross, "space", across_pairs(peers))
    near_part, mate = lax.optimization_barrier((near_part, mate))
    mate = to_mate(mate)
    if halo:
        fields = with_x_borders(jnp.concatenate([cross, fields, mate[None]], axis=0), peers)
        cross, fields, mate = fields[:2], fields[2:-1], fields[-1]

    inner_a, near = first_near(halo, column_heights, fields, own_part, near_part)
    far_part, inner_a = lax.optimization_barrier((far_part, inner_a))
    other_part = to_mate(far_part)
    matrices = fill(column_heights, weight_two, bias_two, inner_a)
    inner_b, row_seven, far = first_far(halo, column_heights, fields, mate, far_part, other_part, near, matrices[-1])
    mate = to_mate(row_seven)
    done_inner, sums = second_inner(halo, column_heights, fields, near, far, inner_a, inner_b, row_seven, matrices)
    hidden = (inner_a, inner_b, row_seven, mate)
    return last(halo, column_heights, fields, cross, near, far, sums, hidden, done_inner, matrices)


def solution(mesh):
    placed = (
        P("space", None, None, None, None),
        P(),
        P(None, "chan", None),
        P("chan"),
        P(None, "chan", None),
        P("chan"),
    )
    return jax.shard_map(
        on_device,
        mesh=mesh,
        in_specs=placed,
        out_specs=P("space", "chan", None, None, None),
        check_vma=False,
    )
```

```python
import functools

import jax
import jax.numpy as jnp
from jax import lax
from jax.experimental import pallas as pl
from jax.experimental.pallas import tpu as pltpu
from jax.sharding import PartitionSpec as P

COL_Y = 8
TAPS = 3
BF16 = jnp.bfloat16
F32 = jnp.float32
ANY = pl.BlockSpec(memory_space=pl.ANY)
WHOLE = pl.BlockSpec(memory_space=pltpu.VMEM)
SCALARS = pl.BlockSpec(memory_space=pltpu.SMEM)


class Place:
    def __init__(self, heights):
        self.heights = heights
        self.column = lax.axis_index("space")
        self.peers = lax.axis_size("space")
        self.odd = lax.rem(self.column, 2)
        chan = lax.axis_index("chan")
        self.half = lax.div(chan, 2)
        near = lax.rem(chan, 2)
        far = jnp.where(self.odd == 1, 1 - near, near)
        self.slots = (near, 1 - near, far, 1 - far)

    def top(self, by_x=0, across=False):
        column, inside = self.column, True
        if across:
            y = lax.rem(column, COL_Y)
            step = jnp.where(self.odd == 1, 1, -1)
            inside = (y + step >= 0) & (y + step < COL_Y)
            column = column + step
        if by_x:
            column = column + by_x * COL_Y
            inside = inside & (column >= 0) & (column < self.peers)
        column = jnp.clip(column, 0, self.peers - 1)
        return jnp.where(inside, self.heights[column] * 8, 0)


def as_column(row):
    size = row.shape[1]
    wide = jnp.broadcast_to(row, (size, size))
    same = lax.broadcasted_iota(jnp.int32, (size, size), 0) == lax.broadcasted_iota(jnp.int32, (size, size), 1)
    return jnp.sum(jnp.where(same, wide, 0.0), axis=1, keepdims=True)


def order_kernel(swap):
    odd = lax.rem(lax.axis_index("space"), 2)
    group = swap.shape[0] // COL_Y
    row = lax.broadcasted_iota(jnp.int32, swap.shape, 0)
    column = lax.broadcasted_iota(jnp.int32, swap.shape, 1)
    u = lax.div(row, group)
    y = jnp.where(odd == 1, COL_Y - 1 - u, u)
    swap[...] = (column == lax.rem(row, group) * COL_Y + y).astype(F32).astype(BF16)


def pack_kernel(weights, bias, after, packed):
    taps, rows, lanes = weights.shape
    packed[:taps] = weights[...]
    column = as_column(bias[...])
    lane = lax.broadcasted_iota(jnp.int32, (rows, lanes), 1)
    extra = jnp.zeros((rows, lanes), F32)
    for at in range(3):
        piece = column.astype(BF16).astype(F32)
        extra = jnp.where(lane == at, piece, extra)
        column = column - piece
    packed[taps] = extra.astype(BF16)


def arrange_kernel(heights, features, swap, after, fields, cross, mate):
    _, channels, width, _, depth = features.shape
    place = Place(heights)
    group = 256 // COL_Y
    live = lax.broadcasted_iota(jnp.int32, (1, depth), 1) < place.top()
    for x in range(width):
        for first in range(0, channels, group):
            tile = features[0, first : first + group, x].reshape(256, depth)
            moved = jnp.dot(swap[...], tile, preferred_element_type=F32)
            moved = jnp.where(live, moved, 0.0).astype(BF16).reshape(COL_Y, group, depth)
            fields[:, x, first : first + group] = moved
            cross[:, x, first : first + group] = moved[:2]
            mate[x, first : first + group] = moved[COL_Y - 1]


def finish(partial, bias, live_top):
    rows, depth = partial.shape[0] // TAPS, partial.shape[1]
    z = lax.broadcasted_iota(jnp.int32, (rows, depth), 1)
    below = jnp.where(z == 0, 0.0, pltpu.roll(partial[:rows], 1, 1))
    above = jnp.where(z == depth - 1, 0.0, pltpu.roll(partial[2 * rows :], depth - 1, 1))
    total = jnp.maximum(below + partial[rows : 2 * rows] + above + bias, 0.0)
    return jnp.where(z < live_top, total, 0.0).astype(BF16)


def fill_first(parts, slots, odd, matrix, low_matrix, high_matrix, bias):
    quarter, channels = parts[0].shape[1], parts[0].shape[2]
    block = quarter * len(parts)
    for part, slot in zip(parts, slots, strict=True):
        at = slot * quarter
        for k in range(TAPS):
            span = pl.ds(pl.multiple_of(k * block + at, quarter), quarter)
            for j in range(TAPS):
                tap_j = jnp.where(odd == 1, 2 - j, j)
                for i in range(TAPS):
                    tile = part[9 * i + 3 * tap_j + k]
                    matrix[span, pl.ds((j * TAPS + i) * channels, channels)] = tile
                    if i > 0:
                        low_matrix[span, pl.ds((j * 2 + i - 1) * channels, channels)] = tile
                    if i < 2:
                        high_matrix[span, pl.ds((j * 2 + i) * channels, channels)] = tile
        extra = part[27].astype(F32)
        value = extra[:, 0:1] + extra[:, 1:2] + extra[:, 2:3]
        bias[pl.ds(pl.multiple_of(at, quarter), quarter), :] = jnp.broadcast_to(value, (quarter, bias.shape[1]))


def reach(x, width, stored, pad):
    return max(x - 1 + pad, 0), min(x + width + 1 + pad, stored)


def first_sums(get, stored, halo, matrices, taps=range(TAPS)):
    for x in range(-halo, COL_Y + halo):
        low, high = reach(x, 1, stored, 2 * halo)
        lhs = matrices[0]
        if high - low == 2:
            lhs = matrices[1] if x == 0 else matrices[2]
        wide = lhs.shape[1] // TAPS
        taken = jnp.concatenate([get(j, low, high) for j in taps], axis=0)
        columns = slice(taps[0] * wide, (taps[-1] + 1) * wide)
        yield x, jnp.dot(lhs[:, columns], taken, preferred_element_type=F32)


def first_row(get, stored, halo, matrices, bias, top):
    for x, partial in first_sums(get, stored, halo, matrices):
        yield x + halo, finish(partial, bias[:, 0:1], top(side_of(x)))


def side_of(x):
    return -1 if x < 0 else 1 if x >= COL_Y else 0


def span_of(ref, *at):
    *lead, low, high = at
    value = ref[(*lead, slice(low, high))]
    return value.reshape(-1, value.shape[-1])


def inner_rows(own, out, halo, matrices, bias, top):
    for u in range(COL_Y - 2):
        for x, done in first_row(lambda j, a, b: span_of(own, u + j, a, b), own.shape[1], halo, matrices, bias, top):
            out[u, x] = done


def first_near_kernel(halo, heights, own, part_a, part_b, out, matrix, low_matrix, high_matrix, bias):
    place = Place(heights)
    fill_first([part_a, part_b], place.slots[:2], place.odd, matrix, low_matrix, high_matrix, bias)
    inner_rows(own, out, halo, (matrix, low_matrix, high_matrix), bias, place.top)


def first_far_kernel(
    halo, heights, own, mate, part_a, part_b, near, low_near, high_near, bias_near, after,
    out, out_last, matrix, low_matrix, high_matrix, bias,
):
    place = Place(heights)
    fill_first([part_a, part_b], place.slots[2:], place.odd, matrix, low_matrix, high_matrix, bias)
    far = (matrix, low_matrix, high_matrix)
    inner_rows(own, out, halo, far, bias, place.top)

    def get(j, a, b):
        return span_of(mate, a, b) if j == 2 else span_of(own, COL_Y - 2 + j, a, b)

    matrices, biases = join(((near, low_near, high_near), bias_near), (far, bias))
    for x, done in first_row(get, own.shape[1], halo, matrices, biases, place.top):
        out_last[x] = done


class Joined:
    def __init__(self, near, far):
        self.near, self.far = near, far
        self.shape = (2 * near.shape[0], near.shape[1])

    def __getitem__(self, at):
        columns = at[1]
        rows = self.near.shape[0] // TAPS
        pieces = [ref[k * rows : (k + 1) * rows, columns] for k in range(TAPS) for ref in (self.near, self.far)]
        return jnp.concatenate(pieces, axis=0)


def join(near, far):
    return [Joined(*each) for each in zip(near[0], far[0], strict=True)], jnp.concatenate([near[1][...], far[1][...]], axis=0)


def fill_second(weights, place, matrix, low_matrix, high_matrix):
    quarter, channels = weights.shape[1], weights.shape[2]
    empty = jnp.zeros((quarter, channels), BF16)
    for k in range(TAPS):
        for to in range(2):
            span = pl.ds((k * 2 + to) * quarter, quarter)
            for j in range(TAPS):
                tap_j = jnp.where(place.odd == 1, 2 - j, j)
                for at in range(4):
                    tile = empty
                    if 0 <= at - to < TAPS:
                        tile = weights[9 * (at - to) + 3 * tap_j + k].astype(F32)
                        tile = jnp.where(place.half == 1, pltpu.roll(tile, channels // 2, 1), tile).astype(BF16)
                    matrix[span, pl.ds((j * 4 + at) * channels, channels)] = tile
                    if at > 0:
                        low_matrix[span, pl.ds((j * 3 + at - 1) * channels, channels)] = tile
                    if at < 3:
                        high_matrix[span, pl.ds((j * 3 + at) * channels, channels)] = tile


def second_row(get, stored, halo, matrices, both, top):
    quarter = both.shape[0] // 2
    for x in range(0, COL_Y, 2):
        low, high = reach(x, 2, stored, halo)
        lhs = matrices[0]
        if high - low == 3:
            lhs = matrices[1] if x == 0 else matrices[2]
        taken = jnp.concatenate([piece for j in range(TAPS) for piece in get(j, low, high)], axis=0)
        partial = jnp.dot(lhs[...], taken, preferred_element_type=F32)
        done = finish(partial, both, top)
        yield x, done[:quarter], done[quarter:]


def halves(ref_a, ref_b, *at):
    *lead, low, high = at
    return [ref[(*lead, x)] for x in range(low, high) for ref in (ref_a, ref_b)]


def fill_bias(bias, both):
    quarter = bias.shape[1]
    column = jnp.broadcast_to(as_column(bias[...]), (quarter, both.shape[1]))
    both[:quarter] = column
    both[quarter:] = column


def fill_kernel(heights, weights, bias, after, matrix, low_matrix, high_matrix, both):
    fill_second(weights, Place(heights), matrix, low_matrix, high_matrix)
    fill_bias(bias, both)


def second_inner_kernel(
    halo, heights, own, near, low_near, high_near, bias_near, far, low_far, high_far, bias_far,
    inner_a, inner_b, row_seven, matrix, low_matrix, high_matrix, both, out, sums_before, sums_zero,
):
    top = Place(heights).top()
    two = (matrix, low_matrix, high_matrix)

    def row(u, a, b):
        return halves(inner_a, inner_b, u - 1, a, b) if u < 7 else [row_seven[x] for x in range(a, b)]

    for u in range(2, 7):
        for x, here, beside in second_row(lambda j, a, b: row(u - 1 + j, a, b), inner_a.shape[1], halo, two, both[:, 0:1], top):
            out[u - 2, x] = here
            out[u - 2, x + 1] = beside

    matrices, _ = join(((near, low_near, high_near), bias_near), ((far, low_far, high_far), bias_far))
    width = own.shape[1]
    for x, sums in first_sums(lambda j, a, b: span_of(own, j - 2, a, b), width, halo, matrices, (2,)):
        sums_before[x + halo] = sums
    for x, sums in first_sums(lambda j, a, b: span_of(own, j - 1, a, b), width, halo, matrices, (1, 2)):
        sums_zero[x + halo] = sums


def last_kernel(
    halo, heights, own, cross, near, low_near, high_near, bias_near, far, low_far, high_far, bias_far, sums_before, sums_zero,
    inner_a, inner_b, row_seven, mate, done_inner, matrix_two, low_two, high_two, both, out, edge, done_edge, result, sems,
):
    place = Place(heights)
    width, depth = cross.shape[1], cross.shape[3]
    matrices, biases = join(((near, low_near, high_near), bias_near), ((far, low_far, high_far), bias_far))
    for u, sums_own, taps in ((-1, sums_before, (0, 1)), (0, sums_zero, (0,))):
        for x, sums in first_sums(lambda j, a, b: span_of(cross, -u - j, a, b), width, halo, matrices, taps):
            top = place.top(side_of(x), across=u < 0)
            edge[u + 1, x + halo] = finish(sums + sums_own[x + halo], biases[:, 0:1], top)

    def row(u, a, b):
        if 0 < u < 7:
            return halves(inner_a, inner_b, u - 1, a, b)
        return [edge[u + 1, x] if u < 1 else (row_seven if u == 7 else mate)[x] for x in range(a, b)]

    two = (matrix_two, low_two, high_two)
    for at, u in enumerate((0, 1, 7)):
        for x, here, beside in second_row(
            lambda j, a, b: row(u - 1 + j, a, b), inner_a.shape[1], halo, two, both[:, 0:1], place.top()
        ):
            done_edge[at, x] = here
            done_edge[at, x + 1] = beside
    quarter = out.shape[1]
    size = quarter * COL_Y
    at_row = lax.broadcasted_iota(jnp.int32, (size, size), 0)
    at_column = lax.broadcasted_iota(jnp.int32, (size, size), 1)
    y = lax.rem(at_row, COL_Y)
    u = jnp.where(place.odd == 1, COL_Y - 1 - y, y)
    swap = (at_column == u * quarter + lax.div(at_row, COL_Y)).astype(F32).astype(BF16)
    for x in range(COL_Y):
        tiles = [done_edge[0, x], done_edge[1, x]] + [done_inner[v, x] for v in range(COL_Y - 3)] + [done_edge[2, x]]
        tile = jnp.concatenate(tiles, axis=0)
        moved = jnp.dot(swap, tile, preferred_element_type=F32).astype(BF16)
        result[x] = moved.reshape(quarter, COL_Y, depth)
        pltpu.make_async_copy(result.at[x], out.at[0, :, x], sems.at[x]).start()
    for x in range(COL_Y):
        pltpu.make_async_copy(result.at[x], out.at[0, :, x], sems.at[x]).wait()


SHORT, LONG = 2**6, 2**27


def call(kernel, name, inputs, outputs, scratch, nbytes, *args, kinds=None, place=WHOLE):
    return pl.pallas_call(
        kernel,
        out_shape=[jax.ShapeDtypeStruct(*each) for each in zip(outputs, kinds or [BF16] * len(outputs))],
        in_specs=inputs,
        out_specs=[place] * len(outputs),
        scratch_shapes=scratch,
        compiler_params=pltpu.CompilerParams(vmem_limit_bytes=16 * 2**20),
        cost_estimate=pl.CostEstimate(flops=64 * nbytes, bytes_accessed=nbytes, transcendentals=0),
        name=name,
    )(*args)


def order():
    return call(order_kernel, "order", [], [(256, 256)], [], LONG)[0]


def pack(weights, bias, after):
    taps, rows, lanes = weights.shape
    outputs = [(taps + 1, rows, lanes)]
    return call(pack_kernel, "pack", [WHOLE, WHOLE, ANY], outputs, [], LONG, weights, bias[None], after)[0]


def arrange(heights, features, swap, after):
    _, channels, width, _, depth = features.shape
    row = (width, channels, depth)
    outputs = [(COL_Y, *row), (2, *row), row]
    return call(arrange_kernel, "arrange", [SCALARS, WHOLE, WHOLE, ANY], outputs, [], SHORT, heights, features, swap, after)


def first_matrices(channels, rows):
    wide = TAPS * channels
    shapes = [(TAPS * rows, 3 * wide), (TAPS * rows, 2 * wide), (TAPS * rows, 2 * wide), (rows, 128)]
    return shapes, [BF16, BF16, BF16, F32]


def fill(heights, weights, bias, after):
    quarter, channels = weights.shape[1], weights.shape[2]
    tall = TAPS * 2 * quarter
    outputs = [(tall, 12 * channels), (tall, 9 * channels), (tall, 9 * channels), (2 * quarter, 128)]
    kinds = [BF16, BF16, BF16, F32]
    return call(fill_kernel, "fill", [SCALARS, WHOLE, WHOLE, ANY], outputs, [], SHORT, heights, weights, bias[None], after, kinds=kinds)


def first_near(halo, heights, own, part_a, part_b):
    _, _, channels, depth = own.shape
    half, width = 2 * part_a.shape[1], COL_Y + 2 * halo
    shapes, kinds = first_matrices(channels, half)
    inner, *matrices = call(
        functools.partial(first_near_kernel, halo), "first_near", [SCALARS] + [WHOLE] * 3,
        [(COL_Y - 2, width, half, depth), *shapes], [], LONG, heights, own, part_a, part_b, kinds=[BF16, *kinds],
    )
    return inner, matrices


def first_far(halo, heights, own, mate, part_a, part_b, near, after):
    _, _, channels, depth = own.shape
    half, width = 2 * part_a.shape[1], COL_Y + 2 * halo
    shapes, kinds = first_matrices(channels, half)
    inner, row_seven, *matrices = call(
        functools.partial(first_far_kernel, halo), "first_far", [SCALARS] + [WHOLE] * 8 + [ANY],
        [(COL_Y - 2, width, half, depth), (width, channels, depth), *shapes], [], SHORT,
        heights, own, mate, part_a, part_b, *near, after, kinds=[BF16, BF16, *kinds],
    )
    return inner, row_seven, matrices


def second_inner(halo, heights, own, near, far, inner_a, inner_b, row_seven, matrices):
    rows, _, _, depth = inner_a.shape
    channels, width = own.shape[2], COL_Y + 2 * halo
    quarter = matrices[-1].shape[0] // 2
    sums = (width, TAPS * channels, depth)
    outputs, kinds = [(rows - 1, COL_Y, quarter, depth), sums, sums], [BF16, F32, F32]
    args = (heights, own, *near, *far, inner_a, inner_b, row_seven, *matrices)
    kernel = functools.partial(second_inner_kernel, halo)
    done, *sums = call(kernel, "second_inner", [SCALARS] + [WHOLE] * (len(args) - 1), outputs, [], SHORT, *args, kinds=kinds)
    return done, sums


def last(halo, heights, own, cross, near, far, sums, hidden, done_inner, matrices):
    _, _, channels, depth = cross.shape
    quarter, width = matrices[-1].shape[0] // 2, COL_Y + 2 * halo
    scratch = [pltpu.VMEM((2, width, channels, depth), BF16), pltpu.VMEM((3, COL_Y, quarter, depth), BF16)]
    scratch += [pltpu.VMEM((COL_Y, quarter, COL_Y, depth), BF16), pltpu.SemaphoreType.DMA((COL_Y,))]
    outputs = [(1, quarter, COL_Y, COL_Y, depth)]
    args = (heights, own, cross, *near, *far, *sums, *hidden, done_inner, *matrices)
    kernel = functools.partial(last_kernel, halo)
    return call(kernel, "last", [SCALARS] + [WHOLE] * (len(args) - 1), outputs, scratch, SHORT, *args, place=ANY)[0]


def across_pairs(peers):
    pairs = []
    for i in range(peers):
        to = i + 1 if i % 2 else i - 1
        if 0 <= to < peers and to // COL_Y == i // COL_Y:
            pairs.append((i, to))
    return pairs


def to_mate(value):
    return lax.ppermute(value, "space", [(i, i ^ 1) for i in range(lax.axis_size("space"))])


def far_pairs(peers, chans):
    return [(i * chans + c, i * chans + (c ^ (3 if i % 2 else 2))) for i in range(peers) for c in range(chans)]


def with_x_borders(rows, peers):
    forth = [(i, i + COL_Y) for i in range(peers - COL_Y)]
    back = [(i + COL_Y, i) for i in range(peers - COL_Y)]
    before = lax.ppermute(rows[:, COL_Y - 2 :], "space", forth)
    behind = lax.ppermute(rows[:, :2], "space", back)
    return jnp.concatenate([before, rows, behind], axis=1)


def on_device(features, column_heights, weight_one, bias_one, weight_two, bias_two):
    peers, chans = lax.axis_size("space"), lax.axis_size("chan")
    halo = 1 if peers > COL_Y else 0

    swap = order()
    own_part = pack(weight_one, bias_one, swap)
    near_part = lax.ppermute(own_part, "chan", [(c, c ^ 1) for c in range(chans)])
    fields, cross, mate = arrange(column_heights, features, swap, own_part)
    sent_part, cross = lax.optimization_barrier((own_part, cross))
    far_part = lax.ppermute(sent_part, ("space", "chan"), far_pairs(peers, chans))
    cross = lax.ppermute(cross, "space", across_pairs(peers))
    near_part, mate = lax.optimization_barrier((near_part, mate))
    mate = to_mate(mate)
    if halo:
        fields = with_x_borders(jnp.concatenate([cross, fields, mate[None]], axis=0), peers)
        cross, fields, mate = fields[:2], fields[2:-1], fields[-1]

    inner_a, near = first_near(halo, column_heights, fields, own_part, near_part)
    far_part, inner_a = lax.optimization_barrier((far_part, inner_a))
    other_part = to_mate(far_part)
    matrices = fill(column_heights, weight_two, bias_two, inner_a)
    inner_b, row_seven, far = first_far(halo, column_heights, fields, mate, far_part, other_part, near, matrices[-1])
    mate = to_mate(row_seven)
    done_inner, sums = second_inner(halo, column_heights, fields, near, far, inner_a, inner_b, row_seven, matrices)
    hidden = (inner_a, inner_b, row_seven, mate)
    return last(halo, column_heights, fields, cross, near, far, sums, hidden, done_inner, matrices)


def solution(mesh):
    placed = (
        P("space", None, None, None, None),
        P(),
        P(None, "chan", None),
        P("chan"),
        P(None, "chan", None),
        P("chan"),
    )
    return jax.shard_map(
        on_device,
        mesh=mesh,
        in_specs=placed,
        out_specs=P("space", "chan", None, None, None),
        check_vma=False,
    )
```

```python
import functools

import jax
import jax.numpy as jnp
from jax import lax
from jax.experimental import pallas as pl
from jax.experimental.pallas import tpu as pltpu
from jax.sharding import PartitionSpec as P

COL_Y = 8
TAPS = 3
BF16 = jnp.bfloat16
F32 = jnp.float32
ANY = pl.BlockSpec(memory_space=pl.ANY)
WHOLE = pl.BlockSpec(memory_space=pltpu.VMEM)
SCALARS = pl.BlockSpec(memory_space=pltpu.SMEM)


class Place:
    def __init__(self, heights):
        self.heights = heights
        self.column = lax.axis_index("space")
        self.peers = lax.axis_size("space")
        self.odd = lax.rem(self.column, 2)
        chan = lax.axis_index("chan")
        self.half = lax.div(chan, 2)
        near = lax.rem(chan, 2)
        far = jnp.where(self.odd == 1, 1 - near, near)
        self.slots = (near, 1 - near, far, 1 - far)

    def top(self, by_x=0, across=False):
        column, inside = self.column, True
        if across:
            y = lax.rem(column, COL_Y)
            step = jnp.where(self.odd == 1, 1, -1)
            inside = (y + step >= 0) & (y + step < COL_Y)
            column = column + step
        if by_x:
            column = column + by_x * COL_Y
            inside = inside & (column >= 0) & (column < self.peers)
        column = jnp.clip(column, 0, self.peers - 1)
        return jnp.where(inside, self.heights[column] * 8, 0)


def as_column(row):
    size = row.shape[1]
    wide = jnp.broadcast_to(row, (size, size))
    same = lax.broadcasted_iota(jnp.int32, (size, size), 0) == lax.broadcasted_iota(jnp.int32, (size, size), 1)
    return jnp.sum(jnp.where(same, wide, 0.0), axis=1, keepdims=True)


def order_kernel(swap):
    odd = lax.rem(lax.axis_index("space"), 2)
    group = swap.shape[0] // COL_Y
    row = lax.broadcasted_iota(jnp.int32, swap.shape, 0)
    column = lax.broadcasted_iota(jnp.int32, swap.shape, 1)
    u = lax.div(row, group)
    y = jnp.where(odd == 1, COL_Y - 1 - u, u)
    swap[...] = (column == lax.rem(row, group) * COL_Y + y).astype(F32).astype(BF16)


def pack_kernel(weights, bias, after, packed):
    taps, rows, lanes = weights.shape
    packed[:taps] = weights[...]
    column = as_column(bias[...])
    lane = lax.broadcasted_iota(jnp.int32, (rows, lanes), 1)
    extra = jnp.zeros((rows, lanes), F32)
    for at in range(3):
        piece = column.astype(BF16).astype(F32)
        extra = jnp.where(lane == at, piece, extra)
        column = column - piece
    packed[taps] = extra.astype(BF16)


def arrange_kernel(heights, features, swap, after, fields, cross, mate):
    _, channels, width, _, depth = features.shape
    place = Place(heights)
    group = 256 // COL_Y
    live = lax.broadcasted_iota(jnp.int32, (1, depth), 1) < place.top()
    for x in range(width):
        for first in range(0, channels, group):
            tile = features[0, first : first + group, x].reshape(256, depth)
            moved = jnp.dot(swap[...], tile, preferred_element_type=F32)
            moved = jnp.where(live, moved, 0.0).astype(BF16).reshape(COL_Y, group, depth)
            fields[:, x, first : first + group] = moved
            cross[:, x, first : first + group] = moved[:2]
            mate[x, first : first + group] = moved[COL_Y - 1]


def finish(partial, bias, live_top):
    rows, depth = partial.shape[0] // TAPS, partial.shape[1]
    z = lax.broadcasted_iota(jnp.int32, (rows, depth), 1)
    below = jnp.where(z == 0, 0.0, pltpu.roll(partial[:rows], 1, 1))
    above = jnp.where(z == depth - 1, 0.0, pltpu.roll(partial[2 * rows :], depth - 1, 1))
    total = jnp.maximum(below + partial[rows : 2 * rows] + above + bias, 0.0)
    return jnp.where(z < live_top, total, 0.0).astype(BF16)


def fill_first(parts, slots, odd, matrix, low_matrix, high_matrix, bias):
    quarter, channels = parts[0].shape[1], parts[0].shape[2]
    block = quarter * len(parts)
    for part, slot in zip(parts, slots, strict=True):
        at = slot * quarter
        for k in range(TAPS):
            span = pl.ds(pl.multiple_of(k * block + at, quarter), quarter)
            for j in range(TAPS):
                tap_j = jnp.where(odd == 1, 2 - j, j)
                for i in range(TAPS):
                    tile = part[9 * i + 3 * tap_j + k]
                    matrix[span, pl.ds((j * TAPS + i) * channels, channels)] = tile
                    if i > 0:
                        low_matrix[span, pl.ds((j * 2 + i - 1) * channels, channels)] = tile
                    if i < 2:
                        high_matrix[span, pl.ds((j * 2 + i) * channels, channels)] = tile
        extra = part[27].astype(F32)
        value = extra[:, 0:1] + extra[:, 1:2] + extra[:, 2:3]
        bias[pl.ds(pl.multiple_of(at, quarter), quarter), :] = jnp.broadcast_to(value, (quarter, bias.shape[1]))


def reach(x, width, stored, pad):
    return max(x - 1 + pad, 0), min(x + width + 1 + pad, stored)


def first_sums(get, stored, halo, matrices, taps=range(TAPS)):
    for x in range(-halo, COL_Y + halo):
        low, high = reach(x, 1, stored, 2 * halo)
        lhs = matrices[0]
        if high - low == 2:
            lhs = matrices[1] if x == 0 else matrices[2]
        wide = lhs.shape[1] // TAPS
        taken = jnp.concatenate([get(j, low, high) for j in taps], axis=0)
        columns = slice(taps[0] * wide, (taps[-1] + 1) * wide)
        yield x, jnp.dot(lhs[:, columns], taken, preferred_element_type=F32)


def first_row(get, stored, halo, matrices, bias, top):
    for x, partial in first_sums(get, stored, halo, matrices):
        yield x + halo, finish(partial, bias[:, 0:1], top(side_of(x)))


def side_of(x):
    return -1 if x < 0 else 1 if x >= COL_Y else 0


def span_of(ref, *at):
    *lead, low, high = at
    value = ref[(*lead, slice(low, high))]
    return value.reshape(-1, value.shape[-1])


def inner_rows(own, out, halo, matrices, bias, top):
    for u in range(COL_Y - 2):
        for x, done in first_row(lambda j, a, b: span_of(own, u + j, a, b), own.shape[1], halo, matrices, bias, top):
            out[u, x] = done


def first_near_kernel(halo, heights, own, part_a, part_b, out, matrix, low_matrix, high_matrix, bias):
    place = Place(heights)
    fill_first([part_a, part_b], place.slots[:2], place.odd, matrix, low_matrix, high_matrix, bias)
    inner_rows(own, out, halo, (matrix, low_matrix, high_matrix), bias, place.top)


def first_far_kernel(
    halo, heights, own, mate, part_a, part_b, near, low_near, high_near, bias_near, after,
    out, out_last, matrix, low_matrix, high_matrix, bias,
):
    place = Place(heights)
    fill_first([part_a, part_b], place.slots[2:], place.odd, matrix, low_matrix, high_matrix, bias)
    far = (matrix, low_matrix, high_matrix)
    inner_rows(own, out, halo, far, bias, place.top)

    def get(j, a, b):
        return span_of(mate, a, b) if j == 2 else span_of(own, COL_Y - 2 + j, a, b)

    matrices, biases = join(((near, low_near, high_near), bias_near), (far, bias))
    for x, done in first_row(get, own.shape[1], halo, matrices, biases, place.top):
        out_last[x] = done


class Joined:
    def __init__(self, near, far):
        self.near, self.far = near, far
        self.shape = (2 * near.shape[0], near.shape[1])

    def __getitem__(self, at):
        columns = at[1]
        rows = self.near.shape[0] // TAPS
        pieces = [ref[k * rows : (k + 1) * rows, columns] for k in range(TAPS) for ref in (self.near, self.far)]
        return jnp.concatenate(pieces, axis=0)


def join(near, far):
    return [Joined(*each) for each in zip(near[0], far[0], strict=True)], jnp.concatenate([near[1][...], far[1][...]], axis=0)


def fill_second(weights, place, matrix, low_matrix, high_matrix):
    quarter, channels = weights.shape[1], weights.shape[2]
    empty = jnp.zeros((quarter, channels), BF16)
    for k in range(TAPS):
        for to in range(2):
            span = pl.ds((k * 2 + to) * quarter, quarter)
            for j in range(TAPS):
                tap_j = jnp.where(place.odd == 1, 2 - j, j)
                for at in range(4):
                    tile = empty
                    if 0 <= at - to < TAPS:
                        tile = weights[9 * (at - to) + 3 * tap_j + k].astype(F32)
                        tile = jnp.where(place.half == 1, pltpu.roll(tile, channels // 2, 1), tile).astype(BF16)
                    matrix[span, pl.ds((j * 4 + at) * channels, channels)] = tile
                    if at > 0:
                        low_matrix[span, pl.ds((j * 3 + at - 1) * channels, channels)] = tile
                    if at < 3:
                        high_matrix[span, pl.ds((j * 3 + at) * channels, channels)] = tile


def second_sums(get, stored, halo, matrices, taps=range(TAPS)):
    for x in range(0, COL_Y, 2):
        low, high = reach(x, 2, stored, halo)
        lhs = matrices[0]
        if high - low == 3:
            lhs = matrices[1] if x == 0 else matrices[2]
        wide = lhs.shape[1] // TAPS
        taken = jnp.concatenate([piece for j in taps for piece in get(j, low, high)], axis=0)
        yield x, jnp.dot(lhs[:, taps[0] * wide : (taps[-1] + 1) * wide], taken, preferred_element_type=F32)


def second_row(get, stored, halo, matrices, both, top):
    quarter = both.shape[0] // 2
    for x, partial in second_sums(get, stored, halo, matrices):
        done = finish(partial, both, top)
        yield x, done[:quarter], done[quarter:]


def halves(ref_a, ref_b, *at):
    *lead, low, high = at
    return [ref[(*lead, x)] for x in range(low, high) for ref in (ref_a, ref_b)]


def fill_bias(bias, both):
    quarter = bias.shape[1]
    column = jnp.broadcast_to(as_column(bias[...]), (quarter, both.shape[1]))
    both[:quarter] = column
    both[quarter:] = column


def fill_kernel(heights, weights, bias, after, matrix, low_matrix, high_matrix, both):
    fill_second(weights, Place(heights), matrix, low_matrix, high_matrix)
    fill_bias(bias, both)


def second_inner_kernel(
    halo, heights, own, near, low_near, high_near, bias_near, far, low_far, high_far, bias_far,
    inner_a, inner_b, row_seven, matrix, low_matrix, high_matrix, both, out, sums_before, sums_zero, sums_two,
):
    top = Place(heights).top()
    two = (matrix, low_matrix, high_matrix)

    def row(u, a, b):
        return halves(inner_a, inner_b, u - 1, a, b) if u < 7 else [row_seven[x] for x in range(a, b)]

    for u in range(2, 7):
        for x, here, beside in second_row(lambda j, a, b: row(u - 1 + j, a, b), inner_a.shape[1], halo, two, both[:, 0:1], top):
            out[u - 2, x] = here
            out[u - 2, x + 1] = beside
    for u, taps in ((0, (2,)), (1, (1, 2))):
        for x, sums in second_sums(lambda j, a, b: row(u - 1 + j, a, b), inner_a.shape[1], halo, two, taps):
            sums_two[u, x // 2] = sums

    matrices, _ = join(((near, low_near, high_near), bias_near), ((far, low_far, high_far), bias_far))
    width = own.shape[1]
    for x, sums in first_sums(lambda j, a, b: span_of(own, j - 2, a, b), width, halo, matrices, (2,)):
        sums_before[x + halo] = sums
    for x, sums in first_sums(lambda j, a, b: span_of(own, j - 1, a, b), width, halo, matrices, (1, 2)):
        sums_zero[x + halo] = sums


def last_kernel(
    halo, heights, own, cross, near, low_near, high_near, bias_near, far, low_far, high_far, bias_far, sums_before, sums_zero, sums_two,
    inner_a, inner_b, row_seven, mate, done_inner, matrix_two, low_two, high_two, both, out, edge, done_edge, result, sems,
):
    place = Place(heights)
    width, depth = cross.shape[1], cross.shape[3]
    matrices, biases = join(((near, low_near, high_near), bias_near), ((far, low_far, high_far), bias_far))
    for u, sums_own, taps in ((-1, sums_before, (0, 1)), (0, sums_zero, (0,))):
        for x, sums in first_sums(lambda j, a, b: span_of(cross, -u - j, a, b), width, halo, matrices, taps):
            top = place.top(side_of(x), across=u < 0)
            edge[u + 1, x + halo] = finish(sums + sums_own[x + halo], biases[:, 0:1], top)

    two, stored, quarter = (matrix_two, low_two, high_two), inner_a.shape[1], out.shape[1]
    for u, taps in ((0, (0, 1)), (1, (0,))):
        for x, sums in second_sums(lambda j, a, b: [edge[u + j, x] for x in range(a, b)], stored, halo, two, taps):
            done = finish(sums + sums_two[u, x // 2], both[:, 0:1], place.top())
            done_edge[u, x] = done[:quarter]
            done_edge[u, x + 1] = done[quarter:]

    def row(j, a, b):
        return halves(inner_a, inner_b, 5, a, b) if j == 0 else [(row_seven if j == 1 else mate)[x] for x in range(a, b)]

    for x, here, beside in second_row(row, stored, halo, two, both[:, 0:1], place.top()):
        done_edge[2, x] = here
        done_edge[2, x + 1] = beside
    size = quarter * COL_Y
    at_row = lax.broadcasted_iota(jnp.int32, (size, size), 0)
    at_column = lax.broadcasted_iota(jnp.int32, (size, size), 1)
    y = lax.rem(at_row, COL_Y)
    u = jnp.where(place.odd == 1, COL_Y - 1 - y, y)
    swap = (at_column == u * quarter + lax.div(at_row, COL_Y)).astype(F32).astype(BF16)
    for x in range(COL_Y):
        tiles = [done_edge[0, x], done_edge[1, x]] + [done_inner[v, x] for v in range(COL_Y - 3)] + [done_edge[2, x]]
        tile = jnp.concatenate(tiles, axis=0)
        moved = jnp.dot(swap, tile, preferred_element_type=F32).astype(BF16)
        result[x] = moved.reshape(quarter, COL_Y, depth)
        pltpu.make_async_copy(result.at[x], out.at[0, :, x], sems.at[x]).start()
    for x in range(COL_Y):
        pltpu.make_async_copy(result.at[x], out.at[0, :, x], sems.at[x]).wait()


SHORT, LONG = 2**6, 2**27


def call(kernel, name, inputs, outputs, scratch, nbytes, *args, kinds=None, place=WHOLE):
    return pl.pallas_call(
        kernel,
        out_shape=[jax.ShapeDtypeStruct(*each) for each in zip(outputs, kinds or [BF16] * len(outputs))],
        in_specs=inputs,
        out_specs=[place] * len(outputs),
        scratch_shapes=scratch,
        compiler_params=pltpu.CompilerParams(vmem_limit_bytes=16 * 2**20),
        cost_estimate=pl.CostEstimate(flops=64 * nbytes, bytes_accessed=nbytes, transcendentals=0),
        name=name,
    )(*args)


def order():
    return call(order_kernel, "order", [], [(256, 256)], [], LONG)[0]


def pack(weights, bias, after):
    taps, rows, lanes = weights.shape
    outputs = [(taps + 1, rows, lanes)]
    return call(pack_kernel, "pack", [WHOLE, WHOLE, ANY], outputs, [], LONG, weights, bias[None], after)[0]


def arrange(heights, features, swap, after):
    _, channels, width, _, depth = features.shape
    row = (width, channels, depth)
    outputs = [(COL_Y, *row), (2, *row), row]
    return call(arrange_kernel, "arrange", [SCALARS, WHOLE, WHOLE, ANY], outputs, [], SHORT, heights, features, swap, after)


def first_matrices(channels, rows):
    wide = TAPS * channels
    shapes = [(TAPS * rows, 3 * wide), (TAPS * rows, 2 * wide), (TAPS * rows, 2 * wide), (rows, 128)]
    return shapes, [BF16, BF16, BF16, F32]


def fill(heights, weights, bias, after):
    quarter, channels = weights.shape[1], weights.shape[2]
    tall = TAPS * 2 * quarter
    outputs = [(tall, 12 * channels), (tall, 9 * channels), (tall, 9 * channels), (2 * quarter, 128)]
    kinds = [BF16, BF16, BF16, F32]
    return call(fill_kernel, "fill", [SCALARS, WHOLE, WHOLE, ANY], outputs, [], SHORT, heights, weights, bias[None], after, kinds=kinds)


def first_near(halo, heights, own, part_a, part_b):
    _, _, channels, depth = own.shape
    half, width = 2 * part_a.shape[1], COL_Y + 2 * halo
    shapes, kinds = first_matrices(channels, half)
    inner, *matrices = call(
        functools.partial(first_near_kernel, halo), "first_near", [SCALARS] + [WHOLE] * 3,
        [(COL_Y - 2, width, half, depth), *shapes], [], LONG, heights, own, part_a, part_b, kinds=[BF16, *kinds],
    )
    return inner, matrices


def first_far(halo, heights, own, mate, part_a, part_b, near, after):
    _, _, channels, depth = own.shape
    half, width = 2 * part_a.shape[1], COL_Y + 2 * halo
    shapes, kinds = first_matrices(channels, half)
    inner, row_seven, *matrices = call(
        functools.partial(first_far_kernel, halo), "first_far", [SCALARS] + [WHOLE] * 8 + [ANY],
        [(COL_Y - 2, width, half, depth), (width, channels, depth), *shapes], [], SHORT,
        heights, own, mate, part_a, part_b, *near, after, kinds=[BF16, BF16, *kinds],
    )
    return inner, row_seven, matrices


def second_inner(halo, heights, own, near, far, inner_a, inner_b, row_seven, matrices):
    rows, _, _, depth = inner_a.shape
    channels, width = own.shape[2], COL_Y + 2 * halo
    quarter = matrices[-1].shape[0] // 2
    sums = (width, TAPS * channels, depth)
    outputs = [(rows - 1, COL_Y, quarter, depth), sums, sums, (2, COL_Y // 2, TAPS * 2 * quarter, depth)]
    kinds = [BF16, F32, F32, F32]
    args = (heights, own, *near, *far, inner_a, inner_b, row_seven, *matrices)
    kernel = functools.partial(second_inner_kernel, halo)
    done, *sums = call(kernel, "second_inner", [SCALARS] + [WHOLE] * (len(args) - 1), outputs, [], SHORT, *args, kinds=kinds)
    return done, sums


def last(halo, heights, own, cross, near, far, sums, hidden, done_inner, matrices):
    _, _, channels, depth = cross.shape
    quarter, width = matrices[-1].shape[0] // 2, COL_Y + 2 * halo
    scratch = [pltpu.VMEM((2, width, channels, depth), BF16), pltpu.VMEM((3, COL_Y, quarter, depth), BF16)]
    scratch += [pltpu.VMEM((COL_Y, quarter, COL_Y, depth), BF16), pltpu.SemaphoreType.DMA((COL_Y,))]
    outputs = [(1, quarter, COL_Y, COL_Y, depth)]
    args = (heights, own, cross, *near, *far, *sums, *hidden, done_inner, *matrices)
    kernel = functools.partial(last_kernel, halo)
    return call(kernel, "last", [SCALARS] + [WHOLE] * (len(args) - 1), outputs, scratch, SHORT, *args, place=ANY)[0]


def across_pairs(peers):
    pairs = []
    for i in range(peers):
        to = i + 1 if i % 2 else i - 1
        if 0 <= to < peers and to // COL_Y == i // COL_Y:
            pairs.append((i, to))
    return pairs


def to_mate(value):
    return lax.ppermute(value, "space", [(i, i ^ 1) for i in range(lax.axis_size("space"))])


def far_pairs(peers, chans):
    return [(i * chans + c, i * chans + (c ^ (3 if i % 2 else 2))) for i in range(peers) for c in range(chans)]


def with_x_borders(rows, peers):
    forth = [(i, i + COL_Y) for i in range(peers - COL_Y)]
    back = [(i + COL_Y, i) for i in range(peers - COL_Y)]
    before = lax.ppermute(rows[:, COL_Y - 2 :], "space", forth)
    behind = lax.ppermute(rows[:, :2], "space", back)
    return jnp.concatenate([before, rows, behind], axis=1)


def on_device(features, column_heights, weight_one, bias_one, weight_two, bias_two):
    peers, chans = lax.axis_size("space"), lax.axis_size("chan")
    halo = 1 if peers > COL_Y else 0

    swap = order()
    own_part = pack(weight_one, bias_one, swap)
    near_part = lax.ppermute(own_part, "chan", [(c, c ^ 1) for c in range(chans)])
    fields, cross, mate = arrange(column_heights, features, swap, own_part)
    sent_part, cross = lax.optimization_barrier((own_part, cross))
    far_part = lax.ppermute(sent_part, ("space", "chan"), far_pairs(peers, chans))
    cross = lax.ppermute(cross, "space", across_pairs(peers))
    near_part, mate = lax.optimization_barrier((near_part, mate))
    mate = to_mate(mate)
    if halo:
        fields = with_x_borders(jnp.concatenate([cross, fields, mate[None]], axis=0), peers)
        cross, fields, mate = fields[:2], fields[2:-1], fields[-1]

    inner_a, near = first_near(halo, column_heights, fields, own_part, near_part)
    far_part, inner_a = lax.optimization_barrier((far_part, inner_a))
    other_part = to_mate(far_part)
    matrices = fill(column_heights, weight_two, bias_two, inner_a)
    inner_b, row_seven, far = first_far(halo, column_heights, fields, mate, far_part, other_part, near, matrices[-1])
    mate = to_mate(row_seven)
    done_inner, sums = second_inner(halo, column_heights, fields, near, far, inner_a, inner_b, row_seven, matrices)
    hidden = (inner_a, inner_b, row_seven, mate)
    return last(halo, column_heights, fields, cross, near, far, sums, hidden, done_inner, matrices)


def solution(mesh):
    placed = (
        P("space", None, None, None, None),
        P(),
        P(None, "chan", None),
        P("chan"),
        P(None, "chan", None),
        P("chan"),
    )
    return jax.shard_map(
        on_device,
        mesh=mesh,
        in_specs=placed,
        out_specs=P("space", "chan", None, None, None),
        check_vma=False,
    )
```

```python
import functools

import jax
import jax.numpy as jnp
from jax import lax
from jax.experimental import pallas as pl
from jax.experimental.pallas import tpu as pltpu
from jax.sharding import PartitionSpec as P

COL_Y = 8
TAPS = 3
BF16 = jnp.bfloat16
F32 = jnp.float32
ANY = pl.BlockSpec(memory_space=pl.ANY)
WHOLE = pl.BlockSpec(memory_space=pltpu.VMEM)
SCALARS = pl.BlockSpec(memory_space=pltpu.SMEM)


class Place:
    def __init__(self, heights):
        self.heights = heights
        self.column = lax.axis_index("space")
        self.peers = lax.axis_size("space")
        self.odd = lax.rem(self.column, 2)
        chan = lax.axis_index("chan")
        self.half = lax.div(chan, 2)
        near = lax.rem(chan, 2)
        far = jnp.where(self.odd == 1, 1 - near, near)
        self.slots = (near, 1 - near, far, 1 - far)

    def top(self, by_x=0, across=False):
        column, inside = self.column, True
        if across:
            y = lax.rem(column, COL_Y)
            step = jnp.where(self.odd == 1, 1, -1)
            inside = (y + step >= 0) & (y + step < COL_Y)
            column = column + step
        if by_x:
            column = column + by_x * COL_Y
            inside = inside & (column >= 0) & (column < self.peers)
        column = jnp.clip(column, 0, self.peers - 1)
        return jnp.where(inside, self.heights[column] * 8, 0)


def as_column(row):
    size = row.shape[1]
    wide = jnp.broadcast_to(row, (size, size))
    same = lax.broadcasted_iota(jnp.int32, (size, size), 0) == lax.broadcasted_iota(jnp.int32, (size, size), 1)
    return jnp.sum(jnp.where(same, wide, 0.0), axis=1, keepdims=True)


def order_kernel(swap):
    odd = lax.rem(lax.axis_index("space"), 2)
    group = swap.shape[0] // COL_Y
    row = lax.broadcasted_iota(jnp.int32, swap.shape, 0)
    column = lax.broadcasted_iota(jnp.int32, swap.shape, 1)
    u = lax.div(row, group)
    y = jnp.where(odd == 1, COL_Y - 1 - u, u)
    swap[...] = (column == lax.rem(row, group) * COL_Y + y).astype(F32).astype(BF16)


def pack_kernel(weights, bias, after, packed):
    taps, rows, lanes = weights.shape
    packed[:taps] = weights[...]
    column = as_column(bias[...])
    lane = lax.broadcasted_iota(jnp.int32, (rows, lanes), 1)
    extra = jnp.zeros((rows, lanes), F32)
    for at in range(3):
        piece = column.astype(BF16).astype(F32)
        extra = jnp.where(lane == at, piece, extra)
        column = column - piece
    packed[taps] = extra.astype(BF16)


def arrange_kernel(heights, features, swap, after, fields, cross, mate):
    _, channels, width, _, depth = features.shape
    place = Place(heights)
    group = 256 // COL_Y
    live = lax.broadcasted_iota(jnp.int32, (1, depth), 1) < place.top()
    for x in range(width):
        for first in range(0, channels, group):
            tile = features[0, first : first + group, x].reshape(256, depth)
            moved = jnp.dot(swap[...], tile, preferred_element_type=F32)
            moved = jnp.where(live, moved, 0.0).astype(BF16).reshape(COL_Y, group, depth)
            fields[:, x, first : first + group] = moved
            cross[:, x, first : first + group] = moved[:2]
            mate[x, first : first + group] = moved[COL_Y - 1]


def finish(partial, bias, live_top):
    rows, depth = partial.shape[0] // TAPS, partial.shape[1]
    z = lax.broadcasted_iota(jnp.int32, (rows, depth), 1)
    below = jnp.where(z == 0, 0.0, pltpu.roll(partial[:rows], 1, 1))
    above = jnp.where(z == depth - 1, 0.0, pltpu.roll(partial[2 * rows :], depth - 1, 1))
    total = jnp.maximum(below + partial[rows : 2 * rows] + above + bias, 0.0)
    return jnp.where(z < live_top, total, 0.0).astype(BF16)


def fill_first(parts, slots, odd, matrix, low_matrix, high_matrix, bias):
    quarter, channels = parts[0].shape[1], parts[0].shape[2]
    block = quarter * len(parts)
    for part, slot in zip(parts, slots, strict=True):
        at = slot * quarter
        for k in range(TAPS):
            span = pl.ds(pl.multiple_of(k * block + at, quarter), quarter)
            for j in range(TAPS):
                tap_j = jnp.where(odd == 1, 2 - j, j)
                for i in range(TAPS):
                    tile = part[9 * i + 3 * tap_j + k]
                    matrix[span, pl.ds((j * TAPS + i) * channels, channels)] = tile
                    if i > 0:
                        low_matrix[span, pl.ds((j * 2 + i - 1) * channels, channels)] = tile
                    if i < 2:
                        high_matrix[span, pl.ds((j * 2 + i) * channels, channels)] = tile
        extra = part[27].astype(F32)
        value = extra[:, 0:1] + extra[:, 1:2] + extra[:, 2:3]
        bias[pl.ds(pl.multiple_of(at, quarter), quarter), :] = jnp.broadcast_to(value, (quarter, bias.shape[1]))


def reach(x, width, stored, pad):
    return max(x - 1 + pad, 0), min(x + width + 1 + pad, stored)


def first_sums(get, stored, halo, matrices, taps=range(TAPS)):
    for x in range(-halo, COL_Y + halo):
        low, high = reach(x, 1, stored, 2 * halo)
        lhs = matrices[0]
        if high - low == 2:
            lhs = matrices[1] if x == 0 else matrices[2]
        wide = lhs.shape[1] // TAPS
        taken = jnp.concatenate([get(j, low, high) for j in taps], axis=0)
        columns = slice(taps[0] * wide, (taps[-1] + 1) * wide)
        yield x, jnp.dot(lhs[:, columns], taken, preferred_element_type=F32)


def first_row(get, stored, halo, matrices, bias, top):
    for x, partial in first_sums(get, stored, halo, matrices):
        yield x + halo, finish(partial, bias[:, 0:1], top(side_of(x)))


def side_of(x):
    return -1 if x < 0 else 1 if x >= COL_Y else 0


def span_of(ref, *at):
    *lead, low, high = at
    value = ref[(*lead, slice(low, high))]
    return value.reshape(-1, value.shape[-1])


def inner_rows(own, out, halo, matrices, bias, top):
    for u in range(COL_Y - 2):
        for x, done in first_row(lambda j, a, b: span_of(own, u + j, a, b), own.shape[1], halo, matrices, bias, top):
            out[u, x] = done


def first_near_kernel(halo, heights, own, part_a, part_b, out, matrix, low_matrix, high_matrix, bias):
    place = Place(heights)
    fill_first([part_a, part_b], place.slots[:2], place.odd, matrix, low_matrix, high_matrix, bias)
    inner_rows(own, out, halo, (matrix, low_matrix, high_matrix), bias, place.top)


def first_far_kernel(halo, heights, own, mate, part_a, part_b, near_seven, out, out_last, matrix, low_matrix, high_matrix, bias):
    place = Place(heights)
    fill_first([part_a, part_b], place.slots[2:], place.odd, matrix, low_matrix, high_matrix, bias)
    far = (matrix, low_matrix, high_matrix)
    inner_rows(own, out, halo, far, bias, place.top)

    def get(j, a, b):
        return span_of(mate, a, b) if j == 2 else span_of(own, COL_Y - 2 + j, a, b)

    half = bias.shape[0]
    out_last[:, :half] = near_seven[...]
    for x, done in first_row(get, own.shape[1], halo, far, bias, place.top):
        out_last[x, half:] = done


class Joined:
    def __init__(self, near, far):
        self.near, self.far = near, far
        self.shape = (2 * near.shape[0], near.shape[1])

    def __getitem__(self, at):
        columns = at[1]
        rows = self.near.shape[0] // TAPS
        pieces = [ref[k * rows : (k + 1) * rows, columns] for k in range(TAPS) for ref in (self.near, self.far)]
        return jnp.concatenate(pieces, axis=0)


def join(near, far):
    return [Joined(*each) for each in zip(near[0], far[0], strict=True)], jnp.concatenate([near[1][...], far[1][...]], axis=0)


def fill_second(weights, place, matrix, low_matrix, high_matrix):
    quarter, channels = weights.shape[1], weights.shape[2]
    empty = jnp.zeros((quarter, channels), BF16)
    for k in range(TAPS):
        for to in range(2):
            span = pl.ds((k * 2 + to) * quarter, quarter)
            for j in range(TAPS):
                tap_j = jnp.where(place.odd == 1, 2 - j, j)
                for at in range(4):
                    tile = empty
                    if 0 <= at - to < TAPS:
                        tile = weights[9 * (at - to) + 3 * tap_j + k].astype(F32)
                        tile = jnp.where(place.half == 1, pltpu.roll(tile, channels // 2, 1), tile).astype(BF16)
                    matrix[span, pl.ds((j * 4 + at) * channels, channels)] = tile
                    if at > 0:
                        low_matrix[span, pl.ds((j * 3 + at - 1) * channels, channels)] = tile
                    if at < 3:
                        high_matrix[span, pl.ds((j * 3 + at) * channels, channels)] = tile


def second_sums(get, stored, halo, matrices, taps=range(TAPS)):
    for x in range(0, COL_Y, 2):
        low, high = reach(x, 2, stored, halo)
        lhs = matrices[0]
        if high - low == 3:
            lhs = matrices[1] if x == 0 else matrices[2]
        wide = lhs.shape[1] // TAPS
        taken = jnp.concatenate([piece for j in taps for piece in get(j, low, high)], axis=0)
        yield x, jnp.dot(lhs[:, taps[0] * wide : (taps[-1] + 1) * wide], taken, preferred_element_type=F32)


def second_row(get, stored, halo, matrices, both, top):
    quarter = both.shape[0] // 2
    for x, partial in second_sums(get, stored, halo, matrices):
        done = finish(partial, both, top)
        yield x, done[:quarter], done[quarter:]


def halves(ref_a, ref_b, *at):
    *lead, low, high = at
    return [ref[(*lead, x)] for x in range(low, high) for ref in (ref_a, ref_b)]


def fill_bias(bias, both):
    quarter = bias.shape[1]
    column = jnp.broadcast_to(as_column(bias[...]), (quarter, both.shape[1]))
    both[:quarter] = column
    both[quarter:] = column


def fill_kernel(
    halo, heights, weights, bias, own, mate, near, low_near, high_near, bias_near, after,
    matrix, low_matrix, high_matrix, both, near_seven,
):
    place = Place(heights)
    fill_second(weights, place, matrix, low_matrix, high_matrix)
    fill_bias(bias, both)

    def get(j, a, b):
        return span_of(mate, a, b) if j == 2 else span_of(own, COL_Y - 2 + j, a, b)

    for x, done in first_row(get, own.shape[1], halo, (near, low_near, high_near), bias_near, place.top):
        near_seven[x] = done


def second_inner_kernel(
    halo, heights, own, near, low_near, high_near, bias_near, far, low_far, high_far, bias_far,
    inner_a, inner_b, row_seven, matrix, low_matrix, high_matrix, both, out, sums_before, sums_zero, sums_two,
):
    top = Place(heights).top()
    two = (matrix, low_matrix, high_matrix)

    def row(u, a, b):
        return halves(inner_a, inner_b, u - 1, a, b) if u < 7 else [row_seven[x] for x in range(a, b)]

    for u in range(2, 7):
        for x, here, beside in second_row(lambda j, a, b: row(u - 1 + j, a, b), inner_a.shape[1], halo, two, both[:, 0:1], top):
            out[u - 2, x] = here
            out[u - 2, x + 1] = beside
    for u, taps in ((0, (2,)), (1, (1, 2))):
        for x, sums in second_sums(lambda j, a, b: row(u - 1 + j, a, b), inner_a.shape[1], halo, two, taps):
            sums_two[u, x // 2] = sums

    matrices, _ = join(((near, low_near, high_near), bias_near), ((far, low_far, high_far), bias_far))
    width = own.shape[1]
    for x, sums in first_sums(lambda j, a, b: span_of(own, j - 2, a, b), width, halo, matrices, (2,)):
        sums_before[x + halo] = sums
    for x, sums in first_sums(lambda j, a, b: span_of(own, j - 1, a, b), width, halo, matrices, (1, 2)):
        sums_zero[x + halo] = sums


def last_kernel(
    halo, heights, own, cross, near, low_near, high_near, bias_near, far, low_far, high_far, bias_far, sums_before, sums_zero, sums_two,
    inner_a, inner_b, row_seven, mate, done_inner, matrix_two, low_two, high_two, both, out, edge, result, sems,
):
    place = Place(heights)
    width, depth = cross.shape[1], cross.shape[3]
    matrices, biases = join(((near, low_near, high_near), bias_near), ((far, low_far, high_far), bias_far))
    for u, sums_own, taps in ((-1, sums_before, (0, 1)), (0, sums_zero, (0,))):
        for x, sums in first_sums(lambda j, a, b: span_of(cross, -u - j, a, b), width, halo, matrices, taps):
            top = place.top(side_of(x), across=u < 0)
            edge[u + 1, x + halo] = finish(sums + sums_own[x + halo], biases[:, 0:1], top)

    two, stored, quarter = (matrix_two, low_two, high_two), inner_a.shape[1], out.shape[1]
    size = quarter * COL_Y
    at_row = lax.broadcasted_iota(jnp.int32, (size, size), 0)
    at_column = lax.broadcasted_iota(jnp.int32, (size, size), 1)
    y = lax.rem(at_row, COL_Y)
    u = jnp.where(place.odd == 1, COL_Y - 1 - y, y)
    swap = (at_column == u * quarter + lax.div(at_row, COL_Y)).astype(F32).astype(BF16)

    def row(j, a, b):
        return halves(inner_a, inner_b, 5, a, b) if j == 0 else [(row_seven if j == 1 else mate)[x] for x in range(a, b)]

    rows_two = [
        second_row(row, stored, halo, two, both[:, 0:1], place.top()),
        second_sums(lambda j, a, b: [edge[j, x] for x in range(a, b)], stored, halo, two, (0, 1)),
        second_sums(lambda j, a, b: [edge[1 + j, x] for x in range(a, b)], stored, halo, two, (0,)),
    ]
    for (x, *seven), (_, sums_a), (_, sums_b) in zip(*rows_two, strict=True):
        first = finish(sums_a + sums_two[0, x // 2], both[:, 0:1], place.top())
        second = finish(sums_b + sums_two[1, x // 2], both[:, 0:1], place.top())
        for more in range(2):
            span = slice(more * quarter, (more + 1) * quarter)
            tiles = [first[span], second[span]] + [done_inner[v, x + more] for v in range(COL_Y - 3)] + [seven[more]]
            moved = jnp.dot(swap, jnp.concatenate(tiles, axis=0), preferred_element_type=F32).astype(BF16)
            result[x + more] = moved.reshape(quarter, COL_Y, depth)
            pltpu.make_async_copy(result.at[x + more], out.at[0, :, x + more], sems.at[x + more]).start()
    for x in range(COL_Y):
        pltpu.make_async_copy(result.at[x], out.at[0, :, x], sems.at[x]).wait()


SHORT, LONG = 2**6, 2**27


def call(kernel, name, inputs, outputs, scratch, nbytes, *args, kinds=None, place=WHOLE):
    return pl.pallas_call(
        kernel,
        out_shape=[jax.ShapeDtypeStruct(*each) for each in zip(outputs, kinds or [BF16] * len(outputs))],
        in_specs=inputs,
        out_specs=[place] * len(outputs),
        scratch_shapes=scratch,
        compiler_params=pltpu.CompilerParams(vmem_limit_bytes=16 * 2**20),
        cost_estimate=pl.CostEstimate(flops=64 * nbytes, bytes_accessed=nbytes, transcendentals=0),
        name=name,
    )(*args)


def order():
    return call(order_kernel, "order", [], [(256, 256)], [], LONG)[0]


def pack(weights, bias, after):
    taps, rows, lanes = weights.shape
    outputs = [(taps + 1, rows, lanes)]
    return call(pack_kernel, "pack", [WHOLE, WHOLE, ANY], outputs, [], LONG, weights, bias[None], after)[0]


def arrange(heights, features, swap, after):
    _, channels, width, _, depth = features.shape
    row = (width, channels, depth)
    outputs = [(COL_Y, *row), (2, *row), row]
    return call(arrange_kernel, "arrange", [SCALARS, WHOLE, WHOLE, ANY], outputs, [], SHORT, heights, features, swap, after)


def first_matrices(channels, rows):
    wide = TAPS * channels
    shapes = [(TAPS * rows, 3 * wide), (TAPS * rows, 2 * wide), (TAPS * rows, 2 * wide), (rows, 128)]
    return shapes, [BF16, BF16, BF16, F32]


def fill(halo, heights, weights, bias, own, mate, near, after):
    quarter, channels, depth = weights.shape[1], weights.shape[2], own.shape[3]
    tall, half = TAPS * 2 * quarter, near[-1].shape[0]
    outputs = [(tall, 12 * channels), (tall, 9 * channels), (tall, 9 * channels), (2 * quarter, 128)]
    outputs.append((COL_Y + 2 * halo, half, depth))
    args = (heights, weights, bias[None], own, mate, *near, after)
    inputs = [SCALARS] + [WHOLE] * (len(args) - 2) + [ANY]
    kernel = functools.partial(fill_kernel, halo)
    *matrices, seven = call(kernel, "fill", inputs, outputs, [], SHORT, *args, kinds=[BF16, BF16, BF16, F32, BF16])
    return matrices, seven


def first_near(halo, heights, own, part_a, part_b):
    _, _, channels, depth = own.shape
    half, width = 2 * part_a.shape[1], COL_Y + 2 * halo
    shapes, kinds = first_matrices(channels, half)
    inner, *matrices = call(
        functools.partial(first_near_kernel, halo), "first_near", [SCALARS] + [WHOLE] * 3,
        [(COL_Y - 2, width, half, depth), *shapes], [], LONG, heights, own, part_a, part_b, kinds=[BF16, *kinds],
    )
    return inner, matrices


def first_far(halo, heights, own, mate, part_a, part_b, near_seven):
    _, _, channels, depth = own.shape
    half, width = 2 * part_a.shape[1], COL_Y + 2 * halo
    shapes, kinds = first_matrices(channels, half)
    inner, row_seven, *matrices = call(
        functools.partial(first_far_kernel, halo), "first_far", [SCALARS] + [WHOLE] * 5,
        [(COL_Y - 2, width, half, depth), (width, channels, depth), *shapes], [], SHORT,
        heights, own, mate, part_a, part_b, near_seven, kinds=[BF16, BF16, *kinds],
    )
    return inner, row_seven, matrices


def second_inner(halo, heights, own, near, far, inner_a, inner_b, row_seven, matrices):
    rows, _, _, depth = inner_a.shape
    channels, width = own.shape[2], COL_Y + 2 * halo
    quarter = matrices[-1].shape[0] // 2
    sums = (width, TAPS * channels, depth)
    outputs = [(rows - 1, COL_Y, quarter, depth), sums, sums, (2, COL_Y // 2, TAPS * 2 * quarter, depth)]
    kinds = [BF16, F32, F32, F32]
    args = (heights, own, *near, *far, inner_a, inner_b, row_seven, *matrices)
    kernel = functools.partial(second_inner_kernel, halo)
    done, *sums = call(kernel, "second_inner", [SCALARS] + [WHOLE] * (len(args) - 1), outputs, [], SHORT, *args, kinds=kinds)
    return done, sums


def last(halo, heights, own, cross, near, far, sums, hidden, done_inner, matrices):
    _, _, channels, depth = cross.shape
    quarter, width = matrices[-1].shape[0] // 2, COL_Y + 2 * halo
    scratch = [pltpu.VMEM((2, width, channels, depth), BF16)]
    scratch += [pltpu.VMEM((COL_Y, quarter, COL_Y, depth), BF16), pltpu.SemaphoreType.DMA((COL_Y,))]
    outputs = [(1, quarter, COL_Y, COL_Y, depth)]
    args = (heights, own, cross, *near, *far, *sums, *hidden, done_inner, *matrices)
    kernel = functools.partial(last_kernel, halo)
    return call(kernel, "last", [SCALARS] + [WHOLE] * (len(args) - 1), outputs, scratch, SHORT, *args, place=ANY)[0]


def across_pairs(peers):
    pairs = []
    for i in range(peers):
        to = i + 1 if i % 2 else i - 1
        if 0 <= to < peers and to // COL_Y == i // COL_Y:
            pairs.append((i, to))
    return pairs


def to_mate(value):
    return lax.ppermute(value, "space", [(i, i ^ 1) for i in range(lax.axis_size("space"))])


def far_pairs(peers, chans):
    return [(i * chans + c, i * chans + (c ^ (3 if i % 2 else 2))) for i in range(peers) for c in range(chans)]


def with_x_borders(rows, peers):
    forth = [(i, i + COL_Y) for i in range(peers - COL_Y)]
    back = [(i + COL_Y, i) for i in range(peers - COL_Y)]
    before = lax.ppermute(rows[:, COL_Y - 2 :], "space", forth)
    behind = lax.ppermute(rows[:, :2], "space", back)
    return jnp.concatenate([before, rows, behind], axis=1)


def on_device(features, column_heights, weight_one, bias_one, weight_two, bias_two):
    peers, chans = lax.axis_size("space"), lax.axis_size("chan")
    halo = 1 if peers > COL_Y else 0

    swap = order()
    own_part = pack(weight_one, bias_one, swap)
    near_part = lax.ppermute(own_part, "chan", [(c, c ^ 1) for c in range(chans)])
    fields, cross, mate = arrange(column_heights, features, swap, own_part)
    sent_part, cross = lax.optimization_barrier((own_part, cross))
    far_part = lax.ppermute(sent_part, ("space", "chan"), far_pairs(peers, chans))
    cross = lax.ppermute(cross, "space", across_pairs(peers))
    near_part, mate = lax.optimization_barrier((near_part, mate))
    mate = to_mate(mate)
    if halo:
        fields = with_x_borders(jnp.concatenate([cross, fields, mate[None]], axis=0), peers)
        cross, fields, mate = fields[:2], fields[2:-1], fields[-1]

    inner_a, near = first_near(halo, column_heights, fields, own_part, near_part)
    far_part, inner_a = lax.optimization_barrier((far_part, inner_a))
    other_part = to_mate(far_part)
    matrices, seven = fill(halo, column_heights, weight_two, bias_two, fields, mate, near, inner_a)
    inner_b, row_seven, far = first_far(halo, column_heights, fields, mate, far_part, other_part, seven)
    mate = to_mate(row_seven)
    done_inner, sums = second_inner(halo, column_heights, fields, near, far, inner_a, inner_b, row_seven, matrices)
    hidden = (inner_a, inner_b, row_seven, mate)
    return last(halo, column_heights, fields, cross, near, far, sums, hidden, done_inner, matrices)


def solution(mesh):
    placed = (
        P("space", None, None, None, None),
        P(),
        P(None, "chan", None),
        P("chan"),
        P(None, "chan", None),
        P("chan"),
    )
    return jax.shard_map(
        on_device,
        mesh=mesh,
        in_specs=placed,
        out_specs=P("space", "chan", None, None, None),
        check_vma=False,
    )
```

```python
import functools

import jax
import jax.numpy as jnp
from jax import lax
from jax.experimental import pallas as pl
from jax.experimental.pallas import tpu as pltpu
from jax.sharding import PartitionSpec as P

COL_Y = 8
TAPS = 3
BF16 = jnp.bfloat16
F32 = jnp.float32
ANY = pl.BlockSpec(memory_space=pl.ANY)
WHOLE = pl.BlockSpec(memory_space=pltpu.VMEM)
SCALARS = pl.BlockSpec(memory_space=pltpu.SMEM)


class Place:
    def __init__(self, heights):
        self.heights = heights
        self.column = lax.axis_index("space")
        self.peers = lax.axis_size("space")
        self.odd = lax.rem(self.column, 2)
        chan = lax.axis_index("chan")
        self.half = lax.div(chan, 2)
        near = lax.rem(chan, 2)
        far = jnp.where(self.odd == 1, 1 - near, near)
        self.slots = (near, 1 - near, far, 1 - far)

    def top(self, by_x=0, across=False):
        column, inside = self.column, True
        if across:
            y = lax.rem(column, COL_Y)
            step = jnp.where(self.odd == 1, 1, -1)
            inside = (y + step >= 0) & (y + step < COL_Y)
            column = column + step
        if by_x:
            column = column + by_x * COL_Y
            inside = inside & (column >= 0) & (column < self.peers)
        column = jnp.clip(column, 0, self.peers - 1)
        return jnp.where(inside, self.heights[column] * 8, 0)


def as_column(row):
    size = row.shape[1]
    wide = jnp.broadcast_to(row, (size, size))
    same = lax.broadcasted_iota(jnp.int32, (size, size), 0) == lax.broadcasted_iota(jnp.int32, (size, size), 1)
    return jnp.sum(jnp.where(same, wide, 0.0), axis=1, keepdims=True)


def order_kernel(swap):
    odd = lax.rem(lax.axis_index("space"), 2)
    group = swap.shape[0] // COL_Y
    row = lax.broadcasted_iota(jnp.int32, swap.shape, 0)
    column = lax.broadcasted_iota(jnp.int32, swap.shape, 1)
    u = lax.div(row, group)
    y = jnp.where(odd == 1, COL_Y - 1 - u, u)
    swap[...] = (column == lax.rem(row, group) * COL_Y + y).astype(F32).astype(BF16)


def pack_kernel(weights, bias, after, packed):
    taps, rows, lanes = weights.shape
    packed[:taps] = weights[...]
    column = as_column(bias[...])
    lane = lax.broadcasted_iota(jnp.int32, (rows, lanes), 1)
    extra = jnp.zeros((rows, lanes), F32)
    for at in range(3):
        piece = column.astype(BF16).astype(F32)
        extra = jnp.where(lane == at, piece, extra)
        column = column - piece
    packed[taps] = extra.astype(BF16)


def arrange_kernel(heights, features, swap, after, fields, cross, mate):
    _, channels, width, _, depth = features.shape
    place = Place(heights)
    group = 256 // COL_Y
    live = lax.broadcasted_iota(jnp.int32, (1, depth), 1) < place.top()
    for x in range(width):
        for first in range(0, channels, group):
            tile = features[0, first : first + group, x].reshape(256, depth)
            moved = jnp.dot(swap[...], tile, preferred_element_type=F32)
            moved = jnp.where(live, moved, 0.0).astype(BF16).reshape(COL_Y, group, depth)
            fields[:, x, first : first + group] = moved
            cross[:, x, first : first + group] = moved[:2]
            mate[x, first : first + group] = moved[COL_Y - 1]


def finish(partial, bias, live_top):
    rows, depth = partial.shape[0] // TAPS, partial.shape[1]
    z = lax.broadcasted_iota(jnp.int32, (rows, depth), 1)
    below = jnp.where(z == 0, 0.0, pltpu.roll(partial[:rows], 1, 1))
    above = jnp.where(z == depth - 1, 0.0, pltpu.roll(partial[2 * rows :], depth - 1, 1))
    total = jnp.maximum(below + partial[rows : 2 * rows] + above + bias, 0.0)
    return jnp.where(z < live_top, total, 0.0).astype(BF16)


def fill_first(parts, slots, odd, matrix, low_matrix, high_matrix, bias):
    quarter, channels = parts[0].shape[1], parts[0].shape[2]
    block = quarter * len(parts)
    for part, slot in zip(parts, slots, strict=True):
        at = slot * quarter
        for k in range(TAPS):
            span = pl.ds(pl.multiple_of(k * block + at, quarter), quarter)
            for j in range(TAPS):
                tap_j = jnp.where(odd == 1, 2 - j, j)
                for i in range(TAPS):
                    tile = part[9 * i + 3 * tap_j + k]
                    matrix[span, pl.ds((j * TAPS + i) * channels, channels)] = tile
                    if i > 0:
                        low_matrix[span, pl.ds((j * 2 + i - 1) * channels, channels)] = tile
                    if i < 2:
                        high_matrix[span, pl.ds((j * 2 + i) * channels, channels)] = tile
        extra = part[27].astype(F32)
        value = extra[:, 0:1] + extra[:, 1:2] + extra[:, 2:3]
        bias[pl.ds(pl.multiple_of(at, quarter), quarter), :] = jnp.broadcast_to(value, (quarter, bias.shape[1]))


def reach(x, width, stored, pad):
    return max(x - 1 + pad, 0), min(x + width + 1 + pad, stored)


def first_sums(get, stored, halo, matrices, taps=range(TAPS)):
    for x in range(-halo, COL_Y + halo):
        low, high = reach(x, 1, stored, 2 * halo)
        lhs = matrices[0]
        if high - low == 2:
            lhs = matrices[1] if x == 0 else matrices[2]
        wide = lhs.shape[1] // TAPS
        taken = jnp.concatenate([get(j, low, high) for j in taps], axis=0)
        columns = slice(taps[0] * wide, (taps[-1] + 1) * wide)
        yield x, jnp.dot(lhs[:, columns], taken, preferred_element_type=F32)


def first_row(get, stored, halo, matrices, bias, top):
    for x, partial in first_sums(get, stored, halo, matrices):
        yield x + halo, finish(partial, bias[:, 0:1], top(side_of(x)))


def side_of(x):
    return -1 if x < 0 else 1 if x >= COL_Y else 0


def span_of(ref, *at):
    *lead, low, high = at
    value = ref[(*lead, slice(low, high))]
    return value.reshape(-1, value.shape[-1])


def inner_rows(own, out, halo, matrices, bias, top):
    for u in range(COL_Y - 2):
        for x, done in first_row(lambda j, a, b: span_of(own, u + j, a, b), own.shape[1], halo, matrices, bias, top):
            out[u, x] = done


def first_near_kernel(halo, heights, own, part_a, part_b, out, matrix, low_matrix, high_matrix, bias):
    place = Place(heights)
    fill_first([part_a, part_b], place.slots[:2], place.odd, matrix, low_matrix, high_matrix, bias)
    inner_rows(own, out, halo, (matrix, low_matrix, high_matrix), bias, place.top)


def first_far_kernel(halo, heights, own, mate, part_a, part_b, near_seven, out, out_last, matrix, low_matrix, high_matrix, bias):
    place = Place(heights)
    fill_first([part_a, part_b], place.slots[2:], place.odd, matrix, low_matrix, high_matrix, bias)
    far = (matrix, low_matrix, high_matrix)
    inner_rows(own, out, halo, far, bias, place.top)

    def get(j, a, b):
        return span_of(mate, a, b) if j == 2 else span_of(own, COL_Y - 2 + j, a, b)

    half = bias.shape[0]
    out_last[:, :half] = near_seven[...]
    for x, done in first_row(get, own.shape[1], halo, far, bias, place.top):
        out_last[x, half:] = done


class Joined:
    def __init__(self, near, far):
        self.near, self.far = near, far
        self.shape = (2 * near.shape[0], near.shape[1])

    def __getitem__(self, at):
        columns = at[1]
        rows = self.near.shape[0] // TAPS
        pieces = [ref[k * rows : (k + 1) * rows, columns] for k in range(TAPS) for ref in (self.near, self.far)]
        return jnp.concatenate(pieces, axis=0)


def join(near, far):
    return [Joined(*each) for each in zip(near[0], far[0], strict=True)], jnp.concatenate([near[1][...], far[1][...]], axis=0)


def fill_second(weights, place, matrix, low_matrix, high_matrix):
    quarter, channels = weights.shape[1], weights.shape[2]
    empty = jnp.zeros((quarter, channels), BF16)
    for k in range(TAPS):
        for to in range(2):
            span = pl.ds((k * 2 + to) * quarter, quarter)
            for j in range(TAPS):
                tap_j = jnp.where(place.odd == 1, 2 - j, j)
                for at in range(4):
                    tile = empty
                    if 0 <= at - to < TAPS:
                        tile = weights[9 * (at - to) + 3 * tap_j + k].astype(F32)
                        tile = jnp.where(place.half == 1, pltpu.roll(tile, channels // 2, 1), tile).astype(BF16)
                    matrix[span, pl.ds((j * 4 + at) * channels, channels)] = tile
                    if at > 0:
                        low_matrix[span, pl.ds((j * 3 + at - 1) * channels, channels)] = tile
                    if at < 3:
                        high_matrix[span, pl.ds((j * 3 + at) * channels, channels)] = tile


def second_sums(get, stored, halo, matrices, taps=range(TAPS)):
    for x in range(0, COL_Y, 2):
        low, high = reach(x, 2, stored, halo)
        lhs = matrices[0]
        if high - low == 3:
            lhs = matrices[1] if x == 0 else matrices[2]
        wide = lhs.shape[1] // TAPS
        taken = jnp.concatenate([piece for j in taps for piece in get(j, low, high)], axis=0)
        yield x, jnp.dot(lhs[:, taps[0] * wide : (taps[-1] + 1) * wide], taken, preferred_element_type=F32)


def second_row(get, stored, halo, matrices, both, top):
    quarter = both.shape[0] // 2
    for x, partial in second_sums(get, stored, halo, matrices):
        done = finish(partial, both, top)
        yield x, done[:quarter], done[quarter:]


def halves(ref_a, ref_b, *at):
    *lead, low, high = at
    return [ref[(*lead, x)] for x in range(low, high) for ref in (ref_a, ref_b)]


def fill_bias(bias, both):
    quarter = bias.shape[1]
    column = jnp.broadcast_to(as_column(bias[...]), (quarter, both.shape[1]))
    both[:quarter] = column
    both[quarter:] = column


def fill_kernel(
    halo, heights, weights, bias, own, mate, near, low_near, high_near, bias_near, after,
    matrix, low_matrix, high_matrix, both, near_seven,
):
    place = Place(heights)
    fill_second(weights, place, matrix, low_matrix, high_matrix)
    fill_bias(bias, both)

    def get(j, a, b):
        return span_of(mate, a, b) if j == 2 else span_of(own, COL_Y - 2 + j, a, b)

    for x, done in first_row(get, own.shape[1], halo, (near, low_near, high_near), bias_near, place.top):
        near_seven[x] = done


def second_inner_kernel(
    halo, heights, own, near, low_near, high_near, bias_near, far, low_far, high_far, bias_far,
    inner_a, inner_b, row_seven, matrix, low_matrix, high_matrix, both, out, sums_before, sums_zero, sums_two,
):
    top = Place(heights).top()
    two = (matrix, low_matrix, high_matrix)

    def row(u, a, b):
        return halves(inner_a, inner_b, u - 1, a, b) if u < 7 else [row_seven[x] for x in range(a, b)]

    for u in range(2, 7):
        for x, here, beside in second_row(lambda j, a, b: row(u - 1 + j, a, b), inner_a.shape[1], halo, two, both[:, 0:1], top):
            out[u - 2, x] = here
            out[u - 2, x + 1] = beside
    for u, taps in ((0, (2,)), (1, (1, 2))):
        for x, sums in second_sums(lambda j, a, b: row(u - 1 + j, a, b), inner_a.shape[1], halo, two, taps):
            sums_two[u, x // 2] = sums

    matrices, _ = join(((near, low_near, high_near), bias_near), ((far, low_far, high_far), bias_far))
    width = own.shape[1]
    for x, sums in first_sums(lambda j, a, b: span_of(own, j - 2, a, b), width, halo, matrices, (2,)):
        sums_before[x + halo] = sums
    for x, sums in first_sums(lambda j, a, b: span_of(own, j - 1, a, b), width, halo, matrices, (1, 2)):
        sums_zero[x + halo] = sums


def last_kernel(
    halo, heights, own, cross, near, low_near, high_near, bias_near, far, low_far, high_far, bias_far, sums_before, sums_zero, sums_two,
    inner_a, inner_b, row_seven, mate, done_inner, matrix_two, low_two, high_two, both, out, edge, done_edge, result, sems,
):
    place = Place(heights)
    width, depth = cross.shape[1], cross.shape[3]
    matrices, biases = join(((near, low_near, high_near), bias_near), ((far, low_far, high_far), bias_far))
    for u, sums_own, taps in ((-1, sums_before, (0, 1)), (0, sums_zero, (0,))):
        for x, sums in first_sums(lambda j, a, b: span_of(cross, -u - j, a, b), width, halo, matrices, taps):
            top = place.top(side_of(x), across=u < 0)
            edge[u + 1, x + halo] = finish(sums + sums_own[x + halo], biases[:, 0:1], top)

    two, stored, quarter = (matrix_two, low_two, high_two), inner_a.shape[1], out.shape[1]
    for u, taps in ((0, (0, 1)), (1, (0,))):
        for x, sums in second_sums(lambda j, a, b: [edge[u + j, x] for x in range(a, b)], stored, halo, two, taps):
            done = finish(sums + sums_two[u, x // 2], both[:, 0:1], place.top())
            done_edge[u, x] = done[:quarter]
            done_edge[u, x + 1] = done[quarter:]

    def row(j, a, b):
        return halves(inner_a, inner_b, 5, a, b) if j == 0 else [(row_seven if j == 1 else mate)[x] for x in range(a, b)]

    for x, here, beside in second_row(row, stored, halo, two, both[:, 0:1], place.top()):
        done_edge[2, x] = here
        done_edge[2, x + 1] = beside
    size = quarter * COL_Y
    at_row = lax.broadcasted_iota(jnp.int32, (size, size), 0)
    at_column = lax.broadcasted_iota(jnp.int32, (size, size), 1)
    y = lax.rem(at_row, COL_Y)
    u = jnp.where(place.odd == 1, COL_Y - 1 - y, y)
    swap = (at_column == u * quarter + lax.div(at_row, COL_Y)).astype(F32).astype(BF16)
    for x in range(COL_Y):
        tiles = [done_edge[0, x], done_edge[1, x]] + [done_inner[v, x] for v in range(COL_Y - 3)] + [done_edge[2, x]]
        tile = jnp.concatenate(tiles, axis=0)
        moved = jnp.dot(swap, tile, preferred_element_type=F32).astype(BF16)
        result[x] = moved.reshape(quarter, COL_Y, depth)
        pltpu.make_async_copy(result.at[x], out.at[0, :, x], sems.at[x]).start()
    for x in range(COL_Y):
        pltpu.make_async_copy(result.at[x], out.at[0, :, x], sems.at[x]).wait()


SHORT, LONG = 2**6, 2**27


def call(kernel, name, inputs, outputs, scratch, nbytes, *args, kinds=None, place=WHOLE):
    return pl.pallas_call(
        kernel,
        out_shape=[jax.ShapeDtypeStruct(*each) for each in zip(outputs, kinds or [BF16] * len(outputs))],
        in_specs=inputs,
        out_specs=[place] * len(outputs),
        scratch_shapes=scratch,
        compiler_params=pltpu.CompilerParams(vmem_limit_bytes=16 * 2**20),
        cost_estimate=pl.CostEstimate(flops=64 * nbytes, bytes_accessed=nbytes, transcendentals=0),
        name=name,
    )(*args)


def order():
    return call(order_kernel, "order", [], [(256, 256)], [], LONG)[0]


def pack(weights, bias, after):
    taps, rows, lanes = weights.shape
    outputs = [(taps + 1, rows, lanes)]
    return call(pack_kernel, "pack", [WHOLE, WHOLE, ANY], outputs, [], LONG, weights, bias[None], after)[0]


def arrange(heights, features, swap, after):
    _, channels, width, _, depth = features.shape
    row = (width, channels, depth)
    outputs = [(COL_Y, *row), (2, *row), row]
    return call(arrange_kernel, "arrange", [SCALARS, WHOLE, WHOLE, ANY], outputs, [], SHORT, heights, features, swap, after)


def first_matrices(channels, rows):
    wide = TAPS * channels
    shapes = [(TAPS * rows, 3 * wide), (TAPS * rows, 2 * wide), (TAPS * rows, 2 * wide), (rows, 128)]
    return shapes, [BF16, BF16, BF16, F32]


def fill(halo, heights, weights, bias, own, mate, near, after):
    quarter, channels, depth = weights.shape[1], weights.shape[2], own.shape[3]
    tall, half = TAPS * 2 * quarter, near[-1].shape[0]
    outputs = [(tall, 12 * channels), (tall, 9 * channels), (tall, 9 * channels), (2 * quarter, 128)]
    outputs.append((COL_Y + 2 * halo, half, depth))
    args = (heights, weights, bias[None], own, mate, *near, after)
    inputs = [SCALARS] + [WHOLE] * (len(args) - 2) + [ANY]
    kernel = functools.partial(fill_kernel, halo)
    *matrices, seven = call(kernel, "fill", inputs, outputs, [], SHORT, *args, kinds=[BF16, BF16, BF16, F32, BF16])
    return matrices, seven


def first_near(halo, heights, own, part_a, part_b):
    _, _, channels, depth = own.shape
    half, width = 2 * part_a.shape[1], COL_Y + 2 * halo
    shapes, kinds = first_matrices(channels, half)
    inner, *matrices = call(
        functools.partial(first_near_kernel, halo), "first_near", [SCALARS] + [WHOLE] * 3,
        [(COL_Y - 2, width, half, depth), *shapes], [], LONG, heights, own, part_a, part_b, kinds=[BF16, *kinds],
    )
    return inner, matrices


def first_far(halo, heights, own, mate, part_a, part_b, near_seven):
    _, _, channels, depth = own.shape
    half, width = 2 * part_a.shape[1], COL_Y + 2 * halo
    shapes, kinds = first_matrices(channels, half)
    inner, row_seven, *matrices = call(
        functools.partial(first_far_kernel, halo), "first_far", [SCALARS] + [WHOLE] * 5,
        [(COL_Y - 2, width, half, depth), (width, channels, depth), *shapes], [], SHORT,
        heights, own, mate, part_a, part_b, near_seven, kinds=[BF16, BF16, *kinds],
    )
    return inner, row_seven, matrices


def second_inner(halo, heights, own, near, far, inner_a, inner_b, row_seven, matrices):
    rows, _, _, depth = inner_a.shape
    channels, width = own.shape[2], COL_Y + 2 * halo
    quarter = matrices[-1].shape[0] // 2
    sums = (width, TAPS * channels, depth)
    outputs = [(rows - 1, COL_Y, quarter, depth), sums, sums, (2, COL_Y // 2, TAPS * 2 * quarter, depth)]
    kinds = [BF16, F32, F32, F32]
    args = (heights, own, *near, *far, inner_a, inner_b, row_seven, *matrices)
    kernel = functools.partial(second_inner_kernel, halo)
    done, *sums = call(kernel, "second_inner", [SCALARS] + [WHOLE] * (len(args) - 1), outputs, [], SHORT, *args, kinds=kinds)
    return done, sums


def last(halo, heights, own, cross, near, far, sums, hidden, done_inner, matrices):
    _, _, channels, depth = cross.shape
    quarter, width = matrices[-1].shape[0] // 2, COL_Y + 2 * halo
    scratch = [pltpu.VMEM((2, width, channels, depth), BF16), pltpu.VMEM((3, COL_Y, quarter, depth), BF16)]
    scratch += [pltpu.VMEM((COL_Y, quarter, COL_Y, depth), BF16), pltpu.SemaphoreType.DMA((COL_Y,))]
    outputs = [(1, quarter, COL_Y, COL_Y, depth)]
    args = (heights, own, cross, *near, *far, *sums, *hidden, done_inner, *matrices)
    kernel = functools.partial(last_kernel, halo)
    return call(kernel, "last", [SCALARS] + [WHOLE] * (len(args) - 1), outputs, scratch, SHORT, *args, place=ANY)[0]


def across_pairs(peers):
    pairs = []
    for i in range(peers):
        to = i + 1 if i % 2 else i - 1
        if 0 <= to < peers and to // COL_Y == i // COL_Y:
            pairs.append((i, to))
    return pairs


def to_mate(value):
    return lax.ppermute(value, "space", [(i, i ^ 1) for i in range(lax.axis_size("space"))])


def far_pairs(peers, chans):
    return [(i * chans + c, i * chans + (c ^ (3 if i % 2 else 2))) for i in range(peers) for c in range(chans)]


def with_x_borders(rows, peers):
    forth = [(i, i + COL_Y) for i in range(peers - COL_Y)]
    back = [(i + COL_Y, i) for i in range(peers - COL_Y)]
    before = lax.ppermute(rows[:, COL_Y - 2 :], "space", forth)
    behind = lax.ppermute(rows[:, :2], "space", back)
    return jnp.concatenate([before, rows, behind], axis=1)


def on_device(features, column_heights, weight_one, bias_one, weight_two, bias_two):
    peers, chans = lax.axis_size("space"), lax.axis_size("chan")
    halo = 1 if peers > COL_Y else 0

    swap = order()
    own_part = pack(weight_one, bias_one, swap)
    near_part = lax.ppermute(own_part, "chan", [(c, c ^ 1) for c in range(chans)])
    fields, cross, mate = arrange(column_heights, features, swap, own_part)
    sent_part, cross = lax.optimization_barrier((own_part, cross))
    far_part = lax.ppermute(sent_part, ("space", "chan"), far_pairs(peers, chans))
    cross = lax.ppermute(cross, "space", across_pairs(peers))
    near_part, mate = lax.optimization_barrier((near_part, mate))
    mate = to_mate(mate)
    if halo:
        fields = with_x_borders(jnp.concatenate([cross, fields, mate[None]], axis=0), peers)
        cross, fields, mate = fields[:2], fields[2:-1], fields[-1]

    inner_a, near = first_near(halo, column_heights, fields, own_part, near_part)
    far_part, inner_a = lax.optimization_barrier((far_part, inner_a))
    other_part = to_mate(far_part)
    matrices, seven = fill(halo, column_heights, weight_two, bias_two, fields, mate, near, inner_a)
    inner_b, row_seven, far = first_far(halo, column_heights, fields, mate, far_part, other_part, seven)
    mate = to_mate(row_seven)
    done_inner, sums = second_inner(halo, column_heights, fields, near, far, inner_a, inner_b, row_seven, matrices)
    hidden = (inner_a, inner_b, row_seven, mate)
    return last(halo, column_heights, fields, cross, near, far, sums, hidden, done_inner, matrices)


def solution(mesh):
    placed = (
        P("space", None, None, None, None),
        P(),
        P(None, "chan", None),
        P("chan"),
        P(None, "chan", None),
        P("chan"),
    )
    return jax.shard_map(
        on_device,
        mesh=mesh,
        in_specs=placed,
        out_specs=P("space", "chan", None, None, None),
        check_vma=False,
    )
```
